128 devices in a mesh: rep: 8 (over z, x_lo), tr: 16 (over y, x_hi, core).
Axes of the slice: x: 4 (x_hi: 2, x_lo: 2; x = x_hi * 2 + x_lo), y: 4, z: 4, core: 2. Of those that a mesh axis runs over, the one named last changes fastest.
Arguments:
- taps: bfloat16 [64, 96, 3, 4096], P('rep', None, None, 'tr'), may hold values from -6 to 6
- routes: int32 [64, 1], replicated, may hold values from 0 to 7; in each aligned block of 8 rows (0 to 7, 8 to 15, ...) at most 2 rows name the same one
- lengths: int32 [64], replicated, may hold values from 4 to 96, as said below
- merge_weight: bfloat16 [3, 4096, 4096], P(None, 'tr'), may hold values from -0.0546875 to 0.0546875
- norm_gain: float32 [4096], P('tr'), may hold values from 0.5 to 1.5
- head_scale: float32 [32], P('tr'), may hold values from 0.02 to 1
Outputs:
- grad: float32 [3, 4096, 4096], P(None, 'tr', 'rep')
- new_weights: bfloat16 [3, 4096, 4096], P(None, 'tr')
The draws below stay inside these ranges and needn't reach their ends.
Inputs may be any that keep to these rules, and one draw needn't show every extreme that they name: routes[s, 0] names the trainer group of rollout s. Within each aligned block of the 8 rollouts of one replica group, no trainer group is named more than 2 times; some group is named exactly 2 times, and every trainer group is named by some rollout. `lengths`: some rollout has exactly 96 live tokens.
All inputs are finite; a program needn't handle non-finite values.
Results may differ from the reference program's by a relative error of at most 0.0034.
Values may be sent and summed in bfloat16 or wider, within the bound.
No kernel may reach another device: no remote copies, remote signals or barrier semaphores. Data moves between devices by JAX's collectives and lax.ppermute only.
A program may use at most 128 MiB of HBM per device.

```python
import math
import jax
import jax.numpy as jnp
import numpy as np
from jax import lax

D = 4096
HEAD = 128
HEADS = 32
L = 96
CAP = 2
SEQ_SRC = 8
SEQS = 64
N_REP = 8


def draw_lengths(key, part):
    key = jax.random.fold_in(key, 7)
    first, second = jax.random.split(key)
    values = jax.random.randint(first, (SEQS,), 4, L + 1)
    chosen = jax.random.randint(second, (), 0, SEQS)
    return jnp.where(jnp.arange(SEQS) == chosen, L, values).astype(jnp.int32)


def block_levels(key, dims, pieces, least, top_value):
    def one(position, shards_of):
        draws = jax.random.uniform(jax.random.fold_in(jax.random.fold_in(key, 6), position), (shards_of,), jnp.float32, least / len(pieces), top_value / len(pieces))
        return jnp.repeat(jnp.exp(draws), dims[position] // shards_of).reshape((-1,) + (1,) * (len(dims) - position - 1))

    factor_of = one(*pieces[0])
    for cut in pieces[1:]:
        factor_of = factor_of * one(*cut)
    return factor_of


def deal_out(own_key, own, number, rows, count, top, bound, skew):
    order = jax.random.permutation(own_key, count)
    heavy_load, ordinary = portions_of(count, rows * top, bound, skew, True), portions_of(count, rows * top, bound, skew, False)
    places = jnp.arange(count)

    def named(sizes, offset_by):
        used = int((sizes > 0).sum())
        fixed = max(1, used // 4)
        shifted = fixed + (places - fixed + offset_by * (used - fixed)) % max(1, count - fixed)
        return jnp.zeros((count,), jnp.int32).at[order[jnp.where(places < fixed, places, shifted)]].set(jnp.asarray(sizes, jnp.int32))

    sizes = jnp.where(number % 4 == 0, named(heavy_load, number // 4), named(ordinary, number - number // 4 - 1))
    mixed = jax.random.permutation(jax.random.fold_in(own, 3), count)
    donor, taker = mixed[0:count // 2 * 2:2], mixed[1:count // 2 * 2:2]
    room = jnp.minimum(sizes[donor] - 1, bound - sizes[taker]) // 2
    room = jnp.where((donor == order[0]) | (taker == order[0]) | (sizes[taker] == 0), 0, jnp.maximum(room, 0))
    shifted = jax.random.randint(jax.random.fold_in(own, 4), (count // 2,), 0, 1 << 20) % (room + 1)
    sizes = sizes.at[donor].add(-shifted).at[taker].add(shifted)
    labels = jnp.searchsorted(jnp.cumsum(sizes), jnp.arange(rows * top), side="right").astype(jnp.int32)
    listing = labels.reshape(top, rows).T
    listing = listing[jax.random.permutation(jax.random.fold_in(own, 1), rows)]
    offset_by = jax.random.randint(jax.random.fold_in(own, 2), (rows, 1), 0, top)
    return jnp.take_along_axis(listing, (jnp.arange(top)[None, :] + offset_by) % top, axis=1)


def portions_of(number_of, total, reach, slope, full):
    portions = [(1 << 20) // math.isqrt(grade ** slope) + 1 for grade in range(1, number_of + 1)]
    largest = reach if full else min(reach, max(-(-total // number_of), total * portions[0] // sum(portions)))
    least = 1 if total - largest >= number_of - 1 else 0
    holding, surplus = [largest] + [least] * (number_of - 1), total - largest - least * (number_of - 1)
    while surplus > 0:
        candidates = [i for i in range(1, number_of) if holding[i] < largest] or [i for i in range(1, number_of) if holding[i] < reach]
        pool, left = sum([portions[i] for i in candidates]), surplus
        for i in candidates:
            addition = min(reach - holding[i], max(1, left * portions[i] // pool), surplus)
            holding[i] = holding[i] + addition
            surplus = surplus - addition
    return np.array(holding)


def centred(rng, dims, scale, bound, cuts=(), held_as=jnp.bfloat16):
    array = jax.random.normal(rng, dims, jnp.float32) * scale
    if len(cuts) > 0:
        array = block_levels(rng, dims, cuts, -0.22, 0.18) * array
    return jnp.clip(array, min=-bound, max=bound).astype(held_as)


def setup_inputs(seed: int = 0) -> dict:
    arg_keys = jax.random.split(jax.random.key(seed), 7)
    taps = centred(arg_keys[0], (SEQS, L, 3, D), 1.0, 6.0, ((0, 8), (3, 16)))
    routes_keys = jax.random.split(jax.random.fold_in(arg_keys[1], 1), SEQS // SEQ_SRC)
    routes_turns = jax.random.permutation(jax.random.fold_in(arg_keys[1], 3), SEQS // SEQ_SRC)
    routes = jax.vmap(lambda own, number: deal_out(jax.random.fold_in(arg_keys[1], 2), own, number, SEQ_SRC, N_REP, 1, CAP, 2))(routes_keys, routes_turns).reshape((SEQS, 1))
    lengths = draw_lengths(jax.random.fold_in(arg_keys[6], 71), 0)
    merge_weight = centred(arg_keys[3], (3, D, D), (3 * D) ** -0.5, 0.0546875, ((1, 16),))
    norm_gain = jnp.clip(1.0 + 0.1 * jax.random.normal(arg_keys[4], (D,), jnp.float32), 0.5, 1.5)
    head_scale = jnp.clip(jnp.exp(math.log(1.0) - 3.912023 * jax.random.uniform(arg_keys[5], (HEADS,), jnp.float32) ** block_levels(arg_keys[5], (HEADS,), ((0, 16),), -0.2, 0.2)), 0.02, 1.0)
    return dict(taps=taps, routes=routes, lengths=lengths, merge_weight=merge_weight, norm_gain=norm_gain, head_scale=head_scale)


epsilon = 1e-06
step_size = 0.004

def target_count(lens):
    return jnp.maximum(lens - 1, 0) + jnp.maximum(lens - 2, 0) + jnp.maximum(lens - 3, 0)

def unroll_loss(start, targets, lens, weights, scales):
    span = start.shape[1]
    places = jnp.arange(span, dtype=jnp.int32)
    upper = jnp.maximum(lens, 1)
    keymask = (places[None, None, :] <= places[None, :, None]) & (places[None, None, :] < upper[:, None, None])
    current = start
    result = jnp.zeros((), jnp.float32)
    for step in range(3):
        logits = jnp.einsum('bihe,bjhe->bhij', current, start, precision=lax.Precision.HIGHEST)
        logits = logits * scales[None, :, None, None]
        logits = jnp.where(keymask[:, None], logits, -1e+30)
        highest = lax.optimization_barrier(jnp.max(logits, axis=-1, keepdims=True))
        raised = jnp.exp(logits - highest)
        shares = raised / lax.optimization_barrier(jnp.sum(raised, axis=-1, keepdims=True))
        attended = jnp.einsum('bhij,bjhe->bihe', shares, start, precision=lax.Precision.HIGHEST)
        current = current + attended
        later = jnp.concatenate([targets[:, step + 1:], jnp.zeros_like(targets[:, :step + 1])], axis=1)
        active = (places[None, :] + step + 1 < lens[:, None]).astype(jnp.float32) * weights[:, None]
        offset = current - later
        result = result + jnp.sum(active[:, :, None, None] * offset * offset)
    return result

def reference(taps, routes, lengths, merge_weight, norm_gain, head_scale):
    seq_total = taps.shape[0]
    rows = taps.reshape(seq_total * L, 3 * D)
    targets = taps[:, :, 2, :].astype(jnp.float32).reshape(seq_total, L, HEADS, HEAD)
    dest = routes[:, 0]
    owner = (jnp.arange(N_REP, dtype=jnp.int32)[:, None] == dest[None, :]).astype(jnp.float32)
    counts = lax.optimization_barrier(jnp.sum(owner * target_count(lengths).astype(jnp.float32)[None, :], axis=1))
    weights = lax.optimization_barrier(jnp.sum(owner / counts[:, None], axis=0))
    merged = jnp.dot(rows, merge_weight.reshape(3 * D, D), preferred_element_type=jnp.float32)

    def loss_of(merged_rows):
        inverse = lax.rsqrt(lax.optimization_barrier(jnp.mean(merged_rows * merged_rows, axis=1, keepdims=True)) + epsilon)
        normed = merged_rows * inverse * norm_gain[None, :]
        return unroll_loss(normed.reshape(seq_total, L, HEADS, HEAD), targets, lengths, weights, head_scale)
    loss_value, pullback = jax.vjp(loss_of, merged)
    merged_grad, = pullback(jnp.ones((), jnp.float32))
    grad_rows = merged_grad.astype(jnp.bfloat16)
    grad = lax.dot_general(rows, grad_rows, (((0,), (0,)), ((), ())), preferred_element_type=jnp.float32)
    grad = grad.reshape(3, D, D)
    new_weights = (merge_weight.astype(jnp.float32) - step_size * grad).astype(jnp.bfloat16)
    return (grad, new_weights)
```

```python
import jax
import jax.numpy as jnp
from jax import lax
from jax.experimental import pallas as pl
from jax.experimental.pallas import tpu as pltpu
from jax.sharding import PartitionSpec as P

epsilon = 1e-06
step_size = 0.004
SEND = 128.0
SPAN = 96
HEAD = 128
RING = 4
FIRST = ((2, 1), (1, 1), (3, 1), (2, 0), (1, 0), (3, 0), (0, 1), (0, 0))

f32 = jnp.float32
bf16 = jnp.bfloat16
f16 = jnp.float16

ROWS_ROWS = (((1,), (1,)), ((), ()))
ROWS_COLS = (((1,), (0,)), ((), ()))
COLS_COLS = (((0,), (0,)), ((), ()))


def split(a):
    high = a.astype(bf16)
    return high, (a - high.astype(f32)).astype(bf16)


def product(a, b, dims):
    ka, kb = dims[0][0][0], dims[0][1][0]
    return lax.dot_general(
        jnp.concatenate([a[0], a[0], a[1]], axis=ka),
        jnp.concatenate([b[0], b[1], b[0]], axis=kb),
        dims,
        preferred_element_type=f32,
    )


def attention_kernel(lens_ref, weights_ref, scale_ref, merged_ref, square_ref, gain_ref, tap_ref, scaled_ref, cross_ref):
    slots = merged_ref.shape[0]
    heads = scale_ref.shape[0]
    first = pl.program_id(0) * slots
    place = lax.broadcasted_iota(jnp.int32, (SPAN, HEAD), 0)
    key = lax.broadcasted_iota(jnp.int32, (SPAN, HEAD), 1)
    eye = lax.broadcasted_iota(jnp.int32, (SPAN, SPAN), 0) == lax.broadcasted_iota(jnp.int32, (SPAN, SPAN), 1)
    pad = jnp.zeros((HEAD - SPAN, HEAD), f32)
    chains = [(s, h) for s in range(slots) for h in range(heads)]
    every = range(len(chains))
    width = 16 * heads * HEAD
    lens = [lens_ref[first + s] for s, _ in chains]
    weights = [weights_ref[first + s] for s, _ in chains]
    scales = [scale_ref[h] for _, h in chains]
    columns = [pl.ds(h * HEAD, HEAD) for _, h in chains]
    allowed = [(key <= place) & (key < lens[c]) for c in every]
    inverse = []
    for s in range(slots):
        across = lax.rsqrt(square_ref[s] / width + epsilon)
        inverse.append(jnp.sum(jnp.where(eye, across, 0.0), axis=1, keepdims=True))
    gains = [gain_ref[:, columns[c]] for c in every]
    start = [merged_ref[chains[c][0], :, columns[c]] * inverse[chains[c][0]] * gains[c] for c in every]
    keys = [split(jnp.concatenate([start[c], pad], axis=0)) for c in every]
    current = list(start)
    queries, shares, loss_grads = [], [], []
    for step in range(3):
        parts = [split(current[c]) for c in every]
        logits = [product(parts[c], keys[c], ROWS_ROWS) * scales[c] for c in every]
        logits = [jnp.where(allowed[c], logits[c], -1e30) for c in every]
        raised = [jnp.exp(logits[c] - jnp.max(logits[c], axis=1, keepdims=True)) for c in every]
        share = [raised[c] / jnp.sum(raised[c], axis=1, keepdims=True) for c in every]
        share_parts = [split(share[c]) for c in every]
        attended = [product(share_parts[c], keys[c], ROWS_COLS) for c in every]
        current = [current[c] + attended[c] for c in every]
        queries.append(parts)
        shares.append((share, share_parts))
        grads = []
        for c in every:
            later = pltpu.roll(tap_ref[chains[c][0], :, columns[c]].astype(f32), SPAN - (step + 1), 0)
            active = jnp.where(place + (step + 1) < lens[c], 2.0 * weights[c], 0.0)
            grads.append(active * (current[c] - later))
        loss_grads.append(grads)
    grad = loss_grads[2]
    key_grad = None
    for step in (2, 1, 0):
        share, share_parts = shares[step]
        parts = [split(grad[c]) for c in every]
        share_grad = [product(parts[c], keys[c], ROWS_ROWS) for c in every]
        inner = [jnp.sum(share_grad[c] * share[c], axis=1, keepdims=True) for c in every]
        logit_parts = [split(share[c] * (share_grad[c] - inner[c]) * scales[c]) for c in every]
        left = [tuple(jnp.concatenate(z, axis=0) for z in zip(share_parts[c], logit_parts[c])) for c in every]
        right = [tuple(jnp.concatenate(z, axis=0) for z in zip(parts[c], queries[step][c])) for c in every]
        added = [product(left[c], right[c], COLS_COLS) for c in every]
        key_grad = added if key_grad is None else [key_grad[c] + added[c] for c in every]
        grad = [grad[c] + product(logit_parts[c], keys[c], ROWS_COLS) for c in every]
        if step > 0:
            grad = [grad[c] + loss_grads[step - 1][c] for c in every]
    crossed = [None] * slots
    for c in every:
        s = chains[c][0]
        scaled = (grad[c] + key_grad[c][:SPAN]) * gains[c]
        scaled_ref[s, :, columns[c]] = scaled
        inner = jnp.sum(scaled * merged_ref[s, :, columns[c]], axis=1, keepdims=True)
        crossed[s] = inner if crossed[s] is None else crossed[s] + inner
    for s in range(slots):
        cross_ref[s] = jnp.sum(jnp.where(eye, crossed[s], 0.0), axis=0, keepdims=True)


def attention(lens, weights, scales, merged, squares, gain, taps, slots=2):
    count, span, wide = merged.shape
    scalar = pl.BlockSpec(memory_space=pltpu.SMEM)
    block = pl.BlockSpec((slots, span, wide), lambda i: (i, 0, 0))
    flat = pl.BlockSpec((slots, 1, span), lambda i: (i, 0, 0))
    return pl.pallas_call(
        attention_kernel,
        grid=(count // slots,),
        in_specs=[scalar, scalar, scalar, block, flat, pl.BlockSpec((1, wide), lambda i: (0, 0)), block],
        out_specs=[block, flat],
        out_shape=[
            jax.ShapeDtypeStruct((count, span, wide), f32),
            jax.ShapeDtypeStruct((count, 1, span), f32),
        ],
        compiler_params=pltpu.CompilerParams(vmem_limit_bytes=48 * 2**20),
        cost_estimate=pl.CostEstimate(flops=2 * 10**9, bytes_accessed=3 * 10**6, transcendentals=10**6),
    )(lens, weights, scales, merged, squares, gain, taps)


def tr_index(y, x, core):
    return (y % RING * 2 + x % 2) * 2 + core % 2


def to_chip(value, dy, dx, dcore=0):
    pairs = [
        (tr_index(y, x, core), tr_index(y + dy, x + dx, core + dcore))
        for y in range(RING)
        for x in range(2)
        for core in range(2)
    ]
    return lax.ppermute(value, "tr", pairs)


def to_group(value, dz, dx):
    pairs = [(z * 2 + x, (z + dz) % RING * 2 + (x + dx) % 2) for z in range(RING) for x in range(2)]
    return lax.ppermute(value, "rep", pairs)


def to_sibling(value):
    return to_chip(value, 0, 0, 1)


def gather(value, send):
    got = {(0, 0): value}
    got[1, 0] = send(value, 1, 0)
    got[3, 0] = send(value, 3, 0)
    got[0, 1] = send(value, 0, 1)
    got[2, 0] = send(value, 2, 0)
    got[1, 1] = send(got[0, 1], 1, 0)
    got[3, 1] = send(got[0, 1], 3, 0)
    got[2, 1] = send(got[2, 0], 0, 1)
    return got


def sum_over_tr(value):
    value = value + to_sibling(value)
    value = value + to_chip(value, 0, 1)
    return value + to_chip(value, 1, 0) + to_chip(value, 2, 0) + to_chip(value, 3, 0)


def per_device(taps, routes, lengths, merge_weight, norm_gain, head_scale):
    rep = lax.axis_index("rep")
    tr = lax.axis_index("tr")
    core = tr % 2
    x_high = tr // 2 % 2
    y = tr // 4
    x_low = rep % 2
    z = rep // 2
    slots, span, tap_count, wide = taps.shape
    width_all = merge_weight.shape[2]
    flat_in = tap_count * wide
    block = width_all // lax.axis_size("rep")
    rows = taps.reshape(slots * span, flat_in)
    weight = merge_weight.reshape(flat_in, width_all)

    dest = routes[:, 0]
    target = jnp.maximum(lengths - 1, 0) + jnp.maximum(lengths - 2, 0) + jnp.maximum(lengths - 3, 0)
    own_dest = lax.dynamic_slice_in_dim(dest, rep * slots, slots)
    lens = lax.dynamic_slice_in_dim(lengths, rep * slots, slots)
    count = jnp.sum(jnp.where(own_dest[:, None] == dest[None, :], target[None, :], 0), axis=1)
    weights = 1.0 / count.astype(f32)

    def columns_of(dy, dx, parity):
        return tr_index(y + dy, x_high + dx, parity) * wide

    def partial_sum(dy, dx, parity):
        piece = lax.dynamic_slice_in_dim(weight, columns_of(dy, dx, parity), wide, 1)
        return jnp.dot(rows, piece, preferred_element_type=f32)

    crossing = {}
    for dy, dx in FIRST:
        crossing[dy, dx] = to_sibling((partial_sum(dy, dx, 1 - core) * SEND).astype(f16))
    merged = None
    landed = []
    for dy, dx in FIRST:
        both = partial_sum(dy, dx, core) * SEND + crossing[dy, dx].astype(f32)
        if (dy, dx) == (0, 0):
            merged = both
        else:
            landed.append(to_chip(both.astype(f16), dy, dx))
    for piece in landed:
        merged = merged + piece.astype(f32)
    merged = (merged * (1.0 / SEND)).reshape(slots, span, wide)
    squares = sum_over_tr(jnp.sum(merged * merged, axis=2))

    tap_rows = gather(rows, to_group)

    scaled, crossed = attention(
        lens,
        weights,
        head_scale,
        merged,
        squares.reshape(slots, 1, span),
        norm_gain.reshape(1, wide),
        taps[:, :, 2, :],
    )
    crossed = sum_over_tr(crossed.reshape(slots, span))
    inverse = lax.rsqrt(squares / width_all + epsilon)
    merged_grad = (
        scaled * inverse[:, :, None]
        - merged * (inverse * inverse * inverse * crossed / width_all)[:, :, None]
    ).astype(bf16)

    groups, chips = lax.axis_size("rep"), lax.axis_size("tr")
    pairs = [(r * chips + t, (t // 2) * chips + 2 * r + t % 2) for r in range(groups) for t in range(chips)]
    turned = lax.ppermute(merged_grad.reshape(slots * span, wide), ("rep", "tr"), pairs)
    own_half = gather(turned, to_chip)
    other_half = {k: to_sibling(v) for k, v in own_half.items()}

    all_rows = jnp.stack([tap_rows[a, b] for a in range(RING) for b in range(2)])

    def gradient(half):
        total = None
        for (a, b), piece in half.items():
            place = (z - (y - a)) % RING * 2 + (x_low - (x_high - b)) % 2
            source = lax.dynamic_index_in_dim(all_rows, place, 0, keepdims=False)
            part = lax.dot_general(source, piece, COLS_COLS, preferred_element_type=f32)
            total = part if total is None else total + part
        return total

    grad = jnp.zeros((flat_in, block), f32)
    new = jnp.zeros((flat_in, width_all), bf16)
    for half, parity in ((own_half, core), (other_half, 1 - core)):
        grad_half = gradient(half)
        grad = lax.dynamic_update_slice_in_dim(grad, grad_half, parity * wide, 1)
        old = lax.dynamic_slice_in_dim(weight, rep * block + parity * wide, wide, 1)
        new_half = (old.astype(f32) - step_size * grad_half).astype(bf16)
        for (a, b), piece in gather(new_half, to_group).items():
            owner = (z - a) % RING * 2 + (x_low - b) % 2
            new = lax.dynamic_update_slice_in_dim(new, piece, owner * block + parity * wide, 1)
    return grad.reshape(tap_count, wide, block), new.reshape(tap_count, wide, width_all)


def solution(mesh):
    in_specs = (P("rep", None, None, "tr"), P(), P(), P(None, "tr", None), P("tr"), P("tr"))
    out_specs = (P(None, "tr", "rep"), P(None, "tr", None))
    return jax.shard_map(
        per_device, mesh=mesh, in_specs=in_specs, out_specs=out_specs, check_vma=False
    )
```

```python
import jax
import jax.numpy as jnp
from jax import lax
from jax.experimental import pallas as pl
from jax.experimental.pallas import tpu as pltpu
from jax.sharding import PartitionSpec as P

epsilon = 1e-06
step_size = 0.004
SEND = 128.0
SPAN = 96
HEAD = 128
RING = 4
ORDER = (((2, 1), (1, 1), (3, 1), (1, 0)), ((3, 0), (2, 0), (0, 1), (0, 0)))

f32 = jnp.float32
bf16 = jnp.bfloat16
f16 = jnp.float16

ROWS_ROWS = (((1,), (1,)), ((), ()))
ROWS_COLS = (((1,), (0,)), ((), ()))
COLS_COLS = (((0,), (0,)), ((), ()))


def split(a):
    high = a.astype(bf16)
    return high, (a - high.astype(f32)).astype(bf16)


def product(a, b, dims):
    ka, kb = dims[0][0][0], dims[0][1][0]
    return lax.dot_general(
        jnp.concatenate([a[0], a[0], a[1]], axis=ka),
        jnp.concatenate([b[0], b[1], b[0]], axis=kb),
        dims,
        preferred_element_type=f32,
    )


def attention_kernel(lens_ref, weights_ref, scale_ref, merged_ref, square_ref, gain_ref, tap_ref, scaled_ref, cross_ref):
    slots = merged_ref.shape[0]
    heads = scale_ref.shape[0]
    first = pl.program_id(0) * slots
    place = lax.broadcasted_iota(jnp.int32, (SPAN, HEAD), 0)
    key = lax.broadcasted_iota(jnp.int32, (SPAN, HEAD), 1)
    eye = lax.broadcasted_iota(jnp.int32, (SPAN, SPAN), 0) == lax.broadcasted_iota(jnp.int32, (SPAN, SPAN), 1)
    pad = jnp.zeros((HEAD - SPAN, HEAD), f32)
    chains = [(s, h) for s in range(slots) for h in range(heads)]
    every = range(len(chains))
    width = 16 * heads * HEAD
    lens = [lens_ref[first + s] for s, _ in chains]
    weights = [weights_ref[first + s] for s, _ in chains]
    scales = [scale_ref[h] for _, h in chains]
    columns = [pl.ds(h * HEAD, HEAD) for _, h in chains]
    allowed = [(key <= place) & (key < lens[c]) for c in every]
    inverse = []
    for s in range(slots):
        across = lax.rsqrt(square_ref[s] / width + epsilon)
        inverse.append(jnp.sum(jnp.where(eye, across, 0.0), axis=1, keepdims=True))
    gains = [gain_ref[:, columns[c]] for c in every]
    start = [merged_ref[chains[c][0], :, columns[c]] * inverse[chains[c][0]] * gains[c] for c in every]
    keys = [split(jnp.concatenate([start[c], pad], axis=0)) for c in every]
    current = list(start)
    queries, shares, loss_grads = [], [], []
    for step in range(3):
        parts = [split(current[c]) for c in every]
        logits = [product(parts[c], keys[c], ROWS_ROWS) * scales[c] for c in every]
        logits = [jnp.where(allowed[c], logits[c], -1e30) for c in every]
        raised = [jnp.exp(logits[c] - jnp.max(logits[c], axis=1, keepdims=True)) for c in every]
        share = [raised[c] / jnp.sum(raised[c], axis=1, keepdims=True) for c in every]
        share_parts = [split(share[c]) for c in every]
        attended = [product(share_parts[c], keys[c], ROWS_COLS) for c in every]
        current = [current[c] + attended[c] for c in every]
        queries.append(parts)
        shares.append((share, share_parts))
        grads = []
        for c in every:
            later = pltpu.roll(tap_ref[chains[c][0], :, columns[c]].astype(f32), SPAN - (step + 1), 0)
            active = jnp.where(place + (step + 1) < lens[c], 2.0 * weights[c], 0.0)
            grads.append(active * (current[c] - later))
        loss_grads.append(grads)
    grad = loss_grads[2]
    key_grad = None
    for step in (2, 1, 0):
        share, share_parts = shares[step]
        parts = [split(grad[c]) for c in every]
        share_grad = [product(parts[c], keys[c], ROWS_ROWS) for c in every]
        inner = [jnp.sum(share_grad[c] * share[c], axis=1, keepdims=True) for c in every]
        logit_parts = [split(share[c] * (share_grad[c] - inner[c]) * scales[c]) for c in every]
        left = [tuple(jnp.concatenate(z, axis=0) for z in zip(share_parts[c], logit_parts[c])) for c in every]
        right = [tuple(jnp.concatenate(z, axis=0) for z in zip(parts[c], queries[step][c])) for c in every]
        added = [product(left[c], right[c], COLS_COLS) for c in every]
        key_grad = added if key_grad is None else [key_grad[c] + added[c] for c in every]
        grad = [grad[c] + product(logit_parts[c], keys[c], ROWS_COLS) for c in every]
        if step > 0:
            grad = [grad[c] + loss_grads[step - 1][c] for c in every]
    crossed = [None] * slots
    for c in every:
        s = chains[c][0]
        scaled = (grad[c] + key_grad[c][:SPAN]) * gains[c]
        scaled_ref[s, :, columns[c]] = scaled
        inner = jnp.sum(scaled * merged_ref[s, :, columns[c]], axis=1, keepdims=True)
        crossed[s] = inner if crossed[s] is None else crossed[s] + inner
    for s in range(slots):
        cross_ref[s] = jnp.sum(jnp.where(eye, crossed[s], 0.0), axis=0, keepdims=True)


def attention(lens, weights, scales, merged, squares, gain, taps, slots=2):
    count, span, wide = merged.shape
    scalar = pl.BlockSpec(memory_space=pltpu.SMEM)
    block = pl.BlockSpec((slots, span, wide), lambda i: (i, 0, 0))
    flat = pl.BlockSpec((slots, 1, span), lambda i: (i, 0, 0))
    return pl.pallas_call(
        attention_kernel,
        grid=(count // slots,),
        in_specs=[scalar, scalar, scalar, block, flat, pl.BlockSpec((1, wide), lambda i: (0, 0)), block],
        out_specs=[block, flat],
        out_shape=[
            jax.ShapeDtypeStruct((count, span, wide), f32),
            jax.ShapeDtypeStruct((count, 1, span), f32),
        ],
        compiler_params=pltpu.CompilerParams(vmem_limit_bytes=48 * 2**20),
        cost_estimate=pl.CostEstimate(flops=2 * 10**9, bytes_accessed=3 * 10**6, transcendentals=10**6),
    )(lens, weights, scales, merged, squares, gain, taps)


def tr_index(y, x, core):
    return (y % RING * 2 + x % 2) * 2 + core % 2


def to_chip(value, dy, dx, dcore=0):
    pairs = [
        (tr_index(y, x, core), tr_index(y + dy, x + dx, core + dcore))
        for y in range(RING)
        for x in range(2)
        for core in range(2)
    ]
    return lax.ppermute(value, "tr", pairs)


def to_group(value, dz, dx):
    pairs = [(z * 2 + x, (z + dz) % RING * 2 + (x + dx) % 2) for z in range(RING) for x in range(2)]
    return lax.ppermute(value, "rep", pairs)


def to_sibling(value):
    return to_chip(value, 0, 0, 1)


def gather(value, send):
    got = {(0, 0): value}
    got[1, 0] = send(value, 1, 0)
    got[3, 0] = send(value, 3, 0)
    got[0, 1] = send(value, 0, 1)
    got[2, 0] = send(value, 2, 0)
    got[1, 1] = send(got[0, 1], 1, 0)
    got[3, 1] = send(got[0, 1], 3, 0)
    got[2, 1] = send(got[2, 0], 0, 1)
    return got


def gather_relayed(value, send):
    half = value.shape[0] // 2
    up, down, across = send(value, 1, 0), send(value, 3, 0), send(value, 0, 1)
    far_first = send(up[:half], 1, 0)
    far_last = send(down[half:], 3, 0)
    up_across, down_across = send(across, 1, 0), send(across, 3, 0)
    far_across = send(jnp.concatenate([far_first, far_last], axis=0), 0, 1)
    return [
        (0, 0, 0, value),
        (1, 0, 0, up),
        (3, 0, 0, down),
        (0, 1, 0, across),
        (2, 0, 0, far_first),
        (2, 0, half, far_last),
        (1, 1, 0, up_across),
        (3, 1, 0, down_across),
        (2, 1, 0, far_across),
    ]


def product_kernel(blocks_ref, rows_ref, weight_ref, out_ref):
    out_ref[0] = jnp.dot(rows_ref[...], weight_ref[...], preferred_element_type=f32)


def products(rows, weight, blocks, wide):
    count, depth = rows.shape
    number = blocks.shape[0]
    return pl.pallas_call(
        product_kernel,
        grid_spec=pltpu.PrefetchScalarGridSpec(
            num_scalar_prefetch=1,
            grid=(number,),
            in_specs=[
                pl.BlockSpec((count, depth), lambda i, blocks: (0, 0)),
                pl.BlockSpec((depth, wide), lambda i, blocks: (0, blocks[i])),
            ],
            out_specs=pl.BlockSpec((1, count, wide), lambda i, blocks: (i, 0, 0)),
        ),
        out_shape=jax.ShapeDtypeStruct((number, count, wide), f32),
        compiler_params=pltpu.CompilerParams(vmem_limit_bytes=56 * 2**20),
        cost_estimate=pl.CostEstimate(
            flops=2 * count * depth * wide * number,
            bytes_accessed=count * depth * 2 + number * wide * (count * 4 + depth * 2),
            transcendentals=0,
        ),
    )(blocks, rows, weight)


def sum_over_tr(value):
    value = value + to_sibling(value)
    value = value + to_chip(value, 0, 1)
    return value + to_chip(value, 1, 0) + to_chip(value, 2, 0) + to_chip(value, 3, 0)


def per_device(taps, routes, lengths, merge_weight, norm_gain, head_scale):
    rep = lax.axis_index("rep")
    tr = lax.axis_index("tr")
    core = tr % 2
    x_high = tr // 2 % 2
    y = tr // 4
    x_low = rep % 2
    z = rep // 2
    slots, span, tap_count, wide = taps.shape
    width_all = merge_weight.shape[2]
    flat_in = tap_count * wide
    block = width_all // lax.axis_size("rep")
    rows = taps.reshape(slots * span, flat_in)
    weight = merge_weight.reshape(flat_in, width_all)

    dest = routes[:, 0]
    target = jnp.maximum(lengths - 1, 0) + jnp.maximum(lengths - 2, 0) + jnp.maximum(lengths - 3, 0)
    own_dest = lax.dynamic_slice_in_dim(dest, rep * slots, slots)
    lens = lax.dynamic_slice_in_dim(lengths, rep * slots, slots)
    count = jnp.sum(jnp.where(own_dest[:, None] == dest[None, :], target[None, :], 0), axis=1)
    weights = 1.0 / count.astype(f32)

    along_z = [[at_z * 2 + at_x for at_z in range(RING)] for at_x in range(2)]
    rows_across = to_group(rows, 0, 1)
    taps_here = lax.all_gather(rows, "rep", axis_index_groups=along_z)
    taps_across = lax.all_gather(rows_across, "rep", axis_index_groups=along_z)

    def sums(offsets, parity):
        blocks = jnp.stack([tr_index(y + dy, x_high + dx, parity) for dy, dx in offsets])
        return products(rows, weight, blocks.astype(jnp.int32), wide)

    crossing = [to_sibling(sums(offsets, 1 - core)) for offsets in ORDER]
    pairs_of = {}
    for offsets, other in zip(ORDER, crossing):
        own = sums(offsets, core)
        for i, offset in enumerate(offsets):
            pairs_of[offset] = (own[i], other[i])

    def chip_sum(dy, dx):
        own, other = pairs_of[dy, dx]
        return (own + other) * SEND

    def send(value, dy, dx):
        return to_chip(value.astype(f16), dy, dx)

    far_across = send(chip_sum(2, 1), 0, 1).astype(f32)
    up_across = send(chip_sum(1, 1), 1, 0).astype(f32)
    down_across = send(chip_sum(3, 1), 3, 0).astype(f32)
    up = send(chip_sum(1, 0), 1, 0).astype(f32)
    down = send(chip_sum(3, 0), 3, 0).astype(f32)
    far = send(chip_sum(2, 0) + far_across, 2, 0).astype(f32)
    across = send(chip_sum(0, 1) + up_across + down_across, 0, 1).astype(f32)
    merged = (chip_sum(0, 0) + up + down + far + across) * (1.0 / SEND)
    merged = merged.reshape(slots, span, wide)
    squares = sum_over_tr(jnp.sum(merged * merged, axis=2))

    scaled, crossed = attention(
        lens,
        weights,
        head_scale,
        merged,
        squares.reshape(slots, 1, span),
        norm_gain.reshape(1, wide),
        taps[:, :, 2, :],
    )
    crossed = sum_over_tr(crossed.reshape(slots, span))
    inverse = lax.rsqrt(squares / width_all + epsilon)
    merged_grad = (
        scaled * inverse[:, :, None]
        - merged * (inverse * inverse * inverse * crossed / width_all)[:, :, None]
    ).astype(bf16)

    chips = lax.axis_size("tr")
    pairs = [
        (
            (at_z * 2 + at_x) * chips + tr_index(at_y, at_high, at_core),
            (at_y * 2 + at_high) * chips + tr_index(at_y + at_z, at_x, at_core),
        )
        for at_z in range(RING)
        for at_x in range(2)
        for at_y in range(RING)
        for at_high in range(2)
        for at_core in range(2)
    ]
    turned = lax.ppermute(merged_grad.reshape(slots * span, wide), ("rep", "tr"), pairs)
    own_half = gather(turned, to_chip)
    other_half = {k: to_sibling(v) for k, v in own_half.items()}

    all_rows = jnp.concatenate([taps_here, taps_across], axis=0)

    def gradient(half):
        total = None
        for (a, b), piece in half.items():
            place = (x_low + x_high - b) % 2 * RING + (y - a - z) % RING
            source = lax.dynamic_index_in_dim(all_rows, place, 0, keepdims=False)
            part = lax.dot_general(source, piece, COLS_COLS, preferred_element_type=f32)
            total = part if total is None else total + part
        return total

    grad = jnp.zeros((flat_in, block), f32)
    for half, parity in ((own_half, core), (other_half, 1 - core)):
        grad = lax.dynamic_update_slice_in_dim(grad, gradient(half), parity * wide, 1)
    old = lax.dynamic_slice_in_dim(weight, rep * block, block, 1)
    new_block = (old.astype(f32) - step_size * grad).astype(bf16)
    new = jnp.zeros((flat_in, width_all), bf16)
    for a, b, first, piece in gather_relayed(new_block, to_group):
        owner = (z - a) % RING * 2 + (x_low - b) % 2
        new = lax.dynamic_update_slice(new, piece, (first, owner * block))
    return grad.reshape(tap_count, wide, block), new.reshape(tap_count, wide, width_all)


def solution(mesh):
    in_specs = (P("rep", None, None, "tr"), P(), P(), P(None, "tr", None), P("tr"), P("tr"))
    out_specs = (P(None, "tr", "rep"), P(None, "tr", None))
    return jax.shard_map(
        per_device, mesh=mesh, in_specs=in_specs, out_specs=out_specs, check_vma=False
    )
```

```python
import jax
import jax.numpy as jnp
from jax import lax
from jax.experimental import pallas as pl
from jax.experimental.layout import Layout, with_layout_constraint
from jax.experimental.pallas import tpu as pltpu
from jax.sharding import PartitionSpec as P

epsilon = 1e-06
step_size = 0.004
SEND = 128.0
SPAN = 96
HEAD = 128
RING = 4
ORDER = (((2, 1), (1, 1), (3, 1), (1, 0)), ((3, 0), (2, 0), (0, 1), (0, 0)))

f32 = jnp.float32
bf16 = jnp.bfloat16
f16 = jnp.float16

ROWS_ROWS = (((1,), (1,)), ((), ()))
ROWS_COLS = (((1,), (0,)), ((), ()))
COLS_COLS = (((0,), (0,)), ((), ()))


def split(a):
    high = a.astype(bf16)
    return high, (a - high.astype(f32)).astype(bf16)


def product(a, b, dims):
    ka, kb = dims[0][0][0], dims[0][1][0]
    return lax.dot_general(
        jnp.concatenate([a[0], a[0], a[1]], axis=ka),
        jnp.concatenate([b[0], b[1], b[0]], axis=kb),
        dims,
        preferred_element_type=f32,
    )


def attention_kernel(lens_ref, weights_ref, scale_ref, merged_ref, square_ref, gain_ref, tap_ref, scaled_ref, cross_ref):
    slots = merged_ref.shape[0]
    heads = scale_ref.shape[0]
    first = pl.program_id(0) * slots
    place = lax.broadcasted_iota(jnp.int32, (SPAN, HEAD), 0)
    key = lax.broadcasted_iota(jnp.int32, (SPAN, HEAD), 1)
    eye = lax.broadcasted_iota(jnp.int32, (SPAN, SPAN), 0) == lax.broadcasted_iota(jnp.int32, (SPAN, SPAN), 1)
    pad = jnp.zeros((HEAD - SPAN, HEAD), f32)
    chains = [(s, h) for s in range(slots) for h in range(heads)]
    every = range(len(chains))
    width = 16 * heads * HEAD
    lens = [lens_ref[first + s] for s, _ in chains]
    weights = [weights_ref[first + s] for s, _ in chains]
    scales = [scale_ref[h] for _, h in chains]
    columns = [pl.ds(h * HEAD, HEAD) for _, h in chains]
    allowed = [(key <= place) & (key < lens[c]) for c in every]
    inverse = []
    for s in range(slots):
        across = lax.rsqrt(square_ref[s] / width + epsilon)
        inverse.append(jnp.sum(jnp.where(eye, across, 0.0), axis=1, keepdims=True))
    gains = [gain_ref[:, columns[c]] for c in every]
    start = [merged_ref[chains[c][0], :, columns[c]] * inverse[chains[c][0]] * gains[c] for c in every]
    keys = [split(jnp.concatenate([start[c], pad], axis=0)) for c in every]
    current = list(start)
    queries, shares, loss_grads = [], [], []
    for step in range(3):
        parts = [split(current[c]) for c in every]
        logits = [product(parts[c], keys[c], ROWS_ROWS) * scales[c] for c in every]
        logits = [jnp.where(allowed[c], logits[c], -1e30) for c in every]
        raised = [jnp.exp(logits[c] - jnp.max(logits[c], axis=1, keepdims=True)) for c in every]
        share = [raised[c] / jnp.sum(raised[c], axis=1, keepdims=True) for c in every]
        share_parts = [split(share[c]) for c in every]
        attended = [product(share_parts[c], keys[c], ROWS_COLS) for c in every]
        current = [current[c] + attended[c] for c in every]
        queries.append(parts)
        shares.append((share, share_parts))
        grads = []
        for c in every:
            later = pltpu.roll(tap_ref[chains[c][0], :, columns[c]].astype(f32), SPAN - (step + 1), 0)
            active = jnp.where(place + (step + 1) < lens[c], 2.0 * weights[c], 0.0)
            grads.append(active * (current[c] - later))
        loss_grads.append(grads)
    grad = loss_grads[2]
    key_grad = None
    for step in (2, 1, 0):
        share, share_parts = shares[step]
        parts = [split(grad[c]) for c in every]
        share_grad = [product(parts[c], keys[c], ROWS_ROWS) for c in every]
        inner = [jnp.sum(share_grad[c] * share[c], axis=1, keepdims=True) for c in every]
        logit_parts = [split(share[c] * (share_grad[c] - inner[c]) * scales[c]) for c in every]
        left = [tuple(jnp.concatenate(z, axis=0) for z in zip(share_parts[c], logit_parts[c])) for c in every]
        right = [tuple(jnp.concatenate(z, axis=0) for z in zip(parts[c], queries[step][c])) for c in every]
        added = [product(left[c], right[c], COLS_COLS) for c in every]
        key_grad = added if key_grad is None else [key_grad[c] + added[c] for c in every]
        grad = [grad[c] + product(logit_parts[c], keys[c], ROWS_COLS) for c in every]
        if step > 0:
            grad = [grad[c] + loss_grads[step - 1][c] for c in every]
    crossed = [None] * slots
    for c in every:
        s = chains[c][0]
        scaled = (grad[c] + key_grad[c][:SPAN]) * gains[c]
        scaled_ref[s, :, columns[c]] = scaled
        inner = jnp.sum(scaled * merged_ref[s, :, columns[c]], axis=1, keepdims=True)
        crossed[s] = inner if crossed[s] is None else crossed[s] + inner
    for s in range(slots):
        cross_ref[s] = jnp.sum(jnp.where(eye, crossed[s], 0.0), axis=0, keepdims=True)


def attention(lens, weights, scales, merged, squares, gain, taps, slots=2):
    count, span, wide = merged.shape
    scalar = pl.BlockSpec(memory_space=pltpu.SMEM)
    block = pl.BlockSpec((slots, span, wide), lambda i: (i, 0, 0))
    flat = pl.BlockSpec((slots, 1, span), lambda i: (i, 0, 0))
    return pl.pallas_call(
        attention_kernel,
        grid=(count // slots,),
        in_specs=[scalar, scalar, scalar, block, flat, pl.BlockSpec((1, wide), lambda i: (0, 0)), block],
        out_specs=[block, flat],
        out_shape=[
            jax.ShapeDtypeStruct((count, span, wide), f32),
            jax.ShapeDtypeStruct((count, 1, span), f32),
        ],
        compiler_params=pltpu.CompilerParams(vmem_limit_bytes=48 * 2**20),
        cost_estimate=pl.CostEstimate(flops=2 * 10**9, bytes_accessed=3 * 10**6, transcendentals=10**6),
    )(lens, weights, scales, merged, squares, gain, taps)


def row_major(a):
    return with_layout_constraint(a, Layout(major_to_minor=tuple(range(a.ndim))))


def buffer(shape, dtype):
    return pl.pallas_call(
        lambda out_ref: None,
        out_specs=pl.BlockSpec(memory_space=pl.ANY),
        out_shape=jax.ShapeDtypeStruct(shape, dtype),
    )()


def tr_index(y, x, core):
    return (y % RING * 2 + x % 2) * 2 + core % 2


def to_chip(value, dy, dx, dcore=0):
    pairs = [
        (tr_index(y, x, core), tr_index(y + dy, x + dx, core + dcore))
        for y in range(RING)
        for x in range(2)
        for core in range(2)
    ]
    return lax.ppermute(value, "tr", pairs)


def to_group(value, dz, dx):
    pairs = [(z * 2 + x, (z + dz) % RING * 2 + (x + dx) % 2) for z in range(RING) for x in range(2)]
    return lax.ppermute(value, "rep", pairs)


def to_sibling(value):
    return to_chip(value, 0, 0, 1)


def gather(value, send):
    got = {(0, 0): value}
    got[1, 0] = send(value, 1, 0)
    got[3, 0] = send(value, 3, 0)
    got[0, 1] = send(value, 0, 1)
    got[2, 0] = send(value, 2, 0)
    got[1, 1] = send(got[0, 1], 1, 0)
    got[3, 1] = send(got[0, 1], 3, 0)
    got[2, 1] = send(got[2, 0], 0, 1)
    return got


def gather_relayed(value, send):
    half = value.shape[0] // 2
    up, down, across = send(value, 1, 0), send(value, 3, 0), send(value, 0, 1)
    far_first = send(up[:half], 1, 0)
    far_last = send(down[half:], 3, 0)
    up_across, down_across = send(across, 1, 0), send(across, 3, 0)
    far_across = send(jnp.concatenate([far_first, far_last], axis=0), 0, 1)
    return [
        (0, 0, 0, value),
        (1, 0, 0, up),
        (3, 0, 0, down),
        (0, 1, 0, across),
        (2, 0, 0, far_first),
        (2, 0, half, far_last),
        (1, 1, 0, up_across),
        (3, 1, 0, down_across),
        (2, 1, 0, far_across),
    ]


def product_kernel(blocks_ref, rows_ref, weight_ref, out_ref):
    out_ref[0] = jnp.dot(rows_ref[...], weight_ref[...], preferred_element_type=f32)


def products(rows, weight, blocks, wide):
    count, depth = rows.shape
    number = blocks.shape[0]
    return pl.pallas_call(
        product_kernel,
        grid_spec=pltpu.PrefetchScalarGridSpec(
            num_scalar_prefetch=1,
            grid=(number,),
            in_specs=[
                pl.BlockSpec((count, depth), lambda i, blocks: (0, 0)),
                pl.BlockSpec((depth, wide), lambda i, blocks: (0, blocks[i])),
            ],
            out_specs=pl.BlockSpec((1, count, wide), lambda i, blocks: (i, 0, 0)),
        ),
        out_shape=jax.ShapeDtypeStruct((number, count, wide), f32),
        compiler_params=pltpu.CompilerParams(vmem_limit_bytes=8 * 2**20),
        cost_estimate=pl.CostEstimate(
            flops=2 * count * depth * wide * number,
            bytes_accessed=count * depth * 2 + number * wide * (count * 4 + depth * 2),
            transcendentals=0,
        ),
    )(blocks, rows, weight)


def sum_over_tr(value):
    value = value + to_sibling(value)
    value = value + to_chip(value, 0, 1)
    return value + to_chip(value, 1, 0) + to_chip(value, 2, 0) + to_chip(value, 3, 0)


def per_device(taps, routes, lengths, merge_weight, norm_gain, head_scale):
    rep = lax.axis_index("rep")
    tr = lax.axis_index("tr")
    core = tr % 2
    x_high = tr // 2 % 2
    y = tr // 4
    x_low = rep % 2
    z = rep // 2
    slots, span, tap_count, wide = taps.shape
    width_all = merge_weight.shape[2]
    flat_in = tap_count * wide
    block = width_all // lax.axis_size("rep")
    rows = row_major(taps.reshape(slots * span, flat_in))
    weight = merge_weight.reshape(flat_in, width_all)

    dest = routes[:, 0]
    target = jnp.maximum(lengths - 1, 0) + jnp.maximum(lengths - 2, 0) + jnp.maximum(lengths - 3, 0)
    own_dest = lax.dynamic_slice_in_dim(dest, rep * slots, slots)
    lens = lax.dynamic_slice_in_dim(lengths, rep * slots, slots)
    count = jnp.sum(jnp.where(own_dest[:, None] == dest[None, :], target[None, :], 0), axis=1)
    weights = 1.0 / count.astype(f32)

    along_z = [[at_z * 2 + at_x for at_z in range(RING)] for at_x in range(2)]

    def gather_taps(value):
        return row_major(lax.all_gather(value, "rep", axis=0, tiled=True, axis_index_groups=along_z))

    rows_across = row_major(to_group(rows, 0, 1))
    taps_here = gather_taps(rows)

    def sums(offsets, parity):
        blocks = jnp.stack([tr_index(y + dy, x_high + dx, parity) for dy, dx in offsets])
        return products(rows, weight, blocks.astype(jnp.int32), wide)

    crossing = [to_sibling(sums(offsets, 1 - core)) for offsets in ORDER]
    pairs_of = {}
    for offsets, other in zip(ORDER, crossing):
        own = sums(offsets, core)
        for i, offset in enumerate(offsets):
            pairs_of[offset] = (own[i], other[i])

    def chip_sum(dy, dx):
        own, other = pairs_of[dy, dx]
        return (own + other) * SEND

    def send(value, dy, dx):
        return to_chip(value.astype(f16), dy, dx)

    far_across = send(chip_sum(2, 1), 0, 1)
    up_across = send(chip_sum(1, 1), 1, 0).astype(f32)
    down_across = send(chip_sum(3, 1), 3, 0).astype(f32)
    up = send(chip_sum(1, 0), 1, 0).astype(f32)
    down = send(chip_sum(3, 0), 3, 0).astype(f32)
    far_across, rows_across = lax.optimization_barrier((far_across, rows_across))
    taps_across = gather_taps(rows_across)
    far = send(chip_sum(2, 0) + far_across.astype(f32), 2, 0).astype(f32)
    across = send(chip_sum(0, 1) + up_across + down_across, 0, 1).astype(f32)
    merged = (chip_sum(0, 0) + up + down + far + across) * (1.0 / SEND)
    merged = merged.reshape(slots, span, wide)
    squares = sum_over_tr(jnp.sum(merged * merged, axis=2))

    scaled, crossed = attention(
        lens,
        weights,
        head_scale,
        merged,
        squares.reshape(slots, 1, span),
        norm_gain.reshape(1, wide),
        taps[:, :, 2, :],
    )
    crossed = sum_over_tr(crossed.reshape(slots, span))
    inverse = lax.rsqrt(squares / width_all + epsilon)
    merged_grad = (
        scaled * inverse[:, :, None]
        - merged * (inverse * inverse * inverse * crossed / width_all)[:, :, None]
    ).astype(bf16)

    chips = lax.axis_size("tr")
    pairs = [
        (
            (at_z * 2 + at_x) * chips + tr_index(at_y, at_high, at_core),
            (at_y * 2 + at_high) * chips + tr_index(at_y + at_z, at_x, at_core),
        )
        for at_z in range(RING)
        for at_x in range(2)
        for at_y in range(RING)
        for at_high in range(2)
        for at_core in range(2)
    ]
    turned = lax.ppermute(merged_grad.reshape(slots * span, wide), ("rep", "tr"), pairs)
    own_half = gather(turned, to_chip)
    other_half = {k: to_sibling(v) for k, v in own_half.items()}

    def gradient(half):
        total = None
        same = x_low == x_high
        for a in (0, 1, 3, 2):
            straight, crossed = half[a, 0], half[a, 1]
            for taps_of, piece in (
                (taps_here, jnp.where(same, straight, crossed)),
                (taps_across, jnp.where(same, crossed, straight)),
            ):
                at_z = (y - a - z) % RING
                source = lax.dynamic_slice_in_dim(taps_of, at_z * slots * span, slots * span, 0)
                part = lax.dot_general(source, piece, COLS_COLS, preferred_element_type=f32)
                total = part if total is None else total + part
        return total

    grad = buffer((flat_in, block), f32)
    for half, parity in ((own_half, core), (other_half, 1 - core)):
        grad = lax.dynamic_update_slice_in_dim(grad, gradient(half), parity * wide, 1)
    old = lax.dynamic_slice_in_dim(weight, rep * block, block, 1)
    new_block = (old.astype(f32) - step_size * grad).astype(bf16)
    new = buffer((flat_in, width_all), bf16)
    for a, b, first, piece in gather_relayed(new_block, to_group):
        owner = (z - a) % RING * 2 + (x_low - b) % 2
        new = lax.dynamic_update_slice(new, piece, (first, owner * block))
    return grad.reshape(tap_count, wide, block), new.reshape(tap_count, wide, width_all)


def solution(mesh):
    in_specs = (P("rep", None, None, "tr"), P(), P(), P(None, "tr", None), P("tr"), P("tr"))
    out_specs = (P(None, "tr", "rep"), P(None, "tr", None))
    return jax.shard_map(
        per_device, mesh=mesh, in_specs=in_specs, out_specs=out_specs, check_vma=False
    )
```

```python
import jax
import jax.numpy as jnp
from jax import lax
from jax.experimental import pallas as pl
from jax.experimental.layout import Layout, with_layout_constraint
from jax.experimental.pallas import tpu as pltpu
from jax.sharding import PartitionSpec as P

epsilon = 1e-06
step_size = 0.004
SEND = 128.0
SPAN = 96
HEAD = 128
RING = 4
ORDER = (((2, 1), (1, 1), (3, 1)), ((1, 0), (3, 0), (2, 0), (0, 1), (0, 0)))

f32 = jnp.float32
bf16 = jnp.bfloat16
f16 = jnp.float16

ROWS_ROWS = (((1,), (1,)), ((), ()))
ROWS_COLS = (((1,), (0,)), ((), ()))
COLS_COLS = (((0,), (0,)), ((), ()))


def split(a):
    high = a.astype(bf16)
    return high, (a - high.astype(f32)).astype(bf16)


def product(a, b, dims):
    ka, kb = dims[0][0][0], dims[0][1][0]
    return lax.dot_general(
        jnp.concatenate([a[0], a[0], a[1]], axis=ka),
        jnp.concatenate([b[0], b[1], b[0]], axis=kb),
        dims,
        preferred_element_type=f32,
    )


def attention_kernel(lens_ref, weights_ref, scale_ref, merged_ref, square_ref, gain_ref, tap_ref, scaled_ref, cross_ref):
    slots = merged_ref.shape[0]
    heads = scale_ref.shape[0]
    first = pl.program_id(0) * slots
    place = lax.broadcasted_iota(jnp.int32, (SPAN, HEAD), 0)
    key = lax.broadcasted_iota(jnp.int32, (SPAN, HEAD), 1)
    eye = lax.broadcasted_iota(jnp.int32, (SPAN, SPAN), 0) == lax.broadcasted_iota(jnp.int32, (SPAN, SPAN), 1)
    pad = jnp.zeros((HEAD - SPAN, HEAD), f32)
    chains = [(s, h) for s in range(slots) for h in range(heads)]
    every = range(len(chains))
    width = 16 * heads * HEAD
    lens = [lens_ref[first + s] for s, _ in chains]
    weights = [weights_ref[first + s] for s, _ in chains]
    scales = [scale_ref[h] for _, h in chains]
    columns = [pl.ds(h * HEAD, HEAD) for _, h in chains]
    allowed = [(key <= place) & (key < lens[c]) for c in every]
    inverse = []
    for s in range(slots):
        across = lax.rsqrt(square_ref[s] / width + epsilon)
        inverse.append(jnp.sum(jnp.where(eye, across, 0.0), axis=1, keepdims=True))
    gains = [gain_ref[:, columns[c]] for c in every]
    start = [merged_ref[chains[c][0], :, columns[c]] * inverse[chains[c][0]] * gains[c] for c in every]
    keys = [split(jnp.concatenate([start[c], pad], axis=0)) for c in every]
    current = list(start)
    queries, shares, loss_grads = [], [], []
    for step in range(3):
        parts = [split(current[c]) for c in every]
        logits = [product(parts[c], keys[c], ROWS_ROWS) * scales[c] for c in every]
        logits = [jnp.where(allowed[c], logits[c], -1e30) for c in every]
        raised = [jnp.exp(logits[c] - jnp.max(logits[c], axis=1, keepdims=True)) for c in every]
        share = [raised[c] / jnp.sum(raised[c], axis=1, keepdims=True) for c in every]
        share_parts = [split(share[c]) for c in every]
        attended = [product(share_parts[c], keys[c], ROWS_COLS) for c in every]
        current = [current[c] + attended[c] for c in every]
        queries.append(parts)
        shares.append((share, share_parts))
        grads = []
        for c in every:
            later = pltpu.roll(tap_ref[chains[c][0], :, columns[c]].astype(f32), SPAN - (step + 1), 0)
            active = jnp.where(place + (step + 1) < lens[c], 2.0 * weights[c], 0.0)
            grads.append(active * (current[c] - later))
        loss_grads.append(grads)
    grad = loss_grads[2]
    key_grad = None
    for step in (2, 1, 0):
        share, share_parts = shares[step]
        parts = [split(grad[c]) for c in every]
        share_grad = [product(parts[c], keys[c], ROWS_ROWS) for c in every]
        inner = [jnp.sum(share_grad[c] * share[c], axis=1, keepdims=True) for c in every]
        logit_parts = [split(share[c] * (share_grad[c] - inner[c]) * scales[c]) for c in every]
        left = [tuple(jnp.concatenate(z, axis=0) for z in zip(share_parts[c], logit_parts[c])) for c in every]
        right = [tuple(jnp.concatenate(z, axis=0) for z in zip(parts[c], queries[step][c])) for c in every]
        added = [product(left[c], right[c], COLS_COLS) for c in every]
        key_grad = added if key_grad is None else [key_grad[c] + added[c] for c in every]
        grad = [grad[c] + product(logit_parts[c], keys[c], ROWS_COLS) for c in every]
        if step > 0:
            grad = [grad[c] + loss_grads[step - 1][c] for c in every]
    crossed = [None] * slots
    for c in every:
        s = chains[c][0]
        scaled = (grad[c] + key_grad[c][:SPAN]) * gains[c]
        scaled_ref[s, :, columns[c]] = scaled
        inner = jnp.sum(scaled * merged_ref[s, :, columns[c]], axis=1, keepdims=True)
        crossed[s] = inner if crossed[s] is None else crossed[s] + inner
    for s in range(slots):
        cross_ref[s] = jnp.sum(jnp.where(eye, crossed[s], 0.0), axis=0, keepdims=True)


def attention(lens, weights, scales, merged, squares, gain, taps, slots=2):
    count, span, wide = merged.shape
    scalar = pl.BlockSpec(memory_space=pltpu.SMEM)
    block = pl.BlockSpec((slots, span, wide), lambda i: (i, 0, 0))
    flat = pl.BlockSpec((slots, 1, span), lambda i: (i, 0, 0))
    return pl.pallas_call(
        attention_kernel,
        grid=(count // slots,),
        in_specs=[scalar, scalar, scalar, block, flat, pl.BlockSpec((1, wide), lambda i: (0, 0)), block],
        out_specs=[block, flat],
        out_shape=[
            jax.ShapeDtypeStruct((count, span, wide), f32),
            jax.ShapeDtypeStruct((count, 1, span), f32),
        ],
        compiler_params=pltpu.CompilerParams(vmem_limit_bytes=16 * 2**20),
        cost_estimate=pl.CostEstimate(flops=2 * 10**9, bytes_accessed=3 * 10**6, transcendentals=10**6),
    )(lens, weights, scales, merged, squares, gain, taps)


def row_major(a):
    return with_layout_constraint(a, Layout(major_to_minor=tuple(range(a.ndim))))


def buffer(shape, dtype):
    return pl.pallas_call(
        lambda out_ref: None,
        out_specs=pl.BlockSpec(memory_space=pl.ANY),
        out_shape=jax.ShapeDtypeStruct(shape, dtype),
    )()


def tr_index(y, x, core):
    return (y % RING * 2 + x % 2) * 2 + core % 2


def to_chip(value, dy, dx, dcore=0):
    pairs = [
        (tr_index(y, x, core), tr_index(y + dy, x + dx, core + dcore))
        for y in range(RING)
        for x in range(2)
        for core in range(2)
    ]
    return lax.ppermute(value, "tr", pairs)


def to_group(value, dz, dx):
    pairs = [(z * 2 + x, (z + dz) % RING * 2 + (x + dx) % 2) for z in range(RING) for x in range(2)]
    return lax.ppermute(value, "rep", pairs)


def to_sibling(value):
    return to_chip(value, 0, 0, 1)


def gather(value, send):
    got = {(0, 0): value}
    got[1, 0] = send(value, 1, 0)
    got[3, 0] = send(value, 3, 0)
    got[0, 1] = send(value, 0, 1)
    got[2, 0] = send(value, 2, 0)
    got[1, 1] = send(got[0, 1], 1, 0)
    got[3, 1] = send(got[0, 1], 3, 0)
    got[2, 1] = send(got[2, 0], 0, 1)
    return got


def gather_relayed(value, send):
    half = value.shape[0] // 2
    up, down, across = send(value, 1, 0), send(value, 3, 0), send(value, 0, 1)
    far_first = send(up[:half], 1, 0)
    far_last = send(down[half:], 3, 0)
    up_across, down_across = send(across, 1, 0), send(across, 3, 0)
    far_across = send(jnp.concatenate([far_first, far_last], axis=0), 0, 1)
    return [
        (0, 0, 0, value),
        (1, 0, 0, up),
        (3, 0, 0, down),
        (0, 1, 0, across),
        (2, 0, 0, far_first),
        (2, 0, half, far_last),
        (1, 1, 0, up_across),
        (3, 1, 0, down_across),
        (2, 1, 0, far_across),
    ]


def product_kernel(blocks_ref, rows_ref, weight_ref, out_ref):
    out_ref[0] = jnp.dot(rows_ref[...], weight_ref[...], preferred_element_type=f32)


def products(rows, weight, blocks, wide):
    count, depth = rows.shape
    number = blocks.shape[0]
    return pl.pallas_call(
        product_kernel,
        grid_spec=pltpu.PrefetchScalarGridSpec(
            num_scalar_prefetch=1,
            grid=(number,),
            in_specs=[
                pl.BlockSpec((count, depth), lambda i, blocks: (0, 0)),
                pl.BlockSpec((depth, wide), lambda i, blocks: (0, blocks[i])),
            ],
            out_specs=pl.BlockSpec((1, count, wide), lambda i, blocks: (i, 0, 0)),
        ),
        out_shape=jax.ShapeDtypeStruct((number, count, wide), f32),
        compiler_params=pltpu.CompilerParams(vmem_limit_bytes=8 * 2**20),
        cost_estimate=pl.CostEstimate(
            flops=2 * count * depth * wide * number,
            bytes_accessed=count * depth * 2 + number * wide * (count * 4 + depth * 2),
            transcendentals=0,
        ),
    )(blocks, rows, weight)


def sum_over_tr(value):
    value = value + to_sibling(value)
    value = value + to_chip(value, 0, 1)
    return value + to_chip(value, 1, 0) + to_chip(value, 2, 0) + to_chip(value, 3, 0)


def per_device(taps, routes, lengths, merge_weight, norm_gain, head_scale):
    rep = lax.axis_index("rep")
    tr = lax.axis_index("tr")
    core = tr % 2
    x_high = tr // 2 % 2
    y = tr // 4
    x_low = rep % 2
    z = rep // 2
    slots, span, tap_count, wide = taps.shape
    width_all = merge_weight.shape[2]
    flat_in = tap_count * wide
    block = width_all // lax.axis_size("rep")
    rows = row_major(taps.reshape(slots * span, flat_in))
    weight = merge_weight.reshape(flat_in, width_all)

    dest = routes[:, 0]
    target = jnp.maximum(lengths - 1, 0) + jnp.maximum(lengths - 2, 0) + jnp.maximum(lengths - 3, 0)
    own_dest = lax.dynamic_slice_in_dim(dest, rep * slots, slots)
    lens = lax.dynamic_slice_in_dim(lengths, rep * slots, slots)
    count = jnp.sum(jnp.where(own_dest[:, None] == dest[None, :], target[None, :], 0), axis=1)
    weights = 1.0 / count.astype(f32)

    along_z = [[at_z * 2 + at_x for at_z in range(RING)] for at_x in range(2)]

    def gather_taps(value):
        return row_major(lax.all_gather(value, "rep", axis=0, tiled=True, axis_index_groups=along_z))

    taps_here = gather_taps(rows)

    def sums(rows, offsets, parity):
        blocks = jnp.stack([tr_index(y + dy, x_high + dx, parity) for dy, dx in offsets])
        return products(rows, weight, blocks.astype(jnp.int32), wide)

    def chip_sums(rows, offsets):
        other = to_sibling(sums(rows, offsets, 1 - core))
        own = sums(rows, offsets, core)
        return {offset: (own[i] + other[i]) * SEND for i, offset in enumerate(offsets)}

    def send(value, dy, dx):
        return to_chip(value.astype(f16), dy, dx)

    first = chip_sums(rows, ORDER[0])
    far_across, up_across, down_across, rows_now = lax.optimization_barrier(
        tuple(first[offset].astype(f16) for offset in ORDER[0]) + (rows,)
    )
    far_across = send(far_across, 0, 1)
    up_across = send(up_across, 1, 0)
    down_across = send(down_across, 3, 0)
    second = chip_sums(rows_now, ORDER[1])
    far_across, rows_now = lax.optimization_barrier((far_across, rows_now))
    rows_across = row_major(to_group(rows_now, 0, 1))
    up = send(second[1, 0], 1, 0).astype(f32)
    down = send(second[3, 0], 3, 0).astype(f32)
    far = send(second[2, 0] + far_across.astype(f32), 2, 0).astype(f32)
    across = send(second[0, 1] + up_across.astype(f32) + down_across.astype(f32), 0, 1).astype(f32)
    merged = (second[0, 0] + up + down + far + across) * (1.0 / SEND)
    merged = merged.reshape(slots, span, wide)
    squares = sum_over_tr(jnp.sum(merged * merged, axis=2))
    squares, rows_across = lax.optimization_barrier((squares, rows_across))
    taps_across = gather_taps(rows_across)

    scaled, crossed = attention(
        lens,
        weights,
        head_scale,
        merged,
        squares.reshape(slots, 1, span),
        norm_gain.reshape(1, wide),
        taps[:, :, 2, :],
    )
    crossed = sum_over_tr(crossed.reshape(slots, span))
    inverse = lax.rsqrt(squares / width_all + epsilon)
    merged_grad = (
        scaled * inverse[:, :, None]
        - merged * (inverse * inverse * inverse * crossed / width_all)[:, :, None]
    ).astype(bf16)

    chips = lax.axis_size("tr")
    pairs = [
        (
            (at_z * 2 + at_x) * chips + tr_index(at_y, at_high, at_core),
            (at_y * 2 + at_high) * chips + tr_index(at_y + at_z, at_x, at_core),
        )
        for at_z in range(RING)
        for at_x in range(2)
        for at_y in range(RING)
        for at_high in range(2)
        for at_core in range(2)
    ]
    turned = lax.ppermute(merged_grad.reshape(slots * span, wide), ("rep", "tr"), pairs)
    own_half = gather(turned, to_chip)
    other_half = {k: to_sibling(v) for k, v in own_half.items()}

    all_rows = buffer((2, RING * slots * span, flat_in), bf16)
    all_rows = lax.dynamic_update_slice(all_rows, taps_here[None], (0, 0, 0))
    all_rows = lax.dynamic_update_slice(all_rows, taps_across[None], (1, 0, 0))
    all_rows = all_rows.reshape(2 * RING, slots * span, flat_in)

    def gradient(half):
        total = None
        for (a, b), piece in half.items():
            place = (x_low + x_high - b) % 2 * RING + (y - a - z) % RING
            source = lax.dynamic_index_in_dim(all_rows, place, 0, keepdims=False)
            part = lax.dot_general(source, piece, COLS_COLS, preferred_element_type=f32)
            total = part if total is None else total + part
        return total

    grad = buffer((flat_in, block), f32)
    for half, parity in ((own_half, core), (other_half, 1 - core)):
        grad = lax.dynamic_update_slice_in_dim(grad, gradient(half), parity * wide, 1)
    old = lax.dynamic_slice_in_dim(weight, rep * block, block, 1)
    new_block = (old.astype(f32) - step_size * grad).astype(bf16)
    new = buffer((flat_in, width_all), bf16)
    for a, b, first, piece in gather_relayed(new_block, to_group):
        owner = (z - a) % RING * 2 + (x_low - b) % 2
        new = lax.dynamic_update_slice(new, piece, (first, owner * block))
    return grad.reshape(tap_count, wide, block), new.reshape(tap_count, wide, width_all)


def solution(mesh):
    in_specs = (P("rep", None, None, "tr"), P(), P(), P(None, "tr", None), P("tr"), P("tr"))
    out_specs = (P(None, "tr", "rep"), P(None, "tr", None))
    return jax.shard_map(
        per_device, mesh=mesh, in_specs=in_specs, out_specs=out_specs, check_vma=False
    )
```

```python
import jax
import jax.numpy as jnp
from jax import lax
from jax.experimental import pallas as pl
from jax.experimental.layout import Layout, with_layout_constraint
from jax.experimental.pallas import tpu as pltpu
from jax.sharding import PartitionSpec as P

epsilon = 1e-06
step_size = 0.004
SEND = 128.0
SPAN = 96
HEAD = 128
RING = 4
ORDER = ((2, 1), (1, 1), (3, 1), (1, 0), (3, 0), (2, 0), (0, 1), (0, 0))

f32 = jnp.float32
bf16 = jnp.bfloat16
f16 = jnp.float16

ROWS_ROWS = (((1,), (1,)), ((), ()))
ROWS_COLS = (((1,), (0,)), ((), ()))
COLS_COLS = (((0,), (0,)), ((), ()))


def split(a):
    high = a.astype(bf16)
    return high, (a - high.astype(f32)).astype(bf16)


def product(a, b, dims):
    ka, kb = dims[0][0][0], dims[0][1][0]
    return lax.dot_general(
        jnp.concatenate([a[0], a[0], a[1]], axis=ka),
        jnp.concatenate([b[0], b[1], b[0]], axis=kb),
        dims,
        preferred_element_type=f32,
    )


def attention_kernel(lens_ref, weights_ref, scale_ref, merged_ref, square_ref, gain_ref, tap_ref, scaled_ref, cross_ref):
    slots = merged_ref.shape[0]
    heads = scale_ref.shape[0]
    first = pl.program_id(0) * slots
    place = lax.broadcasted_iota(jnp.int32, (SPAN, HEAD), 0)
    key = lax.broadcasted_iota(jnp.int32, (SPAN, HEAD), 1)
    eye = lax.broadcasted_iota(jnp.int32, (SPAN, SPAN), 0) == lax.broadcasted_iota(jnp.int32, (SPAN, SPAN), 1)
    pad = jnp.zeros((HEAD - SPAN, HEAD), f32)
    chains = [(s, h) for s in range(slots) for h in range(heads)]
    every = range(len(chains))
    width = 16 * heads * HEAD
    lens = [lens_ref[first + s] for s, _ in chains]
    weights = [weights_ref[first + s] for s, _ in chains]
    scales = [scale_ref[h] for _, h in chains]
    columns = [pl.ds(h * HEAD, HEAD) for _, h in chains]
    allowed = [(key <= place) & (key < lens[c]) for c in every]
    inverse = []
    for s in range(slots):
        across = lax.rsqrt(square_ref[s] / width + epsilon)
        inverse.append(jnp.sum(jnp.where(eye, across, 0.0), axis=1, keepdims=True))
    gains = [gain_ref[:, columns[c]] for c in every]
    start = [merged_ref[chains[c][0], :, columns[c]] * inverse[chains[c][0]] * gains[c] for c in every]
    keys = [split(jnp.concatenate([start[c], pad], axis=0)) for c in every]
    current = list(start)
    queries, shares, loss_grads = [], [], []
    for step in range(3):
        parts = [split(current[c]) for c in every]
        logits = [product(parts[c], keys[c], ROWS_ROWS) * scales[c] for c in every]
        logits = [jnp.where(allowed[c], logits[c], -1e30) for c in every]
        raised = [jnp.exp(logits[c] - jnp.max(logits[c], axis=1, keepdims=True)) for c in every]
        share = [raised[c] / jnp.sum(raised[c], axis=1, keepdims=True) for c in every]
        share_parts = [split(share[c]) for c in every]
        attended = [product(share_parts[c], keys[c], ROWS_COLS) for c in every]
        current = [current[c] + attended[c] for c in every]
        queries.append(parts)
        shares.append((share, share_parts))
        grads = []
        for c in every:
            later = pltpu.roll(tap_ref[chains[c][0], :, columns[c]].astype(f32), SPAN - (step + 1), 0)
            active = jnp.where(place + (step + 1) < lens[c], 2.0 * weights[c], 0.0)
            grads.append(active * (current[c] - later))
        loss_grads.append(grads)
    grad = loss_grads[2]
    key_grad = None
    for step in (2, 1, 0):
        share, share_parts = shares[step]
        parts = [split(grad[c]) for c in every]
        share_grad = [product(parts[c], keys[c], ROWS_ROWS) for c in every]
        inner = [jnp.sum(share_grad[c] * share[c], axis=1, keepdims=True) for c in every]
        logit_parts = [split(share[c] * (share_grad[c] - inner[c]) * scales[c]) for c in every]
        left = [tuple(jnp.concatenate(z, axis=0) for z in zip(share_parts[c], logit_parts[c])) for c in every]
        right = [tuple(jnp.concatenate(z, axis=0) for z in zip(parts[c], queries[step][c])) for c in every]
        added = [product(left[c], right[c], COLS_COLS) for c in every]
        key_grad = added if key_grad is None else [key_grad[c] + added[c] for c in every]
        grad = [grad[c] + product(logit_parts[c], keys[c], ROWS_COLS) for c in every]
        if step > 0:
            grad = [grad[c] + loss_grads[step - 1][c] for c in every]
    crossed = [None] * slots
    for c in every:
        s = chains[c][0]
        scaled = (grad[c] + key_grad[c][:SPAN]) * gains[c]
        scaled_ref[s, :, columns[c]] = scaled
        inner = jnp.sum(scaled * merged_ref[s, :, columns[c]], axis=1, keepdims=True)
        crossed[s] = inner if crossed[s] is None else crossed[s] + inner
    for s in range(slots):
        cross_ref[s] = jnp.sum(jnp.where(eye, crossed[s], 0.0), axis=0, keepdims=True)


def attention(lens, weights, scales, merged, squares, gain, taps, slots=2):
    count, span, wide = merged.shape
    scalar = pl.BlockSpec(memory_space=pltpu.SMEM)
    block = pl.BlockSpec((slots, span, wide), lambda i: (i, 0, 0))
    flat = pl.BlockSpec((slots, 1, span), lambda i: (i, 0, 0))
    return pl.pallas_call(
        attention_kernel,
        grid=(count // slots,),
        in_specs=[scalar, scalar, scalar, block, flat, pl.BlockSpec((1, wide), lambda i: (0, 0)), block],
        out_specs=[block, flat],
        out_shape=[
            jax.ShapeDtypeStruct((count, span, wide), f32),
            jax.ShapeDtypeStruct((count, 1, span), f32),
        ],
        compiler_params=pltpu.CompilerParams(vmem_limit_bytes=16 * 2**20),
        cost_estimate=pl.CostEstimate(flops=2 * 10**9, bytes_accessed=3 * 10**6, transcendentals=10**6),
    )(lens, weights, scales, merged, squares, gain, taps)


def row_major(a):
    return with_layout_constraint(a, Layout(major_to_minor=tuple(range(a.ndim))))


def buffer(shape, dtype):
    return pl.pallas_call(
        lambda out_ref: None,
        out_specs=pl.BlockSpec(memory_space=pl.ANY),
        out_shape=jax.ShapeDtypeStruct(shape, dtype),
    )()


def tr_index(y, x, core):
    return (y % RING * 2 + x % 2) * 2 + core % 2


def to_chip(value, dy, dx, dcore=0):
    pairs = [
        (tr_index(y, x, core), tr_index(y + dy, x + dx, core + dcore))
        for y in range(RING)
        for x in range(2)
        for core in range(2)
    ]
    return lax.ppermute(value, "tr", pairs)


def to_group(value, dz, dx):
    pairs = [(z * 2 + x, (z + dz) % RING * 2 + (x + dx) % 2) for z in range(RING) for x in range(2)]
    return lax.ppermute(value, "rep", pairs)


def to_sibling(value):
    return to_chip(value, 0, 0, 1)


def gather(value, send):
    got = {(0, 0): value}
    got[1, 0] = send(value, 1, 0)
    got[3, 0] = send(value, 3, 0)
    got[0, 1] = send(value, 0, 1)
    got[2, 0] = send(value, 2, 0)
    got[1, 1] = send(got[0, 1], 1, 0)
    got[3, 1] = send(got[0, 1], 3, 0)
    got[2, 1] = send(got[2, 0], 0, 1)
    return got


def gather_relayed(value, send):
    half = value.shape[0] // 2
    up, down, across = send(value, 1, 0), send(value, 3, 0), send(value, 0, 1)
    far_first = send(up[:half], 1, 0)
    far_last = send(down[half:], 3, 0)
    up_across, down_across = send(across, 1, 0), send(across, 3, 0)
    far_across = send(jnp.concatenate([far_first, far_last], axis=0), 0, 1)
    return [
        (0, 0, 0, value),
        (1, 0, 0, up),
        (3, 0, 0, down),
        (0, 1, 0, across),
        (2, 0, 0, far_first),
        (2, 0, half, far_last),
        (1, 1, 0, up_across),
        (3, 1, 0, down_across),
        (2, 1, 0, far_across),
    ]


def product_kernel(blocks_ref, rows_ref, weight_ref, out_ref):
    out_ref[0] = jnp.dot(rows_ref[...], weight_ref[...], preferred_element_type=f32)


def products(rows, weight, blocks, wide):
    count, depth = rows.shape
    number = blocks.shape[0]
    return pl.pallas_call(
        product_kernel,
        grid_spec=pltpu.PrefetchScalarGridSpec(
            num_scalar_prefetch=1,
            grid=(number,),
            in_specs=[
                pl.BlockSpec((count, depth), lambda i, blocks: (0, 0)),
                pl.BlockSpec((depth, wide), lambda i, blocks: (0, blocks[i])),
            ],
            out_specs=pl.BlockSpec((1, count, wide), lambda i, blocks: (i, 0, 0)),
        ),
        out_shape=jax.ShapeDtypeStruct((number, count, wide), f32),
        compiler_params=pltpu.CompilerParams(vmem_limit_bytes=8 * 2**20),
        cost_estimate=pl.CostEstimate(
            flops=2 * count * depth * wide * number,
            bytes_accessed=count * depth * 2 + number * wide * (count * 4 + depth * 2),
            transcendentals=0,
        ),
    )(blocks, rows, weight)


def sum_over_tr(value):
    value = value + to_sibling(value)
    value = value + to_chip(value, 0, 1)
    return value + to_chip(value, 1, 0) + to_chip(value, 2, 0) + to_chip(value, 3, 0)


def per_device(taps, routes, lengths, merge_weight, norm_gain, head_scale):
    rep = lax.axis_index("rep")
    tr = lax.axis_index("tr")
    core = tr % 2
    x_high = tr // 2 % 2
    y = tr // 4
    x_low = rep % 2
    z = rep // 2
    slots, span, tap_count, wide = taps.shape
    width_all = merge_weight.shape[2]
    flat_in = tap_count * wide
    block = width_all // lax.axis_size("rep")
    rows = row_major(taps.reshape(slots * span, flat_in))
    weight = merge_weight.reshape(flat_in, width_all)

    dest = routes[:, 0]
    target = jnp.maximum(lengths - 1, 0) + jnp.maximum(lengths - 2, 0) + jnp.maximum(lengths - 3, 0)
    own_dest = lax.dynamic_slice_in_dim(dest, rep * slots, slots)
    lens = lax.dynamic_slice_in_dim(lengths, rep * slots, slots)
    count = jnp.sum(jnp.where(own_dest[:, None] == dest[None, :], target[None, :], 0), axis=1)
    weights = 1.0 / count.astype(f32)

    tap_rows = {(0, 0): rows}
    for a, b in ((1, 0), (3, 0), (0, 1)):
        tap_rows[a, b] = to_group(rows, a, b)

    def sums(rows, offsets, parity):
        blocks = jnp.stack([tr_index(y + dy, x_high + dx, parity) for dy, dx in offsets])
        return products(rows, weight, blocks.astype(jnp.int32), wide)

    def chip_sums(rows, offsets):
        other = to_sibling(sums(rows, offsets, 1 - core))
        own = sums(rows, offsets, core)
        return {offset: (own[i] + other[i]) * SEND for i, offset in enumerate(offsets)}

    def send(value, dy, dx):
        return to_chip(value.astype(f16), dy, dx)

    total = chip_sums(rows, ORDER)
    far_across = send(total[2, 1], 0, 1)
    up_across = send(total[1, 1], 1, 0)
    down_across = send(total[3, 1], 3, 0)
    far_across, up_across, down_across, tap_rows[1, 0], tap_rows[3, 0], tap_rows[0, 1], rows = lax.optimization_barrier(
        (far_across, up_across, down_across, tap_rows[1, 0], tap_rows[3, 0], tap_rows[0, 1], rows)
    )
    up = send(total[1, 0], 1, 0).astype(f32)
    down = send(total[3, 0], 3, 0).astype(f32)
    far = send(total[2, 0] + far_across.astype(f32), 2, 0).astype(f32)
    across = send(total[0, 1] + up_across.astype(f32) + down_across.astype(f32), 0, 1).astype(f32)
    tap_rows[2, 0] = to_group(rows, 2, 0)
    merged = (total[0, 0] + up + down + far + across) * (1.0 / SEND)
    merged = merged.reshape(slots, span, wide)
    merged, tap_rows[0, 1] = lax.optimization_barrier((merged, tap_rows[0, 1]))
    tap_rows[1, 1] = to_group(tap_rows[0, 1], 1, 0)
    tap_rows[3, 1] = to_group(tap_rows[0, 1], 3, 0)
    squares = sum_over_tr(jnp.sum(merged * merged, axis=2))
    squares, tap_rows[2, 0] = lax.optimization_barrier((squares, tap_rows[2, 0]))

    scaled, crossed = attention(
        lens,
        weights,
        head_scale,
        merged,
        squares.reshape(slots, 1, span),
        norm_gain.reshape(1, wide),
        taps[:, :, 2, :],
    )
    crossed, tap_rows[0, 1], tap_rows[1, 1], tap_rows[3, 1] = lax.optimization_barrier(
        (crossed, tap_rows[0, 1], tap_rows[1, 1], tap_rows[3, 1])
    )
    tap_rows[2, 1] = to_group(tap_rows[0, 1], 2, 0)
    crossed = sum_over_tr(crossed.reshape(slots, span))
    inverse = lax.rsqrt(squares / width_all + epsilon)
    merged_grad = (
        scaled * inverse[:, :, None]
        - merged * (inverse * inverse * inverse * crossed / width_all)[:, :, None]
    ).astype(bf16)

    chips = lax.axis_size("tr")
    pairs = [
        (
            (at_z * 2 + at_x) * chips + tr_index(at_y, at_high, at_core),
            (at_y * 2 + at_high) * chips + tr_index(at_y + at_z, at_x, at_core),
        )
        for at_z in range(RING)
        for at_x in range(2)
        for at_y in range(RING)
        for at_high in range(2)
        for at_core in range(2)
    ]
    turned = lax.ppermute(merged_grad.reshape(slots * span, wide), ("rep", "tr"), pairs)
    turned, tap_rows[2, 1] = lax.optimization_barrier((turned, tap_rows[2, 1]))
    own_half = gather(turned, to_chip)
    all_grads = buffer((RING * 2, slots * span, block), bf16)
    for (a, b), piece in own_half.items():
        all_grads = lax.dynamic_update_slice(all_grads, piece[None], (a * 2 + b, 0, core * wide))
        other = to_sibling(piece)
        all_grads = lax.dynamic_update_slice(all_grads, other[None], (a * 2 + b, 0, (1 - core) * wide))

    grad = None
    for a, b in ((0, 0), (1, 0), (3, 0), (2, 0), (0, 1), (1, 1), (3, 1), (2, 1)):
        place = (y - 2 * z + a) % RING * 2 + (x_high - x_low + b) % 2
        part = lax.dot_general(
            tap_rows[a, b],
            lax.dynamic_index_in_dim(all_grads, place, 0, keepdims=False),
            COLS_COLS,
            preferred_element_type=f32,
        )
        grad = part if grad is None else grad + part
    old = lax.dynamic_slice_in_dim(weight, rep * block, block, 1)
    new_block = (old.astype(f32) - step_size * grad).astype(bf16)
    new = buffer((flat_in, width_all), bf16)
    for a, b, first, piece in gather_relayed(new_block, to_group):
        owner = (z - a) % RING * 2 + (x_low - b) % 2
        new = lax.dynamic_update_slice(new, piece, (first, owner * block))
    return grad.reshape(tap_count, wide, block), new.reshape(tap_count, wide, width_all)


def solution(mesh):
    in_specs = (P("rep", None, None, "tr"), P(), P(), P(None, "tr", None), P("tr"), P("tr"))
    out_specs = (P(None, "tr", "rep"), P(None, "tr", None))
    return jax.shard_map(
        per_device, mesh=mesh, in_specs=in_specs, out_specs=out_specs, check_vma=False
    )
```

```python
import jax
import jax.numpy as jnp
from jax import lax
from jax.experimental import pallas as pl
from jax.experimental.layout import Layout, with_layout_constraint
from jax.experimental.pallas import tpu as pltpu
from jax.sharding import PartitionSpec as P

epsilon = 1e-06
step_size = 0.004
SEND = 128.0
SPAN = 96
HEAD = 128
RING = 4
ORDER = (((2, 1), (1, 1), (3, 1)), ((1, 0), (3, 0), (2, 0), (0, 1), (0, 0)))

f32 = jnp.float32
bf16 = jnp.bfloat16
f16 = jnp.float16

ROWS_ROWS = (((1,), (1,)), ((), ()))
ROWS_COLS = (((1,), (0,)), ((), ()))
COLS_COLS = (((0,), (0,)), ((), ()))


def split(a):
    high = a.astype(bf16)
    return high, (a - high.astype(f32)).astype(bf16)


def product(a, b, dims):
    ka, kb = dims[0][0][0], dims[0][1][0]
    return lax.dot_general(
        jnp.concatenate([a[0], a[0], a[1]], axis=ka),
        jnp.concatenate([b[0], b[1], b[0]], axis=kb),
        dims,
        preferred_element_type=f32,
    )


def attention_kernel(lens_ref, weights_ref, scale_ref, merged_ref, square_ref, gain_ref, tap_ref, scaled_ref, cross_ref):
    slots = merged_ref.shape[0]
    heads = scale_ref.shape[0]
    first = pl.program_id(0) * slots
    place = lax.broadcasted_iota(jnp.int32, (SPAN, HEAD), 0)
    key = lax.broadcasted_iota(jnp.int32, (SPAN, HEAD), 1)
    eye = lax.broadcasted_iota(jnp.int32, (SPAN, SPAN), 0) == lax.broadcasted_iota(jnp.int32, (SPAN, SPAN), 1)
    pad = jnp.zeros((HEAD - SPAN, HEAD), f32)
    chains = [(s, h) for s in range(slots) for h in range(heads)]
    every = range(len(chains))
    width = 16 * heads * HEAD
    lens = [lens_ref[first + s] for s, _ in chains]
    weights = [weights_ref[first + s] for s, _ in chains]
    scales = [scale_ref[h] for _, h in chains]
    columns = [pl.ds(h * HEAD, HEAD) for _, h in chains]
    allowed = [(key <= place) & (key < lens[c]) for c in every]
    inverse = []
    for s in range(slots):
        across = lax.rsqrt(square_ref[s] / width + epsilon)
        inverse.append(jnp.sum(jnp.where(eye, across, 0.0), axis=1, keepdims=True))
    gains = [gain_ref[:, columns[c]] for c in every]
    start = [merged_ref[chains[c][0], :, columns[c]] * inverse[chains[c][0]] * gains[c] for c in every]
    keys = [split(jnp.concatenate([start[c], pad], axis=0)) for c in every]
    current = list(start)
    queries, shares, loss_grads = [], [], []
    for step in range(3):
        parts = [split(current[c]) for c in every]
        logits = [product(parts[c], keys[c], ROWS_ROWS) * scales[c] for c in every]
        logits = [jnp.where(allowed[c], logits[c], -1e30) for c in every]
        raised = [jnp.exp(logits[c] - jnp.max(logits[c], axis=1, keepdims=True)) for c in every]
        share = [raised[c] / jnp.sum(raised[c], axis=1, keepdims=True) for c in every]
        share_parts = [split(share[c]) for c in every]
        attended = [product(share_parts[c], keys[c], ROWS_COLS) for c in every]
        current = [current[c] + attended[c] for c in every]
        queries.append(parts)
        shares.append((share, share_parts))
        grads = []
        for c in every:
            later = pltpu.roll(tap_ref[chains[c][0], :, columns[c]].astype(f32), SPAN - (step + 1), 0)
            active = jnp.where(place + (step + 1) < lens[c], 2.0 * weights[c], 0.0)
            grads.append(active * (current[c] - later))
        loss_grads.append(grads)
    grad = loss_grads[2]
    key_grad = None
    for step in (2, 1, 0):
        share, share_parts = shares[step]
        parts = [split(grad[c]) for c in every]
        share_grad = [product(parts[c], keys[c], ROWS_ROWS) for c in every]
        inner = [jnp.sum(share_grad[c] * share[c], axis=1, keepdims=True) for c in every]
        logit_parts = [split(share[c] * (share_grad[c] - inner[c]) * scales[c]) for c in every]
        left = [tuple(jnp.concatenate(z, axis=0) for z in zip(share_parts[c], logit_parts[c])) for c in every]
        right = [tuple(jnp.concatenate(z, axis=0) for z in zip(parts[c], queries[step][c])) for c in every]
        added = [product(left[c], right[c], COLS_COLS) for c in every]
        key_grad = added if key_grad is None else [key_grad[c] + added[c] for c in every]
        grad = [grad[c] + product(logit_parts[c], keys[c], ROWS_COLS) for c in every]
        if step > 0:
            grad = [grad[c] + loss_grads[step - 1][c] for c in every]
    crossed = [None] * slots
    for c in every:
        s = chains[c][0]
        scaled = (grad[c] + key_grad[c][:SPAN]) * gains[c]
        scaled_ref[s, :, columns[c]] = scaled
        inner = jnp.sum(scaled * merged_ref[s, :, columns[c]], axis=1, keepdims=True)
        crossed[s] = inner if crossed[s] is None else crossed[s] + inner
    for s in range(slots):
        cross_ref[s] = jnp.sum(jnp.where(eye, crossed[s], 0.0), axis=0, keepdims=True)


def attention(lens, weights, scales, merged, squares, gain, taps, slots=2):
    count, span, wide = merged.shape
    scalar = pl.BlockSpec(memory_space=pltpu.SMEM)
    block = pl.BlockSpec((slots, span, wide), lambda i: (i, 0, 0))
    flat = pl.BlockSpec((slots, 1, span), lambda i: (i, 0, 0))
    return pl.pallas_call(
        attention_kernel,
        grid=(count // slots,),
        in_specs=[scalar, scalar, scalar, block, flat, pl.BlockSpec((1, wide), lambda i: (0, 0)), block],
        out_specs=[block, flat],
        out_shape=[
            jax.ShapeDtypeStruct((count, span, wide), f32),
            jax.ShapeDtypeStruct((count, 1, span), f32),
        ],
        compiler_params=pltpu.CompilerParams(vmem_limit_bytes=16 * 2**20),
        cost_estimate=pl.CostEstimate(flops=2 * 10**9, bytes_accessed=3 * 10**6, transcendentals=10**6),
    )(lens, weights, scales, merged, squares, gain, taps)


def row_major(a):
    return with_layout_constraint(a, Layout(major_to_minor=tuple(range(a.ndim))))


def buffer(shape, dtype):
    return pl.pallas_call(
        lambda out_ref: None,
        out_specs=pl.BlockSpec(memory_space=pl.ANY),
        out_shape=jax.ShapeDtypeStruct(shape, dtype),
    )()


def tr_index(y, x, core):
    return (y % RING * 2 + x % 2) * 2 + core % 2


def to_chip(value, dy, dx, dcore=0):
    pairs = [
        (tr_index(y, x, core), tr_index(y + dy, x + dx, core + dcore))
        for y in range(RING)
        for x in range(2)
        for core in range(2)
    ]
    return lax.ppermute(value, "tr", pairs)


def to_group(value, dz, dx):
    pairs = [(z * 2 + x, (z + dz) % RING * 2 + (x + dx) % 2) for z in range(RING) for x in range(2)]
    return lax.ppermute(value, "rep", pairs)


def to_sibling(value):
    return to_chip(value, 0, 0, 1)


def gather(value, send):
    got = {(0, 0): value}
    got[1, 0] = send(value, 1, 0)
    got[3, 0] = send(value, 3, 0)
    got[0, 1] = send(value, 0, 1)
    got[2, 0] = send(value, 2, 0)
    got[1, 1] = send(got[0, 1], 1, 0)
    got[3, 1] = send(got[0, 1], 3, 0)
    got[2, 1] = send(got[2, 0], 0, 1)
    return got


def gather_relayed(value, send):
    half = value.shape[0] // 2
    up, down, across = send(value, 1, 0), send(value, 3, 0), send(value, 0, 1)
    far_first = send(up[:half], 1, 0)
    far_last = send(down[half:], 3, 0)
    up_across, down_across = send(across, 1, 0), send(across, 3, 0)
    far_across = send(jnp.concatenate([far_first, far_last], axis=0), 0, 1)
    return [
        (0, 0, 0, value),
        (1, 0, 0, up),
        (3, 0, 0, down),
        (0, 1, 0, across),
        (2, 0, 0, far_first),
        (2, 0, half, far_last),
        (1, 1, 0, up_across),
        (3, 1, 0, down_across),
        (2, 1, 0, far_across),
    ]


def product_kernel(blocks_ref, rows_ref, weight_ref, out_ref):
    out_ref[0] = jnp.dot(rows_ref[...], weight_ref[...], preferred_element_type=f32)


def products(rows, weight, blocks, wide):
    count, depth = rows.shape
    number = blocks.shape[0]
    return pl.pallas_call(
        product_kernel,
        grid_spec=pltpu.PrefetchScalarGridSpec(
            num_scalar_prefetch=1,
            grid=(number,),
            in_specs=[
                pl.BlockSpec((count, depth), lambda i, blocks: (0, 0)),
                pl.BlockSpec((depth, wide), lambda i, blocks: (0, blocks[i])),
            ],
            out_specs=pl.BlockSpec((1, count, wide), lambda i, blocks: (i, 0, 0)),
        ),
        out_shape=jax.ShapeDtypeStruct((number, count, wide), f32),
        compiler_params=pltpu.CompilerParams(vmem_limit_bytes=8 * 2**20),
        cost_estimate=pl.CostEstimate(
            flops=2 * count * depth * wide * number,
            bytes_accessed=count * depth * 2 + number * wide * (count * 4 + depth * 2),
            transcendentals=0,
        ),
    )(blocks, rows, weight)


def sum_over_tr(value):
    value = value + to_sibling(value) + to_chip(value, 0, 1) + to_chip(value, 0, 1, 1)
    return value + to_chip(value, 1, 0) + to_chip(value, 3, 0) + to_chip(value, 2, 0)


def per_device(taps, routes, lengths, merge_weight, norm_gain, head_scale):
    rep = lax.axis_index("rep")
    tr = lax.axis_index("tr")
    core = tr % 2
    x_high = tr // 2 % 2
    y = tr // 4
    x_low = rep % 2
    z = rep // 2
    slots, span, tap_count, wide = taps.shape
    width_all = merge_weight.shape[2]
    flat_in = tap_count * wide
    block = width_all // lax.axis_size("rep")
    rows = row_major(taps.reshape(slots * span, flat_in))
    weight = merge_weight.reshape(flat_in, width_all)

    dest = routes[:, 0]
    target = jnp.maximum(lengths - 1, 0) + jnp.maximum(lengths - 2, 0) + jnp.maximum(lengths - 3, 0)
    own_dest = lax.dynamic_slice_in_dim(dest, rep * slots, slots)
    lens = lax.dynamic_slice_in_dim(lengths, rep * slots, slots)
    count = jnp.sum(jnp.where(own_dest[:, None] == dest[None, :], target[None, :], 0), axis=1)
    weights = 1.0 / count.astype(f32)

    along_z = [[at_z * 2 + at_x for at_z in range(RING)] for at_x in range(2)]

    def gather_taps(value):
        return row_major(lax.all_gather(value, "rep", axis=0, tiled=True, axis_index_groups=along_z))

    taps_here = gather_taps(rows)

    def sums(rows, offsets, parity):
        blocks = jnp.stack([tr_index(y + dy, x_high + dx, parity) for dy, dx in offsets])
        return products(rows, weight, blocks.astype(jnp.int32), wide)

    def chip_sums(rows, offsets):
        other = to_sibling(sums(rows, offsets, 1 - core))
        own = sums(rows, offsets, core)
        return {offset: (own[i] + other[i]) * SEND for i, offset in enumerate(offsets)}

    def send(value, dy, dx):
        return to_chip(value.astype(f16), dy, dx)

    first = chip_sums(rows, ORDER[0])
    far_across, up_across, down_across, rows_now = lax.optimization_barrier(
        tuple(first[offset].astype(f16) for offset in ORDER[0]) + (rows,)
    )
    far_across = send(far_across, 0, 1)
    up_across = send(up_across, 1, 0)
    down_across = send(down_across, 3, 0)
    second = chip_sums(rows_now, ORDER[1])
    far_across, rows_now = lax.optimization_barrier((far_across, rows_now))
    rows_across = row_major(to_group(rows_now, 0, 1))
    up = send(second[1, 0], 1, 0).astype(f32)
    down = send(second[3, 0], 3, 0).astype(f32)
    far = send(second[2, 0] + far_across.astype(f32), 2, 0).astype(f32)
    across = send(second[0, 1] + up_across.astype(f32) + down_across.astype(f32), 0, 1).astype(f32)
    merged = (second[0, 0] + up + down + far + across) * (1.0 / SEND)
    merged = merged.reshape(slots, span, wide)
    squares = sum_over_tr(jnp.sum(merged * merged, axis=2))
    squares, rows_across = lax.optimization_barrier((squares, rows_across))
    taps_across = gather_taps(rows_across)

    squares, taps_here = lax.optimization_barrier((squares, taps_here))

    scaled, crossed = attention(
        lens,
        weights,
        head_scale,
        merged,
        squares.reshape(slots, 1, span),
        norm_gain.reshape(1, wide),
        taps[:, :, 2, :],
    )
    crossed = sum_over_tr(crossed.reshape(slots, span))
    inverse = lax.rsqrt(squares / width_all + epsilon)
    merged_grad = (
        scaled * inverse[:, :, None]
        - merged * (inverse * inverse * inverse * crossed / width_all)[:, :, None]
    ).astype(bf16)

    chips = lax.axis_size("tr")
    pairs = [
        (
            (at_z * 2 + at_x) * chips + tr_index(at_y, at_high, at_core),
            (at_y * 2 + at_high) * chips + tr_index(at_y + at_z, at_x, at_core),
        )
        for at_z in range(RING)
        for at_x in range(2)
        for at_y in range(RING)
        for at_high in range(2)
        for at_core in range(2)
    ]
    turned = lax.ppermute(merged_grad.reshape(slots * span, wide), ("rep", "tr"), pairs)
    own_half = gather(turned, to_chip)
    other_half = {k: to_sibling(v) for k, v in own_half.items()}

    def gradient(half):
        total = None
        same = x_low == x_high
        for a in (0, 1, 3, 2):
            straight, crossed = half[a, 0], half[a, 1]
            for taps_of, piece in (
                (taps_here, jnp.where(same, straight, crossed)),
                (taps_across, jnp.where(same, crossed, straight)),
            ):
                at_z = (y - a - z) % RING
                source = lax.dynamic_slice_in_dim(taps_of, at_z * slots * span, slots * span, 0)
                part = lax.dot_general(source, piece, COLS_COLS, preferred_element_type=f32)
                total = part if total is None else total + part
        return total

    grad = buffer((flat_in, block), f32)
    for half, parity in ((own_half, core), (other_half, 1 - core)):
        grad = lax.dynamic_update_slice_in_dim(grad, gradient(half), parity * wide, 1)
    old = lax.dynamic_slice_in_dim(weight, rep * block, block, 1)
    new_block = (old.astype(f32) - step_size * grad).astype(bf16)
    new = buffer((flat_in, width_all), bf16)
    for a, b, first, piece in gather_relayed(new_block, to_group):
        owner = (z - a) % RING * 2 + (x_low - b) % 2
        new = lax.dynamic_update_slice(new, piece, (first, owner * block))
    return grad.reshape(tap_count, wide, block), new.reshape(tap_count, wide, width_all)


def solution(mesh):
    in_specs = (P("rep", None, None, "tr"), P(), P(), P(None, "tr", None), P("tr"), P("tr"))
    out_specs = (P(None, "tr", "rep"), P(None, "tr", None))
    return jax.shard_map(
        per_device, mesh=mesh, in_specs=in_specs, out_specs=out_specs, check_vma=False
    )
```

```python
import jax
import jax.numpy as jnp
from jax import lax
from jax.experimental import pallas as pl
from jax.experimental.layout import Layout, with_layout_constraint
from jax.experimental.pallas import tpu as pltpu
from jax.sharding import PartitionSpec as P

epsilon = 1e-06
step_size = 0.004
SEND = 128.0
SPAN = 96
HEAD = 128
RING = 4
ORDER = (((2, 1), (1, 1), (3, 1)), ((1, 0), (3, 0), (2, 0), (0, 1), (0, 0)))

GRAD_ORDER = (0, 1, 3, 2)

f32 = jnp.float32
bf16 = jnp.bfloat16
f16 = jnp.float16

ROWS_ROWS = (((1,), (1,)), ((), ()))
ROWS_COLS = (((1,), (0,)), ((), ()))
COLS_COLS = (((0,), (0,)), ((), ()))


def split(a):
    high = a.astype(bf16)
    return high, (a - high.astype(f32)).astype(bf16)


def product(a, b, dims):
    ka, kb = dims[0][0][0], dims[0][1][0]
    return lax.dot_general(
        jnp.concatenate([a[0], a[0], a[1]], axis=ka),
        jnp.concatenate([b[0], b[1], b[0]], axis=kb),
        dims,
        preferred_element_type=f32,
    )


def attention_kernel(lens_ref, weights_ref, scale_ref, merged_ref, square_ref, gain_ref, tap_ref, scaled_ref, cross_ref):
    slots = merged_ref.shape[0]
    heads = scale_ref.shape[0]
    first = pl.program_id(0) * slots
    place = lax.broadcasted_iota(jnp.int32, (SPAN, HEAD), 0)
    key = lax.broadcasted_iota(jnp.int32, (SPAN, HEAD), 1)
    eye = lax.broadcasted_iota(jnp.int32, (SPAN, SPAN), 0) == lax.broadcasted_iota(jnp.int32, (SPAN, SPAN), 1)
    pad = jnp.zeros((HEAD - SPAN, HEAD), f32)
    chains = [(s, h) for s in range(slots) for h in range(heads)]
    every = range(len(chains))
    width = 16 * heads * HEAD
    lens = [lens_ref[first + s] for s, _ in chains]
    weights = [weights_ref[first + s] for s, _ in chains]
    scales = [scale_ref[h] for _, h in chains]
    columns = [pl.ds(h * HEAD, HEAD) for _, h in chains]
    allowed = [(key <= place) & (key < lens[c]) for c in every]
    inverse = []
    for s in range(slots):
        across = lax.rsqrt(square_ref[s] / width + epsilon)
        inverse.append(jnp.sum(jnp.where(eye, across, 0.0), axis=1, keepdims=True))
    gains = [gain_ref[:, columns[c]] for c in every]
    start = [merged_ref[chains[c][0], :, columns[c]] * inverse[chains[c][0]] * gains[c] for c in every]
    keys = [split(jnp.concatenate([start[c], pad], axis=0)) for c in every]
    current = list(start)
    queries, shares, loss_grads = [], [], []
    for step in range(3):
        parts = [split(current[c]) for c in every]
        logits = [product(parts[c], keys[c], ROWS_ROWS) * scales[c] for c in every]
        logits = [jnp.where(allowed[c], logits[c], -1e30) for c in every]
        raised = [jnp.exp(logits[c] - jnp.max(logits[c], axis=1, keepdims=True)) for c in every]
        share = [raised[c] / jnp.sum(raised[c], axis=1, keepdims=True) for c in every]
        share_parts = [split(share[c]) for c in every]
        attended = [product(share_parts[c], keys[c], ROWS_COLS) for c in every]
        current = [current[c] + attended[c] for c in every]
        queries.append(parts)
        shares.append((share, share_parts))
        grads = []
        for c in every:
            later = pltpu.roll(tap_ref[chains[c][0], :, columns[c]].astype(f32), SPAN - (step + 1), 0)
            active = jnp.where(place + (step + 1) < lens[c], 2.0 * weights[c], 0.0)
            grads.append(active * (current[c] - later))
        loss_grads.append(grads)
    grad = loss_grads[2]
    key_grad = None
    for step in (2, 1, 0):
        share, share_parts = shares[step]
        parts = [split(grad[c]) for c in every]
        share_grad = [product(parts[c], keys[c], ROWS_ROWS) for c in every]
        inner = [jnp.sum(share_grad[c] * share[c], axis=1, keepdims=True) for c in every]
        logit_parts = [split(share[c] * (share_grad[c] - inner[c]) * scales[c]) for c in every]
        left = [tuple(jnp.concatenate(z, axis=0) for z in zip(share_parts[c], logit_parts[c])) for c in every]
        right = [tuple(jnp.concatenate(z, axis=0) for z in zip(parts[c], queries[step][c])) for c in every]
        added = [product(left[c], right[c], COLS_COLS) for c in every]
        key_grad = added if key_grad is None else [key_grad[c] + added[c] for c in every]
        grad = [grad[c] + product(logit_parts[c], keys[c], ROWS_COLS) for c in every]
        if step > 0:
            grad = [grad[c] + loss_grads[step - 1][c] for c in every]
    crossed = [None] * slots
    for c in every:
        s = chains[c][0]
        scaled = (grad[c] + key_grad[c][:SPAN]) * gains[c]
        scaled_ref[s, :, columns[c]] = scaled
        inner = jnp.sum(scaled * merged_ref[s, :, columns[c]], axis=1, keepdims=True)
        crossed[s] = inner if crossed[s] is None else crossed[s] + inner
    for s in range(slots):
        cross_ref[s] = jnp.sum(jnp.where(eye, crossed[s], 0.0), axis=0, keepdims=True)


def attention(lens, weights, scales, merged, squares, gain, taps, slots=2):
    count, span, wide = merged.shape
    scalar = pl.BlockSpec(memory_space=pltpu.SMEM)
    block = pl.BlockSpec((slots, span, wide), lambda i: (i, 0, 0))
    flat = pl.BlockSpec((slots, 1, span), lambda i: (i, 0, 0))
    return pl.pallas_call(
        attention_kernel,
        grid=(count // slots,),
        in_specs=[scalar, scalar, scalar, block, flat, pl.BlockSpec((1, wide), lambda i: (0, 0)), block],
        out_specs=[block, flat],
        out_shape=[
            jax.ShapeDtypeStruct((count, span, wide), f32),
            jax.ShapeDtypeStruct((count, 1, span), f32),
        ],
        compiler_params=pltpu.CompilerParams(vmem_limit_bytes=16 * 2**20),
        cost_estimate=pl.CostEstimate(flops=2 * 10**9, bytes_accessed=3 * 10**6, transcendentals=10**6),
    )(lens, weights, scales, merged, squares, gain, taps)


def gradient_kernel(places_ref, here_ref, across_ref, *refs):
    number = 2 * len(GRAD_ORDER)
    own, other, old_ref, grad_ref, new_ref = refs[:number], refs[number : 2 * number], *refs[2 * number :]
    step = pl.program_id(0)
    same, core = places_ref[len(GRAD_ORDER)], places_ref[len(GRAD_ORDER) + 1]
    wide = own[0].shape[1]

    @pl.when(step == 0)
    def _():
        grad_ref[...] = jnp.zeros_like(grad_ref)

    for k in range(len(GRAD_ORDER)):

        @pl.when(step == k)
        def _():
            for half, parity in ((own, core), (other, 1 - core)):
                straight, crossed = half[2 * k][...], half[2 * k + 1][...]
                here = jnp.where(same == 1, straight, crossed)
                across = jnp.where(same == 1, crossed, straight)
                columns = pl.ds(pl.multiple_of(parity * wide, wide), wide)
                grad_ref[:, columns] += lax.dot_general(
                    here_ref[...], here, COLS_COLS, preferred_element_type=f32
                ) + lax.dot_general(across_ref[...], across, COLS_COLS, preferred_element_type=f32)

    @pl.when(step == len(GRAD_ORDER) - 1)
    def _():
        new_ref[...] = (old_ref[...].astype(f32) - step_size * grad_ref[...]).astype(bf16)


def gradient(places, here, across, own, other, weight):
    steps = len(GRAD_ORDER)
    rows, wide = own[0].shape
    depth = weight.shape[0]
    piece = pl.BlockSpec((rows, wide), lambda i, places: (0, 0))
    taps = pl.BlockSpec((rows, depth), lambda i, places: (places[i], 0))
    out = pl.BlockSpec((depth, 2 * wide), lambda i, places: (0, 0))
    old = pl.BlockSpec((depth, 2 * wide), lambda i, places: (0, places[steps + 2]))
    return pl.pallas_call(
        gradient_kernel,
        grid_spec=pltpu.PrefetchScalarGridSpec(
            num_scalar_prefetch=1,
            grid=(steps,),
            in_specs=[taps, taps] + [piece] * (4 * steps) + [old],
            out_specs=[out, out],
        ),
        out_shape=[
            jax.ShapeDtypeStruct((depth, 2 * wide), f32),
            jax.ShapeDtypeStruct((depth, 2 * wide), bf16),
        ],
        compiler_params=pltpu.CompilerParams(vmem_limit_bytes=56 * 2**20),
        cost_estimate=pl.CostEstimate(
            flops=8 * steps * rows * depth * wide, bytes_accessed=20 * 2**20, transcendentals=0
        ),
    )(places, here, across, *own, *other, weight)


def row_major(a):
    return with_layout_constraint(a, Layout(major_to_minor=tuple(range(a.ndim))))


def buffer(shape, dtype):
    return pl.pallas_call(
        lambda out_ref: None,
        out_specs=pl.BlockSpec(memory_space=pl.ANY),
        out_shape=jax.ShapeDtypeStruct(shape, dtype),
    )()


def tr_index(y, x, core):
    return (y % RING * 2 + x % 2) * 2 + core % 2


def to_chip(value, dy, dx, dcore=0):
    pairs = [
        (tr_index(y, x, core), tr_index(y + dy, x + dx, core + dcore))
        for y in range(RING)
        for x in range(2)
        for core in range(2)
    ]
    return lax.ppermute(value, "tr", pairs)


def to_group(value, dz, dx):
    pairs = [(z * 2 + x, (z + dz) % RING * 2 + (x + dx) % 2) for z in range(RING) for x in range(2)]
    return lax.ppermute(value, "rep", pairs)


def to_sibling(value):
    return to_chip(value, 0, 0, 1)


def gather(value, send):
    got = {(0, 0): value}
    got[1, 0] = send(value, 1, 0)
    got[3, 0] = send(value, 3, 0)
    got[0, 1] = send(value, 0, 1)
    got[2, 0] = send(value, 2, 0)
    got[1, 1] = send(got[0, 1], 1, 0)
    got[3, 1] = send(got[0, 1], 3, 0)
    got[2, 1] = send(got[2, 0], 0, 1)
    return got


def gather_relayed(value, send):
    half = value.shape[0] // 2
    up, down, across = send(value, 1, 0), send(value, 3, 0), send(value, 0, 1)
    far_first = send(up[:half], 1, 0)
    far_last = send(down[half:], 3, 0)
    up_across, down_across = send(across, 1, 0), send(across, 3, 0)
    far_across = send(jnp.concatenate([far_first, far_last], axis=0), 0, 1)
    return [
        (0, 0, 0, value),
        (1, 0, 0, up),
        (3, 0, 0, down),
        (0, 1, 0, across),
        (2, 0, 0, far_first),
        (2, 0, half, far_last),
        (1, 1, 0, up_across),
        (3, 1, 0, down_across),
        (2, 1, 0, far_across),
    ]


def product_kernel(blocks_ref, rows_ref, weight_ref, out_ref):
    out_ref[0] = jnp.dot(rows_ref[...], weight_ref[...], preferred_element_type=f32)


def products(rows, weight, blocks, wide):
    count, depth = rows.shape
    number = blocks.shape[0]
    return pl.pallas_call(
        product_kernel,
        grid_spec=pltpu.PrefetchScalarGridSpec(
            num_scalar_prefetch=1,
            grid=(number,),
            in_specs=[
                pl.BlockSpec((count, depth), lambda i, blocks: (0, 0)),
                pl.BlockSpec((depth, wide), lambda i, blocks: (0, blocks[i])),
            ],
            out_specs=pl.BlockSpec((1, count, wide), lambda i, blocks: (i, 0, 0)),
        ),
        out_shape=jax.ShapeDtypeStruct((number, count, wide), f32),
        compiler_params=pltpu.CompilerParams(vmem_limit_bytes=8 * 2**20),
        cost_estimate=pl.CostEstimate(
            flops=2 * count * depth * wide * number,
            bytes_accessed=count * depth * 2 + number * wide * (count * 4 + depth * 2),
            transcendentals=0,
        ),
    )(blocks, rows, weight)


def sum_over_tr(value):
    value = value + to_sibling(value)
    value = value + to_chip(value, 0, 1)
    return value + to_chip(value, 1, 0) + to_chip(value, 2, 0) + to_chip(value, 3, 0)


def per_device(taps, routes, lengths, merge_weight, norm_gain, head_scale):
    rep = lax.axis_index("rep")
    tr = lax.axis_index("tr")
    core = tr % 2
    x_high = tr // 2 % 2
    y = tr // 4
    x_low = rep % 2
    z = rep // 2
    slots, span, tap_count, wide = taps.shape
    width_all = merge_weight.shape[2]
    flat_in = tap_count * wide
    block = width_all // lax.axis_size("rep")
    rows = row_major(taps.reshape(slots * span, flat_in))
    weight = merge_weight.reshape(flat_in, width_all)

    dest = routes[:, 0]
    target = jnp.maximum(lengths - 1, 0) + jnp.maximum(lengths - 2, 0) + jnp.maximum(lengths - 3, 0)
    own_dest = lax.dynamic_slice_in_dim(dest, rep * slots, slots)
    lens = lax.dynamic_slice_in_dim(lengths, rep * slots, slots)
    count = jnp.sum(jnp.where(own_dest[:, None] == dest[None, :], target[None, :], 0), axis=1)
    weights = 1.0 / count.astype(f32)

    along_z = [[at_z * 2 + at_x for at_z in range(RING)] for at_x in range(2)]

    def gather_taps(value):
        return row_major(lax.all_gather(value, "rep", axis=0, tiled=True, axis_index_groups=along_z))

    taps_here = gather_taps(rows)

    def sums(rows, offsets, parity):
        blocks = jnp.stack([tr_index(y + dy, x_high + dx, parity) for dy, dx in offsets])
        return products(rows, weight, blocks.astype(jnp.int32), wide)

    def chip_sums(rows, offsets):
        other = to_sibling(sums(rows, offsets, 1 - core))
        own = sums(rows, offsets, core)
        return {offset: (own[i] + other[i]) * SEND for i, offset in enumerate(offsets)}

    def send(value, dy, dx):
        return to_chip(value.astype(f16), dy, dx)

    first = chip_sums(rows, ORDER[0])
    far_across, up_across, down_across, rows_now = lax.optimization_barrier(
        tuple(first[offset].astype(f16) for offset in ORDER[0]) + (rows,)
    )
    far_across = send(far_across, 0, 1)
    up_across = send(up_across, 1, 0)
    down_across = send(down_across, 3, 0)
    second = chip_sums(rows_now, ORDER[1])
    far_across, rows_now = lax.optimization_barrier((far_across, rows_now))
    rows_across = row_major(to_group(rows_now, 0, 1))
    up = send(second[1, 0], 1, 0).astype(f32)
    down = send(second[3, 0], 3, 0).astype(f32)
    far = send(second[2, 0] + far_across.astype(f32), 2, 0).astype(f32)
    across = send(second[0, 1] + up_across.astype(f32) + down_across.astype(f32), 0, 1).astype(f32)
    merged = (second[0, 0] + up + down + far + across) * (1.0 / SEND)
    merged = merged.reshape(slots, span, wide)
    merged, rows_across = lax.optimization_barrier((merged, rows_across))
    taps_across = gather_taps(rows_across)
    squares = sum_over_tr(jnp.sum(merged * merged, axis=2))

    scaled, crossed = attention(
        lens,
        weights,
        head_scale,
        merged,
        squares.reshape(slots, 1, span),
        norm_gain.reshape(1, wide),
        taps[:, :, 2, :],
    )
    crossed = sum_over_tr(crossed.reshape(slots, span))
    inverse = lax.rsqrt(squares / width_all + epsilon)
    merged_grad = (
        scaled * inverse[:, :, None]
        - merged * (inverse * inverse * inverse * crossed / width_all)[:, :, None]
    ).astype(bf16)

    chips = lax.axis_size("tr")
    pairs = [
        (
            (at_z * 2 + at_x) * chips + tr_index(at_y, at_high, at_core),
            (at_y * 2 + at_high) * chips + tr_index(at_y + at_z, at_x, at_core),
        )
        for at_z in range(RING)
        for at_x in range(2)
        for at_y in range(RING)
        for at_high in range(2)
        for at_core in range(2)
    ]
    turned = lax.ppermute(merged_grad.reshape(slots * span, wide), ("rep", "tr"), pairs)
    own_half = gather(turned, to_chip)
    other_half = {k: to_sibling(v) for k, v in own_half.items()}

    offsets = [(a, b) for a in GRAD_ORDER for b in range(2)]
    places = [(y - a - z) % RING for a in GRAD_ORDER] + [jnp.where(x_low == x_high, 1, 0), core, rep]
    grad, new_block = gradient(
        jnp.stack(places).astype(jnp.int32),
        taps_here,
        taps_across,
        [own_half[k] for k in offsets],
        [other_half[k] for k in offsets],
        weight,
    )
    new = buffer((flat_in, width_all), bf16)
    for a, b, first, piece in gather_relayed(new_block, to_group):
        owner = (z - a) % RING * 2 + (x_low - b) % 2
        new = lax.dynamic_update_slice(new, piece, (first, owner * block))
    return grad.reshape(tap_count, wide, block), new.reshape(tap_count, wide, width_all)


def solution(mesh):
    in_specs = (P("rep", None, None, "tr"), P(), P(), P(None, "tr", None), P("tr"), P("tr"))
    out_specs = (P(None, "tr", "rep"), P(None, "tr", None))
    return jax.shard_map(
        per_device, mesh=mesh, in_specs=in_specs, out_specs=out_specs, check_vma=False
    )
```

```python
import jax
import jax.numpy as jnp
from jax import lax
from jax.experimental import pallas as pl
from jax.experimental.layout import Layout, with_layout_constraint
from jax.experimental.pallas import tpu as pltpu
from jax.sharding import PartitionSpec as P

epsilon = 1e-06
step_size = 0.004
SEND = 128.0
SPAN = 96
HEAD = 128
RING = 4
ORDER = (((2, 1), (1, 1), (3, 1)), ((1, 0), (3, 0), (2, 0), (0, 1), (0, 0)))

GRAD_ORDER = (0, 1, 3, 2)

f32 = jnp.float32
bf16 = jnp.bfloat16
f16 = jnp.float16

ROWS_ROWS = (((1,), (1,)), ((), ()))
ROWS_COLS = (((1,), (0,)), ((), ()))
COLS_COLS = (((0,), (0,)), ((), ()))


def split(a):
    high = a.astype(bf16)
    return high, (a - high.astype(f32)).astype(bf16)


def product(a, b, dims):
    ka, kb = dims[0][0][0], dims[0][1][0]
    return lax.dot_general(
        jnp.concatenate([a[0], a[0], a[1]], axis=ka),
        jnp.concatenate([b[0], b[1], b[0]], axis=kb),
        dims,
        preferred_element_type=f32,
    )


def attention_kernel(lens_ref, weights_ref, scale_ref, merged_ref, square_ref, gain_ref, tap_ref, scaled_ref, cross_ref):
    slots = merged_ref.shape[0]
    heads = scale_ref.shape[0]
    first = pl.program_id(0) * slots
    place = lax.broadcasted_iota(jnp.int32, (SPAN, HEAD), 0)
    key = lax.broadcasted_iota(jnp.int32, (SPAN, HEAD), 1)
    eye = lax.broadcasted_iota(jnp.int32, (SPAN, SPAN), 0) == lax.broadcasted_iota(jnp.int32, (SPAN, SPAN), 1)
    pad = jnp.zeros((HEAD - SPAN, HEAD), f32)
    chains = [(s, h) for s in range(slots) for h in range(heads)]
    every = range(len(chains))
    width = 16 * heads * HEAD
    lens = [lens_ref[first + s] for s, _ in chains]
    weights = [weights_ref[first + s] for s, _ in chains]
    scales = [scale_ref[h] for _, h in chains]
    columns = [pl.ds(h * HEAD, HEAD) for _, h in chains]
    allowed = [(key <= place) & (key < lens[c]) for c in every]
    inverse = []
    for s in range(slots):
        across = lax.rsqrt(square_ref[s] / width + epsilon)
        inverse.append(jnp.sum(jnp.where(eye, across, 0.0), axis=1, keepdims=True))
    gains = [gain_ref[:, columns[c]] for c in every]
    start = [merged_ref[chains[c][0], :, columns[c]] * inverse[chains[c][0]] * gains[c] for c in every]
    keys = [split(jnp.concatenate([start[c], pad], axis=0)) for c in every]
    current = list(start)
    queries, shares, loss_grads = [], [], []
    for step in range(3):
        parts = [split(current[c]) for c in every]
        logits = [product(parts[c], keys[c], ROWS_ROWS) * scales[c] for c in every]
        logits = [jnp.where(allowed[c], logits[c], -1e30) for c in every]
        raised = [jnp.exp(logits[c] - jnp.max(logits[c], axis=1, keepdims=True)) for c in every]
        share = [raised[c] / jnp.sum(raised[c], axis=1, keepdims=True) for c in every]
        share_parts = [split(share[c]) for c in every]
        attended = [product(share_parts[c], keys[c], ROWS_COLS) for c in every]
        current = [current[c] + attended[c] for c in every]
        queries.append(parts)
        shares.append((share, share_parts))
        grads = []
        for c in every:
            later = pltpu.roll(tap_ref[chains[c][0], :, columns[c]].astype(f32), SPAN - (step + 1), 0)
            active = jnp.where(place + (step + 1) < lens[c], 2.0 * weights[c], 0.0)
            grads.append(active * (current[c] - later))
        loss_grads.append(grads)
    grad = loss_grads[2]
    key_grad = None
    for step in (2, 1, 0):
        share, share_parts = shares[step]
        parts = [split(grad[c]) for c in every]
        share_grad = [product(parts[c], keys[c], ROWS_ROWS) for c in every]
        inner = [jnp.sum(share_grad[c] * share[c], axis=1, keepdims=True) for c in every]
        logit_parts = [split(share[c] * (share_grad[c] - inner[c]) * scales[c]) for c in every]
        left = [tuple(jnp.concatenate(z, axis=0) for z in zip(share_parts[c], logit_parts[c])) for c in every]
        right = [tuple(jnp.concatenate(z, axis=0) for z in zip(parts[c], queries[step][c])) for c in every]
        added = [product(left[c], right[c], COLS_COLS) for c in every]
        key_grad = added if key_grad is None else [key_grad[c] + added[c] for c in every]
        grad = [grad[c] + product(logit_parts[c], keys[c], ROWS_COLS) for c in every]
        if step > 0:
            grad = [grad[c] + loss_grads[step - 1][c] for c in every]
    crossed = [None] * slots
    for c in every:
        s = chains[c][0]
        scaled = (grad[c] + key_grad[c][:SPAN]) * gains[c]
        scaled_ref[s, :, columns[c]] = scaled
        inner = jnp.sum(scaled * merged_ref[s, :, columns[c]], axis=1, keepdims=True)
        crossed[s] = inner if crossed[s] is None else crossed[s] + inner
    for s in range(slots):
        cross_ref[s] = jnp.sum(jnp.where(eye, crossed[s], 0.0), axis=0, keepdims=True)


def attention(lens, weights, scales, merged, squares, gain, taps, slots=4):
    count, span, wide = merged.shape
    scalar = pl.BlockSpec(memory_space=pltpu.SMEM)
    block = pl.BlockSpec((slots, span, wide), lambda i: (i, 0, 0))
    flat = pl.BlockSpec((slots, 1, span), lambda i: (i, 0, 0))
    return pl.pallas_call(
        attention_kernel,
        grid=(count // slots,),
        in_specs=[scalar, scalar, scalar, block, flat, pl.BlockSpec((1, wide), lambda i: (0, 0)), block],
        out_specs=[block, flat],
        out_shape=[
            jax.ShapeDtypeStruct((count, span, wide), f32),
            jax.ShapeDtypeStruct((count, 1, span), f32),
        ],
        compiler_params=pltpu.CompilerParams(vmem_limit_bytes=16 * 2**20),
        cost_estimate=pl.CostEstimate(flops=2 * 10**9, bytes_accessed=3 * 10**6, transcendentals=10**6),
    )(lens, weights, scales, merged, squares, gain, taps)


def gradient_kernel(places_ref, here_ref, across_ref, *refs):
    number = 2 * len(GRAD_ORDER)
    own, other, old_ref, grad_ref, new_ref = refs[:number], refs[number : 2 * number], *refs[2 * number :]
    step = pl.program_id(0)
    same, core = places_ref[len(GRAD_ORDER)], places_ref[len(GRAD_ORDER) + 1]
    wide = own[0].shape[1]

    @pl.when(step == 0)
    def _():
        grad_ref[...] = jnp.zeros_like(grad_ref)

    for k in range(len(GRAD_ORDER)):

        @pl.when(step == k)
        def _():
            for half, parity in ((own, core), (other, 1 - core)):
                straight, crossed = half[2 * k][...], half[2 * k + 1][...]
                here = jnp.where(same == 1, straight, crossed)
                across = jnp.where(same == 1, crossed, straight)
                columns = pl.ds(pl.multiple_of(parity * wide, wide), wide)
                grad_ref[:, columns] += lax.dot_general(
                    here_ref[...], here, COLS_COLS, preferred_element_type=f32
                ) + lax.dot_general(across_ref[...], across, COLS_COLS, preferred_element_type=f32)

    @pl.when(step == len(GRAD_ORDER) - 1)
    def _():
        new_ref[...] = (old_ref[...].astype(f32) - step_size * grad_ref[...]).astype(bf16)


def gradient(places, here, across, own, other, weight):
    steps = len(GRAD_ORDER)
    rows, wide = own[0].shape
    depth = weight.shape[0]
    piece = pl.BlockSpec((rows, wide), lambda i, places: (0, 0))
    taps = pl.BlockSpec((rows, depth), lambda i, places: (places[i], 0))
    out = pl.BlockSpec((depth, 2 * wide), lambda i, places: (0, 0))
    old = pl.BlockSpec((depth, 2 * wide), lambda i, places: (0, places[steps + 2]))
    return pl.pallas_call(
        gradient_kernel,
        grid_spec=pltpu.PrefetchScalarGridSpec(
            num_scalar_prefetch=1,
            grid=(steps,),
            in_specs=[taps, taps] + [piece] * (4 * steps) + [old],
            out_specs=[out, out],
        ),
        out_shape=[
            jax.ShapeDtypeStruct((depth, 2 * wide), f32),
            jax.ShapeDtypeStruct((depth, 2 * wide), bf16),
        ],
        compiler_params=pltpu.CompilerParams(vmem_limit_bytes=56 * 2**20),
        cost_estimate=pl.CostEstimate(
            flops=8 * steps * rows * depth * wide, bytes_accessed=20 * 2**20, transcendentals=0
        ),
    )(places, here, across, *own, *other, weight)


def row_major(a):
    return with_layout_constraint(a, Layout(major_to_minor=tuple(range(a.ndim))))


def buffer(shape, dtype):
    return pl.pallas_call(
        lambda out_ref: None,
        out_specs=pl.BlockSpec(memory_space=pl.ANY),
        out_shape=jax.ShapeDtypeStruct(shape, dtype),
    )()


def tr_index(y, x, core):
    return (y % RING * 2 + x % 2) * 2 + core % 2


def to_chip(value, dy, dx, dcore=0):
    pairs = [
        (tr_index(y, x, core), tr_index(y + dy, x + dx, core + dcore))
        for y in range(RING)
        for x in range(2)
        for core in range(2)
    ]
    return lax.ppermute(value, "tr", pairs)


def to_group(value, dz, dx):
    pairs = [(z * 2 + x, (z + dz) % RING * 2 + (x + dx) % 2) for z in range(RING) for x in range(2)]
    return lax.ppermute(value, "rep", pairs)


def to_sibling(value):
    return to_chip(value, 0, 0, 1)


def gather(value, send):
    got = {(0, 0): value}
    got[1, 0] = send(value, 1, 0)
    got[3, 0] = send(value, 3, 0)
    got[0, 1] = send(value, 0, 1)
    got[2, 0] = send(value, 2, 0)
    got[1, 1] = send(got[0, 1], 1, 0)
    got[3, 1] = send(got[0, 1], 3, 0)
    got[2, 1] = send(got[2, 0], 0, 1)
    return got


def gather_relayed(value, send):
    half = value.shape[0] // 2
    up, down, across = send(value, 1, 0), send(value, 3, 0), send(value, 0, 1)
    far_first = send(up[:half], 1, 0)
    far_last = send(down[half:], 3, 0)
    up_across, down_across = send(across, 1, 0), send(across, 3, 0)
    far_across = send(jnp.concatenate([far_first, far_last], axis=0), 0, 1)
    return [
        (0, 0, 0, value),
        (1, 0, 0, up),
        (3, 0, 0, down),
        (0, 1, 0, across),
        (2, 0, 0, far_first),
        (2, 0, half, far_last),
        (1, 1, 0, up_across),
        (3, 1, 0, down_across),
        (2, 1, 0, far_across),
    ]


def product_kernel(blocks_ref, rows_ref, weight_ref, out_ref):
    out_ref[0] = jnp.dot(rows_ref[...], weight_ref[...], preferred_element_type=f32)


def products(rows, weight, blocks, wide):
    count, depth = rows.shape
    number = blocks.shape[0]
    return pl.pallas_call(
        product_kernel,
        grid_spec=pltpu.PrefetchScalarGridSpec(
            num_scalar_prefetch=1,
            grid=(number,),
            in_specs=[
                pl.BlockSpec((count, depth), lambda i, blocks: (0, 0)),
                pl.BlockSpec((depth, wide), lambda i, blocks: (0, blocks[i])),
            ],
            out_specs=pl.BlockSpec((1, count, wide), lambda i, blocks: (i, 0, 0)),
        ),
        out_shape=jax.ShapeDtypeStruct((number, count, wide), f32),
        compiler_params=pltpu.CompilerParams(vmem_limit_bytes=8 * 2**20),
        cost_estimate=pl.CostEstimate(
            flops=2 * count * depth * wide * number,
            bytes_accessed=count * depth * 2 + number * wide * (count * 4 + depth * 2),
            transcendentals=0,
        ),
    )(blocks, rows, weight)


def sum_over_tr(value):
    value = value + to_sibling(value)
    value = value + to_chip(value, 0, 1)
    return value + to_chip(value, 1, 0) + to_chip(value, 2, 0) + to_chip(value, 3, 0)


def per_device(taps, routes, lengths, merge_weight, norm_gain, head_scale):
    rep = lax.axis_index("rep")
    tr = lax.axis_index("tr")
    core = tr % 2
    x_high = tr // 2 % 2
    y = tr // 4
    x_low = rep % 2
    z = rep // 2
    slots, span, tap_count, wide = taps.shape
    width_all = merge_weight.shape[2]
    flat_in = tap_count * wide
    block = width_all // lax.axis_size("rep")
    rows = row_major(taps.reshape(slots * span, flat_in))
    weight = merge_weight.reshape(flat_in, width_all)

    dest = routes[:, 0]
    target = jnp.maximum(lengths - 1, 0) + jnp.maximum(lengths - 2, 0) + jnp.maximum(lengths - 3, 0)
    own_dest = lax.dynamic_slice_in_dim(dest, rep * slots, slots)
    lens = lax.dynamic_slice_in_dim(lengths, rep * slots, slots)
    count = jnp.sum(jnp.where(own_dest[:, None] == dest[None, :], target[None, :], 0), axis=1)
    weights = 1.0 / count.astype(f32)

    along_z = [[at_z * 2 + at_x for at_z in range(RING)] for at_x in range(2)]

    def gather_taps(value):
        return row_major(lax.all_gather(value, "rep", axis=0, tiled=True, axis_index_groups=along_z))

    taps_here = gather_taps(rows)

    def sums(rows, offsets, parity):
        blocks = jnp.stack([tr_index(y + dy, x_high + dx, parity) for dy, dx in offsets])
        return products(rows, weight, blocks.astype(jnp.int32), wide)

    def chip_sums(rows, offsets):
        other = to_sibling(sums(rows, offsets, 1 - core))
        own = sums(rows, offsets, core)
        return {offset: (own[i] + other[i]) * SEND for i, offset in enumerate(offsets)}

    def send(value, dy, dx):
        return to_chip(value.astype(f16), dy, dx)

    first = chip_sums(rows, ORDER[0])
    far_across, up_across, down_across, rows_now = lax.optimization_barrier(
        tuple(first[offset].astype(f16) for offset in ORDER[0]) + (rows,)
    )
    far_across = send(far_across, 0, 1)
    up_across = send(up_across, 1, 0)
    down_across = send(down_across, 3, 0)
    second = chip_sums(rows_now, ORDER[1])
    up = send(second[1, 0], 1, 0).astype(f32)
    down = send(second[3, 0], 3, 0).astype(f32)
    far = send(second[2, 0] + far_across.astype(f32), 2, 0).astype(f32)
    across = send(second[0, 1] + up_across.astype(f32) + down_across.astype(f32), 0, 1).astype(f32)
    merged = (second[0, 0] + up + down + far + across) * (1.0 / SEND)
    merged = merged.reshape(slots, span, wide)
    merged, rows_now = lax.optimization_barrier((merged, rows_now))
    rows_across = row_major(to_group(rows_now, 0, 1))
    squares = sum_over_tr(jnp.sum(merged * merged, axis=2))

    scaled, crossed = attention(
        lens,
        weights,
        head_scale,
        merged,
        squares.reshape(slots, 1, span),
        norm_gain.reshape(1, wide),
        taps[:, :, 2, :],
    )
    crossed, rows_across = lax.optimization_barrier((crossed, rows_across))
    taps_across = gather_taps(rows_across)
    crossed = sum_over_tr(crossed.reshape(slots, span))
    inverse = lax.rsqrt(squares / width_all + epsilon)
    merged_grad = (
        scaled * inverse[:, :, None]
        - merged * (inverse * inverse * inverse * crossed / width_all)[:, :, None]
    ).astype(bf16)

    chips = lax.axis_size("tr")
    pairs = [
        (
            (at_z * 2 + at_x) * chips + tr_index(at_y, at_high, at_core),
            (at_y * 2 + at_high) * chips + tr_index(at_y + at_z, at_x, at_core),
        )
        for at_z in range(RING)
        for at_x in range(2)
        for at_y in range(RING)
        for at_high in range(2)
        for at_core in range(2)
    ]
    turned = lax.ppermute(merged_grad.reshape(slots * span, wide), ("rep", "tr"), pairs)
    own_half = gather(turned, to_chip)
    other_half = {k: to_sibling(v) for k, v in own_half.items()}

    offsets = [(a, b) for a in GRAD_ORDER for b in range(2)]
    places = [(y - a - z) % RING for a in GRAD_ORDER] + [jnp.where(x_low == x_high, 1, 0), core, rep]
    grad, new_block = gradient(
        jnp.stack(places).astype(jnp.int32),
        taps_here,
        taps_across,
        [own_half[k] for k in offsets],
        [other_half[k] for k in offsets],
        weight,
    )
    new = buffer((flat_in, width_all), bf16)
    for a, b, first, piece in gather_relayed(new_block, to_group):
        owner = (z - a) % RING * 2 + (x_low - b) % 2
        new = lax.dynamic_update_slice(new, piece, (first, owner * block))
    return grad.reshape(tap_count, wide, block), new.reshape(tap_count, wide, width_all)


def solution(mesh):
    in_specs = (P("rep", None, None, "tr"), P(), P(), P(None, "tr", None), P("tr"), P("tr"))
    out_specs = (P(None, "tr", "rep"), P(None, "tr", None))
    return jax.shard_map(
        per_device, mesh=mesh, in_specs=in_specs, out_specs=out_specs, check_vma=False
    )
```

```python
import jax
import jax.numpy as jnp
from jax import lax
from jax.experimental import pallas as pl
from jax.experimental.layout import Layout, with_layout_constraint
from jax.experimental.pallas import tpu as pltpu
from jax.sharding import PartitionSpec as P

epsilon = 1e-06
step_size = 0.004
SEND = 128.0
SPAN = 96
HEAD = 128
RING = 4
ORDER = (((2, 1), (1, 1), (3, 1)), ((1, 0), (3, 0), (2, 0), (0, 1), (0, 0)))

GRAD_ORDER = (0, 1, 3, 2)

f32 = jnp.float32
bf16 = jnp.bfloat16
f16 = jnp.float16

ROWS_ROWS = (((1,), (1,)), ((), ()))
ROWS_COLS = (((1,), (0,)), ((), ()))
COLS_COLS = (((0,), (0,)), ((), ()))


def split(a):
    high = a.astype(bf16)
    return high, (a - high.astype(f32)).astype(bf16)


def product(a, b, dims):
    ka, kb = dims[0][0][0], dims[0][1][0]
    return lax.dot_general(
        jnp.concatenate([a[0], a[0], a[1]], axis=ka),
        jnp.concatenate([b[0], b[1], b[0]], axis=kb),
        dims,
        preferred_element_type=f32,
    )


def attention_kernel(lens_ref, weights_ref, scale_ref, merged_ref, square_ref, gain_ref, tap_ref, scaled_ref, cross_ref):
    slots = merged_ref.shape[0]
    heads = scale_ref.shape[0]
    first = pl.program_id(0) * slots
    place = lax.broadcasted_iota(jnp.int32, (SPAN, HEAD), 0)
    key = lax.broadcasted_iota(jnp.int32, (SPAN, HEAD), 1)
    eye = lax.broadcasted_iota(jnp.int32, (SPAN, SPAN), 0) == lax.broadcasted_iota(jnp.int32, (SPAN, SPAN), 1)
    pad = jnp.zeros((HEAD - SPAN, HEAD), f32)
    chains = [(s, h) for s in range(slots) for h in range(heads)]
    every = range(len(chains))
    width = 16 * heads * HEAD
    lens = [lens_ref[first + s] for s, _ in chains]
    weights = [weights_ref[first + s] for s, _ in chains]
    scales = [scale_ref[h] for _, h in chains]
    columns = [pl.ds(h * HEAD, HEAD) for _, h in chains]
    allowed = [(key <= place) & (key < lens[c]) for c in every]
    inverse = []
    for s in range(slots):
        across = lax.rsqrt(square_ref[s] / width + epsilon)
        inverse.append(jnp.sum(jnp.where(eye, across, 0.0), axis=1, keepdims=True))
    gains = [gain_ref[:, columns[c]] for c in every]
    start = [merged_ref[chains[c][0], :, columns[c]] * inverse[chains[c][0]] * gains[c] for c in every]
    keys = [split(jnp.concatenate([start[c], pad], axis=0)) for c in every]
    current = list(start)
    queries, shares, loss_grads = [], [], []
    for step in range(3):
        parts = [split(current[c]) for c in every]
        logits = [product(parts[c], keys[c], ROWS_ROWS) * scales[c] for c in every]
        logits = [jnp.where(allowed[c], logits[c], -1e30) for c in every]
        raised = [jnp.exp(logits[c] - jnp.max(logits[c], axis=1, keepdims=True)) for c in every]
        share = [raised[c] / jnp.sum(raised[c], axis=1, keepdims=True) for c in every]
        share_parts = [split(share[c]) for c in every]
        attended = [product(share_parts[c], keys[c], ROWS_COLS) for c in every]
        current = [current[c] + attended[c] for c in every]
        queries.append(parts)
        shares.append((share, share_parts))
        grads = []
        for c in every:
            later = pltpu.roll(tap_ref[chains[c][0], :, columns[c]].astype(f32), SPAN - (step + 1), 0)
            active = jnp.where(place + (step + 1) < lens[c], 2.0 * weights[c], 0.0)
            grads.append(active * (current[c] - later))
        loss_grads.append(grads)
    grad = loss_grads[2]
    key_grad = None
    for step in (2, 1, 0):
        share, share_parts = shares[step]
        parts = [split(grad[c]) for c in every]
        share_grad = [product(parts[c], keys[c], ROWS_ROWS) for c in every]
        inner = [jnp.sum(share_grad[c] * share[c], axis=1, keepdims=True) for c in every]
        logit_parts = [split(share[c] * (share_grad[c] - inner[c]) * scales[c]) for c in every]
        left = [tuple(jnp.concatenate(z, axis=0) for z in zip(share_parts[c], logit_parts[c])) for c in every]
        right = [tuple(jnp.concatenate(z, axis=0) for z in zip(parts[c], queries[step][c])) for c in every]
        added = [product(left[c], right[c], COLS_COLS) for c in every]
        key_grad = added if key_grad is None else [key_grad[c] + added[c] for c in every]
        grad = [grad[c] + product(logit_parts[c], keys[c], ROWS_COLS) for c in every]
        if step > 0:
            grad = [grad[c] + loss_grads[step - 1][c] for c in every]
    crossed = [None] * slots
    for c in every:
        s = chains[c][0]
        scaled = (grad[c] + key_grad[c][:SPAN]) * gains[c]
        scaled_ref[s, :, columns[c]] = scaled
        inner = jnp.sum(scaled * merged_ref[s, :, columns[c]], axis=1, keepdims=True)
        crossed[s] = inner if crossed[s] is None else crossed[s] + inner
    for s in range(slots):
        cross_ref[s] = jnp.sum(jnp.where(eye, crossed[s], 0.0), axis=0, keepdims=True)


def attention(lens, weights, scales, merged, squares, gain, taps, slots=4):
    count, span, wide = merged.shape
    scalar = pl.BlockSpec(memory_space=pltpu.SMEM)
    block = pl.BlockSpec((slots, span, wide), lambda i: (i, 0, 0))
    flat = pl.BlockSpec((slots, 1, span), lambda i: (i, 0, 0))
    return pl.pallas_call(
        attention_kernel,
        grid=(count // slots,),
        in_specs=[scalar, scalar, scalar, block, flat, pl.BlockSpec((1, wide), lambda i: (0, 0)), block],
        out_specs=[block, flat],
        out_shape=[
            jax.ShapeDtypeStruct((count, span, wide), f32),
            jax.ShapeDtypeStruct((count, 1, span), f32),
        ],
        compiler_params=pltpu.CompilerParams(vmem_limit_bytes=16 * 2**20),
        cost_estimate=pl.CostEstimate(flops=2 * 10**9, bytes_accessed=3 * 10**6, transcendentals=10**6),
    )(lens, weights, scales, merged, squares, gain, taps)


def gradient_kernel(places_ref, here_ref, across_ref, *refs):
    number = 2 * len(GRAD_ORDER)
    own, other, old_ref, grad_ref, new_ref = refs[:number], refs[number : 2 * number], *refs[2 * number :]
    step = pl.program_id(0)
    same, core = places_ref[len(GRAD_ORDER)], places_ref[len(GRAD_ORDER) + 1]
    wide = own[0].shape[1]

    @pl.when(step == 0)
    def _():
        grad_ref[...] = jnp.zeros_like(grad_ref)

    for k in range(len(GRAD_ORDER)):

        @pl.when(step == k)
        def _():
            for half, parity in ((own, core), (other, 1 - core)):
                straight, crossed = half[2 * k][...], half[2 * k + 1][...]
                here = jnp.where(same == 1, straight, crossed)
                across = jnp.where(same == 1, crossed, straight)
                columns = pl.ds(pl.multiple_of(parity * wide, wide), wide)
                grad_ref[:, columns] += lax.dot_general(
                    here_ref[...], here, COLS_COLS, preferred_element_type=f32
                ) + lax.dot_general(across_ref[...], across, COLS_COLS, preferred_element_type=f32)

    @pl.when(step == len(GRAD_ORDER) - 1)
    def _():
        new_ref[...] = (old_ref[...].astype(f32) - step_size * grad_ref[...]).astype(bf16)


def gradient(places, here, across, own, other, weight):
    steps = len(GRAD_ORDER)
    rows, wide = own[0].shape
    depth = weight.shape[0]
    piece = pl.BlockSpec((rows, wide), lambda i, places: (0, 0))
    taps = pl.BlockSpec((rows, depth), lambda i, places: (places[i], 0))
    out = pl.BlockSpec((depth, 2 * wide), lambda i, places: (0, 0))
    old = pl.BlockSpec((depth, 2 * wide), lambda i, places: (0, places[steps + 2]))
    return pl.pallas_call(
        gradient_kernel,
        grid_spec=pltpu.PrefetchScalarGridSpec(
            num_scalar_prefetch=1,
            grid=(steps,),
            in_specs=[taps, taps] + [piece] * (4 * steps) + [old],
            out_specs=[out, out],
        ),
        out_shape=[
            jax.ShapeDtypeStruct((depth, 2 * wide), f32),
            jax.ShapeDtypeStruct((depth, 2 * wide), bf16),
        ],
        compiler_params=pltpu.CompilerParams(vmem_limit_bytes=56 * 2**20),
        cost_estimate=pl.CostEstimate(
            flops=8 * steps * rows * depth * wide, bytes_accessed=20 * 2**20, transcendentals=0
        ),
    )(places, here, across, *own, *other, weight)


def row_major(a):
    return with_layout_constraint(a, Layout(major_to_minor=tuple(range(a.ndim))))


def buffer(shape, dtype):
    return pl.pallas_call(
        lambda out_ref: None,
        out_specs=pl.BlockSpec(memory_space=pl.ANY),
        out_shape=jax.ShapeDtypeStruct(shape, dtype),
    )()


def tr_index(y, x, core):
    return (y % RING * 2 + x % 2) * 2 + core % 2


def to_chip(value, dy, dx, dcore=0):
    pairs = [
        (tr_index(y, x, core), tr_index(y + dy, x + dx, core + dcore))
        for y in range(RING)
        for x in range(2)
        for core in range(2)
    ]
    return lax.ppermute(value, "tr", pairs)


def to_group(value, dz, dx):
    pairs = [(z * 2 + x, (z + dz) % RING * 2 + (x + dx) % 2) for z in range(RING) for x in range(2)]
    return lax.ppermute(value, "rep", pairs)


def to_sibling(value):
    return to_chip(value, 0, 0, 1)


def gather(value, send):
    got = {(0, 0): value}
    got[1, 0] = send(value, 1, 0)
    got[3, 0] = send(value, 3, 0)
    got[0, 1] = send(value, 0, 1)
    got[2, 0] = send(value, 2, 0)
    got[1, 1] = send(got[0, 1], 1, 0)
    got[3, 1] = send(got[0, 1], 3, 0)
    got[2, 1] = send(got[2, 0], 0, 1)
    return got


def gather_relayed(value, send):
    half = value.shape[0] // 2
    up, down, across = send(value, 1, 0), send(value, 3, 0), send(value, 0, 1)
    far_first = send(up[:half], 1, 0)
    far_last = send(down[half:], 3, 0)
    up_across, down_across = send(across, 1, 0), send(across, 3, 0)
    far_across = send(jnp.concatenate([far_first, far_last], axis=0), 0, 1)
    return [
        (0, 0, 0, value),
        (1, 0, 0, up),
        (3, 0, 0, down),
        (0, 1, 0, across),
        (2, 0, 0, far_first),
        (2, 0, half, far_last),
        (1, 1, 0, up_across),
        (3, 1, 0, down_across),
        (2, 1, 0, far_across),
    ]


def product_kernel(blocks_ref, rows_ref, weight_ref, out_ref):
    out_ref[0] = jnp.dot(rows_ref[...], weight_ref[...], preferred_element_type=f32)


def products(rows, weight, blocks, wide):
    count, depth = rows.shape
    number = blocks.shape[0]
    return pl.pallas_call(
        product_kernel,
        grid_spec=pltpu.PrefetchScalarGridSpec(
            num_scalar_prefetch=1,
            grid=(number,),
            in_specs=[
                pl.BlockSpec((count, depth), lambda i, blocks: (0, 0)),
                pl.BlockSpec((depth, wide), lambda i, blocks: (0, blocks[i])),
            ],
            out_specs=pl.BlockSpec((1, count, wide), lambda i, blocks: (i, 0, 0)),
        ),
        out_shape=jax.ShapeDtypeStruct((number, count, wide), f32),
        compiler_params=pltpu.CompilerParams(vmem_limit_bytes=8 * 2**20),
        cost_estimate=pl.CostEstimate(
            flops=2 * count * depth * wide * number,
            bytes_accessed=count * depth * 2 + number * wide * (count * 4 + depth * 2),
            transcendentals=0,
        ),
    )(blocks, rows, weight)


def sum_over_tr(value):
    value = value + to_sibling(value)
    value = value + to_chip(value, 0, 1)
    return value + to_chip(value, 1, 0) + to_chip(value, 2, 0) + to_chip(value, 3, 0)


def per_device(taps, routes, lengths, merge_weight, norm_gain, head_scale):
    rep = lax.axis_index("rep")
    tr = lax.axis_index("tr")
    core = tr % 2
    x_high = tr // 2 % 2
    y = tr // 4
    x_low = rep % 2
    z = rep // 2
    slots, span, tap_count, wide = taps.shape
    width_all = merge_weight.shape[2]
    flat_in = tap_count * wide
    block = width_all // lax.axis_size("rep")
    rows = row_major(taps.reshape(slots * span, flat_in))
    weight = merge_weight.reshape(flat_in, width_all)

    dest = routes[:, 0]
    target = jnp.maximum(lengths - 1, 0) + jnp.maximum(lengths - 2, 0) + jnp.maximum(lengths - 3, 0)
    own_dest = lax.dynamic_slice_in_dim(dest, rep * slots, slots)
    lens = lax.dynamic_slice_in_dim(lengths, rep * slots, slots)
    count = jnp.sum(jnp.where(own_dest[:, None] == dest[None, :], target[None, :], 0), axis=1)
    weights = 1.0 / count.astype(f32)

    along_z = [[at_z * 2 + at_x for at_z in range(RING)] for at_x in range(2)]

    def gather_taps(value):
        return row_major(lax.all_gather(value, "rep", axis=0, tiled=True, axis_index_groups=along_z))

    rows_across = row_major(to_group(rows, 0, 1))
    taps_here = gather_taps(rows)

    def sums(rows, offsets, parity):
        blocks = jnp.stack([tr_index(y + dy, x_high + dx, parity) for dy, dx in offsets])
        return products(rows, weight, blocks.astype(jnp.int32), wide)

    def chip_sums(rows, offsets):
        other = to_sibling(sums(rows, offsets, 1 - core))
        own = sums(rows, offsets, core)
        return {offset: (own[i] + other[i]) * SEND for i, offset in enumerate(offsets)}

    def send(value, dy, dx):
        return to_chip(value.astype(f16), dy, dx)

    first = chip_sums(rows, ORDER[0])
    far_across, up_across, down_across, rows_now = lax.optimization_barrier(
        tuple(first[offset].astype(f16) for offset in ORDER[0]) + (rows,)
    )
    far_across = send(far_across, 0, 1)
    up_across = send(up_across, 1, 0)
    down_across = send(down_across, 3, 0)
    second = chip_sums(rows_now, ORDER[1])
    up = send(second[1, 0], 1, 0).astype(f32)
    down = send(second[3, 0], 3, 0).astype(f32)
    far = send(second[2, 0] + far_across.astype(f32), 2, 0).astype(f32)
    across = send(second[0, 1] + up_across.astype(f32) + down_across.astype(f32), 0, 1).astype(f32)
    merged = (second[0, 0] + up + down + far + across) * (1.0 / SEND)
    merged = merged.reshape(slots, span, wide)
    merged, rows_across = lax.optimization_barrier((merged, rows_across))
    taps_across = gather_taps(rows_across)
    squares = sum_over_tr(jnp.sum(merged * merged, axis=2))

    scaled, crossed = attention(
        lens,
        weights,
        head_scale,
        merged,
        squares.reshape(slots, 1, span),
        norm_gain.reshape(1, wide),
        taps[:, :, 2, :],
    )
    crossed = sum_over_tr(crossed.reshape(slots, span))
    inverse = lax.rsqrt(squares / width_all + epsilon)
    merged_grad = (
        scaled * inverse[:, :, None]
        - merged * (inverse * inverse * inverse * crossed / width_all)[:, :, None]
    ).astype(bf16)

    chips = lax.axis_size("tr")
    pairs = [
        (
            (at_z * 2 + at_x) * chips + tr_index(at_y, at_high, at_core),
            (at_y * 2 + at_high) * chips + tr_index(at_y + at_z, at_x, at_core),
        )
        for at_z in range(RING)
        for at_x in range(2)
        for at_y in range(RING)
        for at_high in range(2)
        for at_core in range(2)
    ]
    turned = lax.ppermute(merged_grad.reshape(slots * span, wide), ("rep", "tr"), pairs)
    own_half = gather(turned, to_chip)
    other_half = {k: to_sibling(v) for k, v in own_half.items()}

    offsets = [(a, b) for a in GRAD_ORDER for b in range(2)]
    places = [(y - a - z) % RING for a in GRAD_ORDER] + [jnp.where(x_low == x_high, 1, 0), core, rep]
    grad, new_block = gradient(
        jnp.stack(places).astype(jnp.int32),
        taps_here,
        taps_across,
        [own_half[k] for k in offsets],
        [other_half[k] for k in offsets],
        weight,
    )
    new = buffer((flat_in, width_all), bf16)
    for a, b, first, piece in gather_relayed(new_block, to_group):
        owner = (z - a) % RING * 2 + (x_low - b) % 2
        new = lax.dynamic_update_slice(new, piece, (first, owner * block))
    return grad.reshape(tap_count, wide, block), new.reshape(tap_count, wide, width_all)


def solution(mesh):
    in_specs = (P("rep", None, None, "tr"), P(), P(), P(None, "tr", None), P("tr"), P("tr"))
    out_specs = (P(None, "tr", "rep"), P(None, "tr", None))
    return jax.shard_map(
        per_device, mesh=mesh, in_specs=in_specs, out_specs=out_specs, check_vma=False
    )
```

```python
import jax
import jax.numpy as jnp
from jax import lax
from jax.experimental import pallas as pl
from jax.experimental.layout import Layout, with_layout_constraint
from jax.experimental.pallas import tpu as pltpu
from jax.sharding import PartitionSpec as P

epsilon = 1e-06
step_size = 0.004
SEND = 128.0
SPAN = 96
HEAD = 128
RING = 4
ORDER = (((2, 1), (1, 1), (3, 1)), ((1, 0), (3, 0), (2, 0), (0, 1), (0, 0)))

GRAD_ORDER = (0, 1, 3, 2)

f32 = jnp.float32
bf16 = jnp.bfloat16
f16 = jnp.float16

ROWS_ROWS = (((1,), (1,)), ((), ()))
ROWS_COLS = (((1,), (0,)), ((), ()))
COLS_COLS = (((0,), (0,)), ((), ()))


def split(a):
    high = a.astype(bf16)
    return high, (a - high.astype(f32)).astype(bf16)


def product(a, b, dims):
    ka, kb = dims[0][0][0], dims[0][1][0]
    return lax.dot_general(
        jnp.concatenate([a[0], a[0], a[1]], axis=ka),
        jnp.concatenate([b[0], b[1], b[0]], axis=kb),
        dims,
        preferred_element_type=f32,
    )


def attention_kernel(lens_ref, weights_ref, scale_ref, merged_ref, square_ref, gain_ref, tap_ref, scaled_ref, cross_ref):
    slots = merged_ref.shape[0]
    heads = scale_ref.shape[0]
    first = pl.program_id(0) * slots
    place = lax.broadcasted_iota(jnp.int32, (SPAN, HEAD), 0)
    key = lax.broadcasted_iota(jnp.int32, (SPAN, HEAD), 1)
    eye = lax.broadcasted_iota(jnp.int32, (SPAN, SPAN), 0) == lax.broadcasted_iota(jnp.int32, (SPAN, SPAN), 1)
    pad = jnp.zeros((HEAD - SPAN, HEAD), f32)
    chains = [(s, h) for s in range(slots) for h in range(heads)]
    every = range(len(chains))
    width = 16 * heads * HEAD
    lens = [lens_ref[first + s] for s, _ in chains]
    weights = [weights_ref[first + s] for s, _ in chains]
    scales = [scale_ref[h] for _, h in chains]
    columns = [pl.ds(h * HEAD, HEAD) for _, h in chains]
    allowed = [(key <= place) & (key < lens[c]) for c in every]
    inverse = []
    for s in range(slots):
        across = lax.rsqrt(square_ref[s] / width + epsilon)
        inverse.append(jnp.sum(jnp.where(eye, across, 0.0), axis=1, keepdims=True))
    gains = [gain_ref[:, columns[c]] for c in every]
    start = [merged_ref[chains[c][0], :, columns[c]] * inverse[chains[c][0]] * gains[c] for c in every]
    keys = [split(jnp.concatenate([start[c], pad], axis=0)) for c in every]
    current = list(start)
    queries, shares, loss_grads = [], [], []
    for step in range(3):
        parts = [split(current[c]) for c in every]
        logits = [product(parts[c], keys[c], ROWS_ROWS) * scales[c] for c in every]
        logits = [jnp.where(allowed[c], logits[c], -1e30) for c in every]
        raised = [jnp.exp(logits[c] - jnp.max(logits[c], axis=1, keepdims=True)) for c in every]
        share = [raised[c] / jnp.sum(raised[c], axis=1, keepdims=True) for c in every]
        share_parts = [split(share[c]) for c in every]
        attended = [product(share_parts[c], keys[c], ROWS_COLS) for c in every]
        current = [current[c] + attended[c] for c in every]
        queries.append(parts)
        shares.append((share, share_parts))
        grads = []
        for c in every:
            later = pltpu.roll(tap_ref[chains[c][0], :, columns[c]].astype(f32), SPAN - (step + 1), 0)
            active = jnp.where(place + (step + 1) < lens[c], 2.0 * weights[c], 0.0)
            grads.append(active * (current[c] - later))
        loss_grads.append(grads)
    grad = loss_grads[2]
    key_grad = None
    for step in (2, 1, 0):
        share, share_parts = shares[step]
        parts = [split(grad[c]) for c in every]
        share_grad = [product(parts[c], keys[c], ROWS_ROWS) for c in every]
        inner = [jnp.sum(share_grad[c] * share[c], axis=1, keepdims=True) for c in every]
        logit_parts = [split(share[c] * (share_grad[c] - inner[c]) * scales[c]) for c in every]
        left = [tuple(jnp.concatenate(z, axis=0) for z in zip(share_parts[c], logit_parts[c])) for c in every]
        right = [tuple(jnp.concatenate(z, axis=0) for z in zip(parts[c], queries[step][c])) for c in every]
        added = [product(left[c], right[c], COLS_COLS) for c in every]
        key_grad = added if key_grad is None else [key_grad[c] + added[c] for c in every]
        grad = [grad[c] + product(logit_parts[c], keys[c], ROWS_COLS) for c in every]
        if step > 0:
            grad = [grad[c] + loss_grads[step - 1][c] for c in every]
    crossed = [None] * slots
    for c in every:
        s = chains[c][0]
        scaled = (grad[c] + key_grad[c][:SPAN]) * gains[c]
        scaled_ref[s, :, columns[c]] = scaled
        inner = jnp.sum(scaled * merged_ref[s, :, columns[c]], axis=1, keepdims=True)
        crossed[s] = inner if crossed[s] is None else crossed[s] + inner
    for s in range(slots):
        cross_ref[s] = jnp.sum(jnp.where(eye, crossed[s], 0.0), axis=0, keepdims=True)


def attention(lens, weights, scales, merged, squares, gain, taps, slots=4):
    count, span, wide = merged.shape
    scalar = pl.BlockSpec(memory_space=pltpu.SMEM)
    block = pl.BlockSpec((slots, span, wide), lambda i: (i, 0, 0))
    flat = pl.BlockSpec((slots, 1, span), lambda i: (i, 0, 0))
    return pl.pallas_call(
        attention_kernel,
        grid=(count // slots,),
        in_specs=[scalar, scalar, scalar, block, flat, pl.BlockSpec((1, wide), lambda i: (0, 0)), block],
        out_specs=[block, flat],
        out_shape=[
            jax.ShapeDtypeStruct((count, span, wide), f32),
            jax.ShapeDtypeStruct((count, 1, span), f32),
        ],
        compiler_params=pltpu.CompilerParams(vmem_limit_bytes=16 * 2**20),
        cost_estimate=pl.CostEstimate(flops=2 * 10**9, bytes_accessed=3 * 10**6, transcendentals=10**6),
    )(lens, weights, scales, merged, squares, gain, taps)


def gradient_kernel(places_ref, here_ref, first_ref, last_ref, *refs):
    number = 2 * len(GRAD_ORDER)
    own, other, old_ref, grad_ref, new_ref = refs[:number], refs[number : 2 * number], *refs[2 * number :]
    step = pl.program_id(0)
    same, core = places_ref[len(GRAD_ORDER)], places_ref[len(GRAD_ORDER) + 1]
    wide = own[0].shape[1]

    @pl.when(step == 0)
    def _():
        grad_ref[...] = jnp.zeros_like(grad_ref)

    for k in range(len(GRAD_ORDER)):

        @pl.when(step == k)
        def _():
            for half, parity in ((own, core), (other, 1 - core)):
                straight, crossed = half[2 * k][...], half[2 * k + 1][...]
                here = jnp.where(same == 1, straight, crossed)
                across = jnp.where(same == 1, crossed, straight)
                columns = pl.ds(pl.multiple_of(parity * wide, wide), wide)
                part = first_ref.shape[0]
                grad_ref[:, columns] += (
                    lax.dot_general(here_ref[...], here, COLS_COLS, preferred_element_type=f32)
                    + lax.dot_general(first_ref[...], across[:part], COLS_COLS, preferred_element_type=f32)
                    + lax.dot_general(last_ref[...], across[part:], COLS_COLS, preferred_element_type=f32)
                )

    @pl.when(step == len(GRAD_ORDER) - 1)
    def _():
        new_ref[...] = (old_ref[...].astype(f32) - step_size * grad_ref[...]).astype(bf16)


def gradient(places, here, first, last, own, other, weight):
    steps = len(GRAD_ORDER)
    rows, wide = own[0].shape
    depth = weight.shape[0]
    piece = pl.BlockSpec((rows, wide), lambda i, places: (0, 0))
    taps = pl.BlockSpec((rows, depth), lambda i, places: (places[i], 0))
    half = pl.BlockSpec((rows // 2, depth), lambda i, places: (places[i], 0))
    out = pl.BlockSpec((depth, 2 * wide), lambda i, places: (0, 0))
    old = pl.BlockSpec((depth, 2 * wide), lambda i, places: (0, places[steps + 2]))
    return pl.pallas_call(
        gradient_kernel,
        grid_spec=pltpu.PrefetchScalarGridSpec(
            num_scalar_prefetch=1,
            grid=(steps,),
            in_specs=[taps, half, half] + [piece] * (4 * steps) + [old],
            out_specs=[out, out],
        ),
        out_shape=[
            jax.ShapeDtypeStruct((depth, 2 * wide), f32),
            jax.ShapeDtypeStruct((depth, 2 * wide), bf16),
        ],
        compiler_params=pltpu.CompilerParams(vmem_limit_bytes=56 * 2**20),
        cost_estimate=pl.CostEstimate(
            flops=8 * steps * rows * depth * wide, bytes_accessed=20 * 2**20, transcendentals=0
        ),
    )(places, here, first, last, *own, *other, weight)


def row_major(a):
    return with_layout_constraint(a, Layout(major_to_minor=tuple(range(a.ndim))))


def buffer(shape, dtype):
    return pl.pallas_call(
        lambda out_ref: None,
        out_specs=pl.BlockSpec(memory_space=pl.ANY),
        out_shape=jax.ShapeDtypeStruct(shape, dtype),
    )()


def tr_index(y, x, core):
    return (y % RING * 2 + x % 2) * 2 + core % 2


def to_chip(value, dy, dx, dcore=0):
    pairs = [
        (tr_index(y, x, core), tr_index(y + dy, x + dx, core + dcore))
        for y in range(RING)
        for x in range(2)
        for core in range(2)
    ]
    return lax.ppermute(value, "tr", pairs)


def to_group(value, dz, dx):
    pairs = [(z * 2 + x, (z + dz) % RING * 2 + (x + dx) % 2) for z in range(RING) for x in range(2)]
    return lax.ppermute(value, "rep", pairs)


def to_sibling(value):
    return to_chip(value, 0, 0, 1)


def gather(value, send):
    got = {(0, 0): value}
    got[1, 0] = send(value, 1, 0)
    got[3, 0] = send(value, 3, 0)
    got[0, 1] = send(value, 0, 1)
    got[2, 0] = send(value, 2, 0)
    got[1, 1] = send(got[0, 1], 1, 0)
    got[3, 1] = send(got[0, 1], 3, 0)
    got[2, 1] = send(got[2, 0], 0, 1)
    return got


def gather_relayed(value, send):
    half = value.shape[0] // 2
    up, down, across = send(value, 1, 0), send(value, 3, 0), send(value, 0, 1)
    far_first = send(up[:half], 1, 0)
    far_last = send(down[half:], 3, 0)
    up_across, down_across = send(across, 1, 0), send(across, 3, 0)
    far_across = send(jnp.concatenate([far_first, far_last], axis=0), 0, 1)
    return [
        (0, 0, 0, value),
        (1, 0, 0, up),
        (3, 0, 0, down),
        (0, 1, 0, across),
        (2, 0, 0, far_first),
        (2, 0, half, far_last),
        (1, 1, 0, up_across),
        (3, 1, 0, down_across),
        (2, 1, 0, far_across),
    ]


def product_kernel(blocks_ref, rows_ref, weight_ref, out_ref):
    out_ref[0] = jnp.dot(rows_ref[...], weight_ref[...], preferred_element_type=f32)


def products(rows, weight, blocks, wide):
    count, depth = rows.shape
    number = blocks.shape[0]
    return pl.pallas_call(
        product_kernel,
        grid_spec=pltpu.PrefetchScalarGridSpec(
            num_scalar_prefetch=1,
            grid=(number,),
            in_specs=[
                pl.BlockSpec((count, depth), lambda i, blocks: (0, 0)),
                pl.BlockSpec((depth, wide), lambda i, blocks: (0, blocks[i])),
            ],
            out_specs=pl.BlockSpec((1, count, wide), lambda i, blocks: (i, 0, 0)),
        ),
        out_shape=jax.ShapeDtypeStruct((number, count, wide), f32),
        compiler_params=pltpu.CompilerParams(vmem_limit_bytes=8 * 2**20),
        cost_estimate=pl.CostEstimate(
            flops=2 * count * depth * wide * number,
            bytes_accessed=count * depth * 2 + number * wide * (count * 4 + depth * 2),
            transcendentals=0,
        ),
    )(blocks, rows, weight)


def sum_over_tr(value):
    value = value + to_sibling(value)
    value = value + to_chip(value, 1, 0) + to_chip(value, 2, 0) + to_chip(value, 3, 0)
    return value + to_chip(value, 0, 1)


def per_device(taps, routes, lengths, merge_weight, norm_gain, head_scale):
    rep = lax.axis_index("rep")
    tr = lax.axis_index("tr")
    core = tr % 2
    x_high = tr // 2 % 2
    y = tr // 4
    x_low = rep % 2
    z = rep // 2
    slots, span, tap_count, wide = taps.shape
    width_all = merge_weight.shape[2]
    flat_in = tap_count * wide
    block = width_all // lax.axis_size("rep")
    rows = row_major(taps.reshape(slots * span, flat_in))
    weight = merge_weight.reshape(flat_in, width_all)

    dest = routes[:, 0]
    target = jnp.maximum(lengths - 1, 0) + jnp.maximum(lengths - 2, 0) + jnp.maximum(lengths - 3, 0)
    own_dest = lax.dynamic_slice_in_dim(dest, rep * slots, slots)
    lens = lax.dynamic_slice_in_dim(lengths, rep * slots, slots)
    count = jnp.sum(jnp.where(own_dest[:, None] == dest[None, :], target[None, :], 0), axis=1)
    weights = 1.0 / count.astype(f32)

    along_z = [[at_z * 2 + at_x for at_z in range(RING)] for at_x in range(2)]

    def gather_taps(value):
        return row_major(lax.all_gather(value, "rep", axis=0, tiled=True, axis_index_groups=along_z))

    taps_here = gather_taps(rows)

    def sums(rows, offsets, parity):
        blocks = jnp.stack([tr_index(y + dy, x_high + dx, parity) for dy, dx in offsets])
        return products(rows, weight, blocks.astype(jnp.int32), wide)

    def chip_sums(rows, offsets):
        other = to_sibling(sums(rows, offsets, 1 - core))
        own = sums(rows, offsets, core)
        return {offset: (own[i] + other[i]) * SEND for i, offset in enumerate(offsets)}

    def send(value, dy, dx):
        return to_chip(value.astype(f16), dy, dx)

    first = chip_sums(rows, ORDER[0])
    far_across, up_across, down_across, rows_now = lax.optimization_barrier(
        tuple(first[offset].astype(f16) for offset in ORDER[0]) + (rows,)
    )
    far_across = send(far_across, 0, 1)
    far_across, rows_now = lax.optimization_barrier((far_across, rows_now))
    part = slots * span // 2
    first_across = row_major(to_group(rows_now[:part], 0, 1))
    up_across = send(up_across, 1, 0)
    down_across = send(down_across, 3, 0)
    second = chip_sums(rows_now, ORDER[1])
    up = send(second[1, 0], 1, 0).astype(f32)
    down = send(second[3, 0], 3, 0).astype(f32)
    far = send(second[2, 0] + far_across.astype(f32), 2, 0).astype(f32)
    across = send(second[0, 1] + up_across.astype(f32) + down_across.astype(f32), 0, 1).astype(f32)
    merged = (second[0, 0] + up + down + far + across) * (1.0 / SEND)
    merged = merged.reshape(slots, span, wide)
    squares = sum_over_tr(jnp.sum(merged * merged, axis=2))
    squares, first_across, rows_now = lax.optimization_barrier((squares, first_across, rows_now))
    taps_first = gather_taps(first_across)
    last_across = row_major(to_group(rows_now[part:], 0, 1))

    scaled, crossed = attention(
        lens,
        weights,
        head_scale,
        merged,
        squares.reshape(slots, 1, span),
        norm_gain.reshape(1, wide),
        taps[:, :, 2, :],
    )
    crossed, last_across = lax.optimization_barrier((crossed, last_across))
    taps_last = gather_taps(last_across)
    crossed = sum_over_tr(crossed.reshape(slots, span))
    inverse = lax.rsqrt(squares / width_all + epsilon)
    merged_grad = (
        scaled * inverse[:, :, None]
        - merged * (inverse * inverse * inverse * crossed / width_all)[:, :, None]
    ).astype(bf16)

    chips = lax.axis_size("tr")
    pairs = [
        (
            (at_z * 2 + at_x) * chips + tr_index(at_y, at_high, at_core),
            (at_y * 2 + at_high) * chips + tr_index(at_y + at_z, at_x, at_core),
        )
        for at_z in range(RING)
        for at_x in range(2)
        for at_y in range(RING)
        for at_high in range(2)
        for at_core in range(2)
    ]
    turned = lax.ppermute(merged_grad.reshape(slots * span, wide), ("rep", "tr"), pairs)
    own_half = gather(turned, to_chip)
    other_half = {k: to_sibling(v) for k, v in own_half.items()}

    offsets = [(a, b) for a in GRAD_ORDER for b in range(2)]
    places = [(y - a - z) % RING for a in GRAD_ORDER] + [jnp.where(x_low == x_high, 1, 0), core, rep]
    grad, new_block = gradient(
        jnp.stack(places).astype(jnp.int32),
        taps_here,
        taps_first,
        taps_last,
        [own_half[k] for k in offsets],
        [other_half[k] for k in offsets],
        weight,
    )
    new = buffer((flat_in, width_all), bf16)
    for a, b, first, piece in gather_relayed(new_block, to_group):
        owner = (z - a) % RING * 2 + (x_low - b) % 2
        new = lax.dynamic_update_slice(new, piece, (first, owner * block))
    return grad.reshape(tap_count, wide, block), new.reshape(tap_count, wide, width_all)


def solution(mesh):
    in_specs = (P("rep", None, None, "tr"), P(), P(), P(None, "tr", None), P("tr"), P("tr"))
    out_specs = (P(None, "tr", "rep"), P(None, "tr", None))
    return jax.shard_map(
        per_device, mesh=mesh, in_specs=in_specs, out_specs=out_specs, check_vma=False
    )
```

```python
import jax
import jax.numpy as jnp
from jax import lax
from jax.experimental import pallas as pl
from jax.experimental.layout import Layout, with_layout_constraint
from jax.experimental.pallas import tpu as pltpu
from jax.sharding import PartitionSpec as P

epsilon = 1e-06
step_size = 0.004
SEND = 128.0
SPAN = 96
HEAD = 128
RING = 4
ORDER = (((2, 1), (1, 1), (3, 1)), ((1, 0), (3, 0), (2, 0), (0, 1), (0, 0)))

GRAD_ORDER = (0, 1, 3, 2)

f32 = jnp.float32
bf16 = jnp.bfloat16
f16 = jnp.float16

ROWS_ROWS = (((1,), (1,)), ((), ()))
ROWS_COLS = (((1,), (0,)), ((), ()))
COLS_COLS = (((0,), (0,)), ((), ()))


def split(a):
    high = a.astype(bf16)
    return high, (a - high.astype(f32)).astype(bf16)


def product(a, b, dims):
    ka, kb = dims[0][0][0], dims[0][1][0]
    return lax.dot_general(
        jnp.concatenate([a[0], a[0], a[1]], axis=ka),
        jnp.concatenate([b[0], b[1], b[0]], axis=kb),
        dims,
        preferred_element_type=f32,
    )


def attention_kernel(lens_ref, weights_ref, scale_ref, merged_ref, square_ref, gain_ref, tap_ref, scaled_ref, cross_ref):
    slots = merged_ref.shape[0]
    heads = scale_ref.shape[0]
    first = pl.program_id(0) * slots
    place = lax.broadcasted_iota(jnp.int32, (SPAN, HEAD), 0)
    key = lax.broadcasted_iota(jnp.int32, (SPAN, HEAD), 1)
    eye = lax.broadcasted_iota(jnp.int32, (SPAN, SPAN), 0) == lax.broadcasted_iota(jnp.int32, (SPAN, SPAN), 1)
    pad = jnp.zeros((HEAD - SPAN, HEAD), f32)
    chains = [(s, h) for s in range(slots) for h in range(heads)]
    every = range(len(chains))
    width = 16 * heads * HEAD
    lens = [lens_ref[first + s] for s, _ in chains]
    weights = [weights_ref[first + s] for s, _ in chains]
    scales = [scale_ref[h] for _, h in chains]
    columns = [pl.ds(h * HEAD, HEAD) for _, h in chains]
    allowed = [(key <= place) & (key < lens[c]) for c in every]
    inverse = []
    for s in range(slots):
        across = lax.rsqrt(square_ref[s] / width + epsilon)
        inverse.append(jnp.sum(jnp.where(eye, across, 0.0), axis=1, keepdims=True))
    gains = [gain_ref[:, columns[c]] for c in every]
    start = [merged_ref[chains[c][0], :, columns[c]] * inverse[chains[c][0]] * gains[c] for c in every]
    keys = [split(jnp.concatenate([start[c], pad], axis=0)) for c in every]
    current = list(start)
    queries, shares, loss_grads = [], [], []
    for step in range(3):
        parts = [split(current[c]) for c in every]
        logits = [product(parts[c], keys[c], ROWS_ROWS) * scales[c] for c in every]
        logits = [jnp.where(allowed[c], logits[c], -1e30) for c in every]
        raised = [jnp.exp(logits[c] - jnp.max(logits[c], axis=1, keepdims=True)) for c in every]
        share = [raised[c] / jnp.sum(raised[c], axis=1, keepdims=True) for c in every]
        share_parts = [split(share[c]) for c in every]
        attended = [product(share_parts[c], keys[c], ROWS_COLS) for c in every]
        current = [current[c] + attended[c] for c in every]
        queries.append(parts)
        shares.append((share, share_parts))
        grads = []
        for c in every:
            later = pltpu.roll(tap_ref[chains[c][0], :, columns[c]].astype(f32), SPAN - (step + 1), 0)
            active = jnp.where(place + (step + 1) < lens[c], 2.0 * weights[c], 0.0)
            grads.append(active * (current[c] - later))
        loss_grads.append(grads)
    grad = loss_grads[2]
    key_grad = None
    for step in (2, 1, 0):
        share, share_parts = shares[step]
        parts = [split(grad[c]) for c in every]
        share_grad = [product(parts[c], keys[c], ROWS_ROWS) for c in every]
        inner = [jnp.sum(share_grad[c] * share[c], axis=1, keepdims=True) for c in every]
        logit_parts = [split(share[c] * (share_grad[c] - inner[c]) * scales[c]) for c in every]
        left = [tuple(jnp.concatenate(z, axis=0) for z in zip(share_parts[c], logit_parts[c])) for c in every]
        right = [tuple(jnp.concatenate(z, axis=0) for z in zip(parts[c], queries[step][c])) for c in every]
        added = [product(left[c], right[c], COLS_COLS) for c in every]
        key_grad = added if key_grad is None else [key_grad[c] + added[c] for c in every]
        grad = [grad[c] + product(logit_parts[c], keys[c], ROWS_COLS) for c in every]
        if step > 0:
            grad = [grad[c] + loss_grads[step - 1][c] for c in every]
    crossed = [None] * slots
    for c in every:
        s = chains[c][0]
        scaled = (grad[c] + key_grad[c][:SPAN]) * gains[c]
        scaled_ref[s, :, columns[c]] = scaled
        inner = jnp.sum(scaled * merged_ref[s, :, columns[c]], axis=1, keepdims=True)
        crossed[s] = inner if crossed[s] is None else crossed[s] + inner
    for s in range(slots):
        cross_ref[s] = jnp.sum(jnp.where(eye, crossed[s], 0.0), axis=0, keepdims=True)


def attention(lens, weights, scales, merged, squares, gain, taps, slots=4):
    count, span, wide = merged.shape
    scalar = pl.BlockSpec(memory_space=pltpu.SMEM)
    block = pl.BlockSpec((slots, span, wide), lambda i: (i, 0, 0))
    flat = pl.BlockSpec((slots, 1, span), lambda i: (i, 0, 0))
    return pl.pallas_call(
        attention_kernel,
        grid=(count // slots,),
        in_specs=[scalar, scalar, scalar, block, flat, pl.BlockSpec((1, wide), lambda i: (0, 0)), block],
        out_specs=[block, flat],
        out_shape=[
            jax.ShapeDtypeStruct((count, span, wide), f32),
            jax.ShapeDtypeStruct((count, 1, span), f32),
        ],
        compiler_params=pltpu.CompilerParams(vmem_limit_bytes=16 * 2**20),
        cost_estimate=pl.CostEstimate(flops=2 * 10**9, bytes_accessed=3 * 10**6, transcendentals=10**6),
    )(lens, weights, scales, merged, squares, gain, taps)


def gradient_kernel(places_ref, here_ref, first_ref, last_ref, *refs):
    number = 2 * len(GRAD_ORDER)
    own, other, old_ref, grad_ref, new_ref = refs[:number], refs[number : 2 * number], *refs[2 * number :]
    step = pl.program_id(0)
    same, core = places_ref[len(GRAD_ORDER)], places_ref[len(GRAD_ORDER) + 1]
    wide = own[0].shape[1]

    @pl.when(step == 0)
    def _():
        grad_ref[...] = jnp.zeros_like(grad_ref)

    for k in range(len(GRAD_ORDER)):

        @pl.when(step == k)
        def _():
            for half, parity in ((own, core), (other, 1 - core)):
                straight, crossed = half[2 * k][...], half[2 * k + 1][...]
                here = jnp.where(same == 1, straight, crossed)
                across = jnp.where(same == 1, crossed, straight)
                columns = pl.ds(pl.multiple_of(parity * wide, wide), wide)
                part = first_ref.shape[0]
                grad_ref[:, columns] += (
                    lax.dot_general(here_ref[...], here, COLS_COLS, preferred_element_type=f32)
                    + lax.dot_general(first_ref[...], across[:part], COLS_COLS, preferred_element_type=f32)
                    + lax.dot_general(last_ref[...], across[part:], COLS_COLS, preferred_element_type=f32)
                )

    @pl.when(step == len(GRAD_ORDER) - 1)
    def _():
        new_ref[...] = (old_ref[...].astype(f32) - step_size * grad_ref[...]).astype(bf16)


def gradient(places, here, first, last, own, other, weight):
    steps = len(GRAD_ORDER)
    rows, wide = own[0].shape
    depth = weight.shape[0]
    piece = pl.BlockSpec((rows, wide), lambda i, places: (0, 0))
    taps = pl.BlockSpec((rows, depth), lambda i, places: (places[i], 0))
    half = pl.BlockSpec((rows // 2, depth), lambda i, places: (places[i], 0))
    out = pl.BlockSpec((depth, 2 * wide), lambda i, places: (0, 0))
    old = pl.BlockSpec((depth, 2 * wide), lambda i, places: (0, places[steps + 2]))
    return pl.pallas_call(
        gradient_kernel,
        grid_spec=pltpu.PrefetchScalarGridSpec(
            num_scalar_prefetch=1,
            grid=(steps,),
            in_specs=[taps, half, half] + [piece] * (4 * steps) + [old],
            out_specs=[out, out],
        ),
        out_shape=[
            jax.ShapeDtypeStruct((depth, 2 * wide), f32),
            jax.ShapeDtypeStruct((depth, 2 * wide), bf16),
        ],
        compiler_params=pltpu.CompilerParams(vmem_limit_bytes=56 * 2**20),
        cost_estimate=pl.CostEstimate(
            flops=8 * steps * rows * depth * wide, bytes_accessed=20 * 2**20, transcendentals=0
        ),
    )(places, here, first, last, *own, *other, weight)


def row_major(a):
    return with_layout_constraint(a, Layout(major_to_minor=tuple(range(a.ndim))))


def buffer(shape, dtype):
    return pl.pallas_call(
        lambda out_ref: None,
        out_specs=pl.BlockSpec(memory_space=pl.ANY),
        out_shape=jax.ShapeDtypeStruct(shape, dtype),
    )()


def tr_index(y, x, core):
    return (y % RING * 2 + x % 2) * 2 + core % 2


def to_chip(value, dy, dx, dcore=0):
    pairs = [
        (tr_index(y, x, core), tr_index(y + dy, x + dx, core + dcore))
        for y in range(RING)
        for x in range(2)
        for core in range(2)
    ]
    return lax.ppermute(value, "tr", pairs)


def to_group(value, dz, dx):
    pairs = [(z * 2 + x, (z + dz) % RING * 2 + (x + dx) % 2) for z in range(RING) for x in range(2)]
    return lax.ppermute(value, "rep", pairs)


def to_sibling(value):
    return to_chip(value, 0, 0, 1)


def gather(value, send):
    got = {(0, 0): value}
    got[1, 0] = send(value, 1, 0)
    got[3, 0] = send(value, 3, 0)
    got[0, 1] = send(value, 0, 1)
    got[2, 0] = send(value, 2, 0)
    got[1, 1] = send(got[0, 1], 1, 0)
    got[3, 1] = send(got[0, 1], 3, 0)
    got[2, 1] = send(got[2, 0], 0, 1)
    return got


def gather_relayed(value, send):
    half = value.shape[0] // 2
    up, down, across = send(value, 1, 0), send(value, 3, 0), send(value, 0, 1)
    far_first = send(up[:half], 1, 0)
    far_last = send(down[half:], 3, 0)
    up_across, down_across = send(across, 1, 0), send(across, 3, 0)
    far_across = send(jnp.concatenate([far_first, far_last], axis=0), 0, 1)
    return [
        (0, 0, 0, value),
        (1, 0, 0, up),
        (3, 0, 0, down),
        (0, 1, 0, across),
        (2, 0, 0, far_first),
        (2, 0, half, far_last),
        (1, 1, 0, up_across),
        (3, 1, 0, down_across),
        (2, 1, 0, far_across),
    ]


def product_kernel(blocks_ref, rows_ref, weight_ref, out_ref):
    out_ref[0] = jnp.dot(rows_ref[...], weight_ref[...], preferred_element_type=f32)


def products(rows, weight, blocks, wide):
    count, depth = rows.shape
    number = blocks.shape[0]
    return pl.pallas_call(
        product_kernel,
        grid_spec=pltpu.PrefetchScalarGridSpec(
            num_scalar_prefetch=1,
            grid=(number,),
            in_specs=[
                pl.BlockSpec((count, depth), lambda i, blocks: (0, 0)),
                pl.BlockSpec((depth, wide), lambda i, blocks: (0, blocks[i])),
            ],
            out_specs=pl.BlockSpec((1, count, wide), lambda i, blocks: (i, 0, 0)),
        ),
        out_shape=jax.ShapeDtypeStruct((number, count, wide), f32),
        compiler_params=pltpu.CompilerParams(vmem_limit_bytes=8 * 2**20),
        cost_estimate=pl.CostEstimate(
            flops=2 * count * depth * wide * number,
            bytes_accessed=count * depth * 2 + number * wide * (count * 4 + depth * 2),
            transcendentals=0,
        ),
    )(blocks, rows, weight)


def sum_over_tr(value):
    value = value + to_sibling(value)
    value = value + to_chip(value, 1, 0) + to_chip(value, 2, 0) + to_chip(value, 3, 0)
    return value + to_chip(value, 0, 1)


def per_device(taps, routes, lengths, merge_weight, norm_gain, head_scale):
    rep = lax.axis_index("rep")
    tr = lax.axis_index("tr")
    core = tr % 2
    x_high = tr // 2 % 2
    y = tr // 4
    x_low = rep % 2
    z = rep // 2
    slots, span, tap_count, wide = taps.shape
    width_all = merge_weight.shape[2]
    flat_in = tap_count * wide
    block = width_all // lax.axis_size("rep")
    rows = row_major(taps.reshape(slots * span, flat_in))
    weight = merge_weight.reshape(flat_in, width_all)

    dest = routes[:, 0]
    target = jnp.maximum(lengths - 1, 0) + jnp.maximum(lengths - 2, 0) + jnp.maximum(lengths - 3, 0)
    own_dest = lax.dynamic_slice_in_dim(dest, rep * slots, slots)
    lens = lax.dynamic_slice_in_dim(lengths, rep * slots, slots)
    count = jnp.sum(jnp.where(own_dest[:, None] == dest[None, :], target[None, :], 0), axis=1)
    weights = 1.0 / count.astype(f32)

    along_z = [[at_z * 2 + at_x for at_z in range(RING)] for at_x in range(2)]

    def gather_taps(value):
        return row_major(lax.all_gather(value, "rep", axis=0, tiled=True, axis_index_groups=along_z))

    taps_here = gather_taps(rows)

    def sums(rows, offsets, parity):
        blocks = jnp.stack([tr_index(y + dy, x_high + dx, parity) for dy, dx in offsets])
        return products(rows, weight, blocks.astype(jnp.int32), wide)

    def chip_sums(rows, offsets):
        other = to_sibling(sums(rows, offsets, 1 - core))
        own = sums(rows, offsets, core)
        return {offset: (own[i] + other[i]) * SEND for i, offset in enumerate(offsets)}

    def send(value, dy, dx):
        return to_chip(value.astype(f16), dy, dx)

    first = chip_sums(rows, ORDER[0])
    far_across, up_across, down_across, rows_now = lax.optimization_barrier(
        tuple(first[offset].astype(f16) for offset in ORDER[0]) + (rows,)
    )
    far_across = send(far_across, 0, 1)
    up_across = send(up_across, 1, 0)
    down_across = send(down_across, 3, 0)
    second = chip_sums(rows_now, ORDER[1])
    up = send(second[1, 0], 1, 0).astype(f32)
    down = send(second[3, 0], 3, 0).astype(f32)
    far = send(second[2, 0] + far_across.astype(f32), 2, 0).astype(f32)
    second_across = (second[0, 1] + up_across.astype(f32) + down_across.astype(f32)).astype(f16)
    second_across, rows_now = lax.optimization_barrier((second_across, rows_now))
    across = send(second_across, 0, 1).astype(f32)
    part = slots * span // 2
    first_across = row_major(to_group(rows_now[:part], 0, 1))
    merged = (second[0, 0] + up + down + far + across) * (1.0 / SEND)
    merged = merged.reshape(slots, span, wide)
    squares = sum_over_tr(jnp.sum(merged * merged, axis=2))
    squares, first_across, rows_now = lax.optimization_barrier((squares, first_across, rows_now))
    taps_first = gather_taps(first_across)
    last_across = row_major(to_group(rows_now[part:], 0, 1))

    scaled, crossed = attention(
        lens,
        weights,
        head_scale,
        merged,
        squares.reshape(slots, 1, span),
        norm_gain.reshape(1, wide),
        taps[:, :, 2, :],
    )
    crossed, last_across = lax.optimization_barrier((crossed, last_across))
    taps_last = gather_taps(last_across)
    crossed = sum_over_tr(crossed.reshape(slots, span))
    inverse = lax.rsqrt(squares / width_all + epsilon)
    merged_grad = (
        scaled * inverse[:, :, None]
        - merged * (inverse * inverse * inverse * crossed / width_all)[:, :, None]
    ).astype(bf16)

    chips = lax.axis_size("tr")
    pairs = [
        (
            (at_z * 2 + at_x) * chips + tr_index(at_y, at_high, at_core),
            (at_y * 2 + at_high) * chips + tr_index(at_y + at_z, at_x, at_core),
        )
        for at_z in range(RING)
        for at_x in range(2)
        for at_y in range(RING)
        for at_high in range(2)
        for at_core in range(2)
    ]
    turned = lax.ppermute(merged_grad.reshape(slots * span, wide), ("rep", "tr"), pairs)
    own_half = gather(turned, to_chip)
    other_half = {k: to_sibling(v) for k, v in own_half.items()}

    offsets = [(a, b) for a in GRAD_ORDER for b in range(2)]
    places = [(y - a - z) % RING for a in GRAD_ORDER] + [jnp.where(x_low == x_high, 1, 0), core, rep]
    grad, new_block = gradient(
        jnp.stack(places).astype(jnp.int32),
        taps_here,
        taps_first,
        taps_last,
        [own_half[k] for k in offsets],
        [other_half[k] for k in offsets],
        weight,
    )
    new = buffer((flat_in, width_all), bf16)
    for a, b, first, piece in gather_relayed(new_block, to_group):
        owner = (z - a) % RING * 2 + (x_low - b) % 2
        new = lax.dynamic_update_slice(new, piece, (first, owner * block))
    return grad.reshape(tap_count, wide, block), new.reshape(tap_count, wide, width_all)


def solution(mesh):
    in_specs = (P("rep", None, None, "tr"), P(), P(), P(None, "tr", None), P("tr"), P("tr"))
    out_specs = (P(None, "tr", "rep"), P(None, "tr", None))
    return jax.shard_map(
        per_device, mesh=mesh, in_specs=in_specs, out_specs=out_specs, check_vma=False
    )
```

```python
import jax
import jax.numpy as jnp
from jax import lax
from jax.experimental import pallas as pl
from jax.experimental.layout import Layout, with_layout_constraint
from jax.experimental.pallas import tpu as pltpu
from jax.sharding import PartitionSpec as P

epsilon = 1e-06
step_size = 0.004
SEND = 128.0
SPAN = 96
HEAD = 128
RING = 4
ORDER = (((2, 1), (1, 1), (3, 1)), ((1, 0), (3, 0), (2, 0), (0, 1), (0, 0)))

GRAD_ORDER = (0, 1, 3, 2)

f32 = jnp.float32
bf16 = jnp.bfloat16
f16 = jnp.float16

ROWS_ROWS = (((1,), (1,)), ((), ()))
ROWS_COLS = (((1,), (0,)), ((), ()))
COLS_COLS = (((0,), (0,)), ((), ()))


def split(a):
    high = a.astype(bf16)
    return high, (a - high.astype(f32)).astype(bf16)


def product(a, b, dims):
    ka, kb = dims[0][0][0], dims[0][1][0]
    return lax.dot_general(
        jnp.concatenate([a[0], a[0], a[1]], axis=ka),
        jnp.concatenate([b[0], b[1], b[0]], axis=kb),
        dims,
        preferred_element_type=f32,
    )


def attention_kernel(lens_ref, weights_ref, scale_ref, merged_ref, square_ref, gain_ref, tap_ref, scaled_ref, cross_ref):
    slots = merged_ref.shape[0]
    heads = scale_ref.shape[0]
    first = pl.program_id(0) * slots
    place = lax.broadcasted_iota(jnp.int32, (SPAN, HEAD), 0)
    key = lax.broadcasted_iota(jnp.int32, (SPAN, HEAD), 1)
    eye = lax.broadcasted_iota(jnp.int32, (SPAN, SPAN), 0) == lax.broadcasted_iota(jnp.int32, (SPAN, SPAN), 1)
    pad = jnp.zeros((HEAD - SPAN, HEAD), f32)
    chains = [(s, h) for s in range(slots) for h in range(heads)]
    every = range(len(chains))
    width = 16 * heads * HEAD
    lens = [lens_ref[first + s] for s, _ in chains]
    weights = [weights_ref[first + s] for s, _ in chains]
    scales = [scale_ref[h] for _, h in chains]
    columns = [pl.ds(h * HEAD, HEAD) for _, h in chains]
    allowed = [(key <= place) & (key < lens[c]) for c in every]
    inverse = []
    for s in range(slots):
        across = lax.rsqrt(square_ref[s] / width + epsilon)
        inverse.append(jnp.sum(jnp.where(eye, across, 0.0), axis=1, keepdims=True))
    gains = [gain_ref[:, columns[c]] for c in every]
    start = [merged_ref[chains[c][0], :, columns[c]] * inverse[chains[c][0]] * gains[c] for c in every]
    keys = [split(jnp.concatenate([start[c], pad], axis=0)) for c in every]
    current = list(start)
    queries, shares, loss_grads = [], [], []
    for step in range(3):
        parts = [split(current[c]) for c in every]
        logits = [product(parts[c], keys[c], ROWS_ROWS) * scales[c] for c in every]
        logits = [jnp.where(allowed[c], logits[c], -1e30) for c in every]
        raised = [jnp.exp(logits[c] - jnp.max(logits[c], axis=1, keepdims=True)) for c in every]
        share = [raised[c] / jnp.sum(raised[c], axis=1, keepdims=True) for c in every]
        share_parts = [split(share[c]) for c in every]
        attended = [product(share_parts[c], keys[c], ROWS_COLS) for c in every]
        current = [current[c] + attended[c] for c in every]
        queries.append(parts)
        shares.append((share, share_parts))
        grads = []
        for c in every:
            later = pltpu.roll(tap_ref[chains[c][0], :, columns[c]].astype(f32), SPAN - (step + 1), 0)
            active = jnp.where(place + (step + 1) < lens[c], 2.0 * weights[c], 0.0)
            grads.append(active * (current[c] - later))
        loss_grads.append(grads)
    grad = loss_grads[2]
    key_grad = None
    for step in (2, 1, 0):
        share, share_parts = shares[step]
        parts = [split(grad[c]) for c in every]
        share_grad = [product(parts[c], keys[c], ROWS_ROWS) for c in every]
        inner = [jnp.sum(share_grad[c] * share[c], axis=1, keepdims=True) for c in every]
        logit_parts = [split(share[c] * (share_grad[c] - inner[c]) * scales[c]) for c in every]
        left = [tuple(jnp.concatenate(z, axis=0) for z in zip(share_parts[c], logit_parts[c])) for c in every]
        right = [tuple(jnp.concatenate(z, axis=0) for z in zip(parts[c], queries[step][c])) for c in every]
        added = [product(left[c], right[c], COLS_COLS) for c in every]
        key_grad = added if key_grad is None else [key_grad[c] + added[c] for c in every]
        grad = [grad[c] + product(logit_parts[c], keys[c], ROWS_COLS) for c in every]
        if step > 0:
            grad = [grad[c] + loss_grads[step - 1][c] for c in every]
    crossed = [None] * slots
    for c in every:
        s = chains[c][0]
        scaled = (grad[c] + key_grad[c][:SPAN]) * gains[c]
        scaled_ref[s, :, columns[c]] = scaled
        inner = jnp.sum(scaled * merged_ref[s, :, columns[c]], axis=1, keepdims=True)
        crossed[s] = inner if crossed[s] is None else crossed[s] + inner
    for s in range(slots):
        cross_ref[s] = jnp.sum(jnp.where(eye, crossed[s], 0.0), axis=0, keepdims=True)


def attention(lens, weights, scales, merged, squares, gain, taps, slots=4):
    count, span, wide = merged.shape
    scalar = pl.BlockSpec(memory_space=pltpu.SMEM)
    block = pl.BlockSpec((slots, span, wide), lambda i: (i, 0, 0))
    flat = pl.BlockSpec((slots, 1, span), lambda i: (i, 0, 0))
    return pl.pallas_call(
        attention_kernel,
        grid=(count // slots,),
        in_specs=[scalar, scalar, scalar, block, flat, pl.BlockSpec((1, wide), lambda i: (0, 0)), block],
        out_specs=[block, flat],
        out_shape=[
            jax.ShapeDtypeStruct((count, span, wide), f32),
            jax.ShapeDtypeStruct((count, 1, span), f32),
        ],
        compiler_params=pltpu.CompilerParams(vmem_limit_bytes=16 * 2**20),
        cost_estimate=pl.CostEstimate(flops=2 * 10**9, bytes_accessed=3 * 10**6, transcendentals=10**6),
    )(lens, weights, scales, merged, squares, gain, taps)


def gradient_kernel(places_ref, here_ref, first_ref, last_ref, *refs):
    number = 2 * len(GRAD_ORDER)
    own, other, old_ref, grad_ref, new_ref = refs[:number], refs[number : 2 * number], *refs[2 * number :]
    step = pl.program_id(0)
    same, core = places_ref[len(GRAD_ORDER)], places_ref[len(GRAD_ORDER) + 1]
    wide = own[0].shape[1]

    @pl.when(step == 0)
    def _():
        grad_ref[...] = jnp.zeros_like(grad_ref)

    for k in range(len(GRAD_ORDER)):

        @pl.when(step == k)
        def _():
            for half, parity in ((own, core), (other, 1 - core)):
                straight, crossed = half[2 * k][...], half[2 * k + 1][...]
                here = jnp.where(same == 1, straight, crossed)
                across = jnp.where(same == 1, crossed, straight)
                columns = pl.ds(pl.multiple_of(parity * wide, wide), wide)
                part = first_ref.shape[0]
                grad_ref[:, columns] += (
                    lax.dot_general(here_ref[...], here, COLS_COLS, preferred_element_type=f32)
                    + lax.dot_general(first_ref[...], across[:part], COLS_COLS, preferred_element_type=f32)
                    + lax.dot_general(last_ref[...], across[part:], COLS_COLS, preferred_element_type=f32)
                )

    @pl.when(step == len(GRAD_ORDER) - 1)
    def _():
        new_ref[...] = (old_ref[...].astype(f32) - step_size * grad_ref[...]).astype(bf16)


def gradient(places, here, first, last, own, other, weight):
    steps = len(GRAD_ORDER)
    rows, wide = own[0].shape
    depth = weight.shape[0]
    piece = pl.BlockSpec((rows, wide), lambda i, places: (0, 0))
    taps = pl.BlockSpec((rows, depth), lambda i, places: (places[i], 0))
    half = pl.BlockSpec((rows // 2, depth), lambda i, places: (places[i], 0))
    out = pl.BlockSpec((depth, 2 * wide), lambda i, places: (0, 0))
    old = pl.BlockSpec((depth, 2 * wide), lambda i, places: (0, places[steps + 2]))
    return pl.pallas_call(
        gradient_kernel,
        grid_spec=pltpu.PrefetchScalarGridSpec(
            num_scalar_prefetch=1,
            grid=(steps,),
            in_specs=[taps, half, half] + [piece] * (4 * steps) + [old],
            out_specs=[out, out],
        ),
        out_shape=[
            jax.ShapeDtypeStruct((depth, 2 * wide), f32),
            jax.ShapeDtypeStruct((depth, 2 * wide), bf16),
        ],
        compiler_params=pltpu.CompilerParams(vmem_limit_bytes=56 * 2**20),
        cost_estimate=pl.CostEstimate(
            flops=8 * steps * rows * depth * wide, bytes_accessed=20 * 2**20, transcendentals=0
        ),
    )(places, here, first, last, *own, *other, weight)


def row_major(a):
    return with_layout_constraint(a, Layout(major_to_minor=tuple(range(a.ndim))))


def buffer(shape, dtype):
    return pl.pallas_call(
        lambda out_ref: None,
        out_specs=pl.BlockSpec(memory_space=pl.ANY),
        out_shape=jax.ShapeDtypeStruct(shape, dtype),
    )()


def tr_index(y, x, core):
    return (y % RING * 2 + x % 2) * 2 + core % 2


def to_chip(value, dy, dx, dcore=0):
    pairs = [
        (tr_index(y, x, core), tr_index(y + dy, x + dx, core + dcore))
        for y in range(RING)
        for x in range(2)
        for core in range(2)
    ]
    return lax.ppermute(value, "tr", pairs)


def to_group(value, dz, dx):
    pairs = [(z * 2 + x, (z + dz) % RING * 2 + (x + dx) % 2) for z in range(RING) for x in range(2)]
    return lax.ppermute(value, "rep", pairs)


def to_sibling(value):
    return to_chip(value, 0, 0, 1)


def gather(value, send):
    got = {(0, 0): value}
    got[1, 0] = send(value, 1, 0)
    got[3, 0] = send(value, 3, 0)
    got[0, 1] = send(value, 0, 1)
    got[2, 0] = send(value, 2, 0)
    got[1, 1] = send(got[0, 1], 1, 0)
    got[3, 1] = send(got[0, 1], 3, 0)
    got[2, 1] = send(got[2, 0], 0, 1)
    return got


def gather_relayed(value, send):
    half = value.shape[0] // 2
    up, down, across = send(value, 1, 0), send(value, 3, 0), send(value, 0, 1)
    far_first = send(up[:half], 1, 0)
    far_last = send(down[half:], 3, 0)
    up_across, down_across = send(across, 1, 0), send(across, 3, 0)
    far_across = send(jnp.concatenate([far_first, far_last], axis=0), 0, 1)
    return [
        (0, 0, 0, value),
        (1, 0, 0, up),
        (3, 0, 0, down),
        (0, 1, 0, across),
        (2, 0, 0, far_first),
        (2, 0, half, far_last),
        (1, 1, 0, up_across),
        (3, 1, 0, down_across),
        (2, 1, 0, far_across),
    ]


def product_kernel(blocks_ref, rows_ref, weight_ref, out_ref):
    out_ref[0] = jnp.dot(rows_ref[...], weight_ref[...], preferred_element_type=f32)


def products(rows, weight, blocks, wide):
    count, depth = rows.shape
    number = blocks.shape[0]
    return pl.pallas_call(
        product_kernel,
        grid_spec=pltpu.PrefetchScalarGridSpec(
            num_scalar_prefetch=1,
            grid=(number,),
            in_specs=[
                pl.BlockSpec((count, depth), lambda i, blocks: (0, 0)),
                pl.BlockSpec((depth, wide), lambda i, blocks: (0, blocks[i])),
            ],
            out_specs=pl.BlockSpec((1, count, wide), lambda i, blocks: (i, 0, 0)),
        ),
        out_shape=jax.ShapeDtypeStruct((number, count, wide), f32),
        compiler_params=pltpu.CompilerParams(vmem_limit_bytes=8 * 2**20),
        cost_estimate=pl.CostEstimate(
            flops=2 * count * depth * wide * number,
            bytes_accessed=count * depth * 2 + number * wide * (count * 4 + depth * 2),
            transcendentals=0,
        ),
    )(blocks, rows, weight)


def sum_over_y(value):
    value = value + to_sibling(value)
    return value + to_chip(value, 1, 0) + to_chip(value, 2, 0) + to_chip(value, 3, 0)


def per_device(taps, routes, lengths, merge_weight, norm_gain, head_scale):
    rep = lax.axis_index("rep")
    tr = lax.axis_index("tr")
    core = tr % 2
    x_high = tr // 2 % 2
    y = tr // 4
    x_low = rep % 2
    z = rep // 2
    slots, span, tap_count, wide = taps.shape
    width_all = merge_weight.shape[2]
    flat_in = tap_count * wide
    block = width_all // lax.axis_size("rep")
    rows = row_major(taps.reshape(slots * span, flat_in))
    weight = merge_weight.reshape(flat_in, width_all)

    dest = routes[:, 0]
    target = jnp.maximum(lengths - 1, 0) + jnp.maximum(lengths - 2, 0) + jnp.maximum(lengths - 3, 0)
    own_dest = lax.dynamic_slice_in_dim(dest, rep * slots, slots)
    lens = lax.dynamic_slice_in_dim(lengths, rep * slots, slots)
    count = jnp.sum(jnp.where(own_dest[:, None] == dest[None, :], target[None, :], 0), axis=1)
    weights = 1.0 / count.astype(f32)

    along_z = [[at_z * 2 + at_x for at_z in range(RING)] for at_x in range(2)]

    def gather_taps(value):
        return row_major(lax.all_gather(value, "rep", axis=0, tiled=True, axis_index_groups=along_z))

    taps_here = gather_taps(rows)

    def sums(rows, offsets, parity):
        blocks = jnp.stack([tr_index(y + dy, x_high + dx, parity) for dy, dx in offsets])
        return products(rows, weight, blocks.astype(jnp.int32), wide)

    def chip_sums(rows, offsets):
        other = to_sibling(sums(rows, offsets, 1 - core))
        own = sums(rows, offsets, core)
        return {offset: (own[i] + other[i]) * SEND for i, offset in enumerate(offsets)}

    def send(value, dy, dx):
        return to_chip(value.astype(f16), dy, dx)

    first = chip_sums(rows, ORDER[0])
    far_across, up_across, down_across, rows_now = lax.optimization_barrier(
        tuple(first[offset].astype(f16) for offset in ORDER[0]) + (rows,)
    )
    far_across = send(far_across, 0, 1)
    up_across = send(up_across, 1, 0)
    down_across = send(down_across, 3, 0)
    second = chip_sums(rows_now, ORDER[1])
    up = send(second[1, 0], 1, 0).astype(f32)
    down = send(second[3, 0], 3, 0).astype(f32)
    far = send(second[2, 0] + far_across.astype(f32), 2, 0).astype(f32)
    second_across = (second[0, 1] + up_across.astype(f32) + down_across.astype(f32)).astype(f16)
    second_across, rows_now = lax.optimization_barrier((second_across, rows_now))
    across = send(second_across, 0, 1).astype(f32)
    part = slots * span // 2
    first_across = row_major(to_group(rows_now[:part], 0, 1))
    merged = (second[0, 0] + up + down + far + across) * (1.0 / SEND)
    merged = merged.reshape(slots, span, wide)
    squares = sum_over_y(jnp.sum(merged * merged, axis=2))
    squares, first_across = lax.optimization_barrier((squares, first_across))
    taps_first = gather_taps(first_across)
    squares = squares + to_chip(squares, 0, 1)
    squares, rows_now = lax.optimization_barrier((squares, rows_now))
    last_across = row_major(to_group(rows_now[part:], 0, 1))

    scaled, crossed = attention(
        lens,
        weights,
        head_scale,
        merged,
        squares.reshape(slots, 1, span),
        norm_gain.reshape(1, wide),
        taps[:, :, 2, :],
    )
    crossed, last_across = lax.optimization_barrier((crossed, last_across))
    crossed = sum_over_y(crossed.reshape(slots, span))
    crossed = crossed + to_chip(crossed, 0, 1)
    inverse = lax.rsqrt(squares / width_all + epsilon)
    merged_grad = (
        scaled * inverse[:, :, None]
        - merged * (inverse * inverse * inverse * crossed / width_all)[:, :, None]
    ).astype(bf16)

    chips = lax.axis_size("tr")
    pairs = [
        (
            (at_z * 2 + at_x) * chips + tr_index(at_y, at_high, at_core),
            (at_y * 2 + at_high) * chips + tr_index(at_y + at_z, at_x, at_core),
        )
        for at_z in range(RING)
        for at_x in range(2)
        for at_y in range(RING)
        for at_high in range(2)
        for at_core in range(2)
    ]
    turned = lax.ppermute(merged_grad.reshape(slots * span, wide), ("rep", "tr"), pairs)
    turned, last_across = lax.optimization_barrier((turned, last_across))
    taps_last = gather_taps(last_across)
    own_half = gather(turned, to_chip)
    other_half = {k: to_sibling(v) for k, v in own_half.items()}

    offsets = [(a, b) for a in GRAD_ORDER for b in range(2)]
    places = [(y - a - z) % RING for a in GRAD_ORDER] + [jnp.where(x_low == x_high, 1, 0), core, rep]
    grad, new_block = gradient(
        jnp.stack(places).astype(jnp.int32),
        taps_here,
        taps_first,
        taps_last,
        [own_half[k] for k in offsets],
        [other_half[k] for k in offsets],
        weight,
    )
    new = buffer((flat_in, width_all), bf16)
    for a, b, first, piece in gather_relayed(new_block, to_group):
        owner = (z - a) % RING * 2 + (x_low - b) % 2
        new = lax.dynamic_update_slice(new, piece, (first, owner * block))
    return grad.reshape(tap_count, wide, block), new.reshape(tap_count, wide, width_all)


def solution(mesh):
    in_specs = (P("rep", None, None, "tr"), P(), P(), P(None, "tr", None), P("tr"), P("tr"))
    out_specs = (P(None, "tr", "rep"), P(None, "tr", None))
    return jax.shard_map(
        per_device, mesh=mesh, in_specs=in_specs, out_specs=out_specs, check_vma=False
    )
```

```python
import jax
import jax.numpy as jnp
from jax import lax
from jax.experimental import pallas as pl
from jax.experimental.layout import Layout, with_layout_constraint
from jax.experimental.pallas import tpu as pltpu
from jax.sharding import PartitionSpec as P

epsilon = 1e-06
step_size = 0.004
SEND = 128.0
SPAN = 96
HEAD = 128
RING = 4
ORDER = (((2, 1), (1, 1), (3, 1)), ((1, 0), (3, 0), (2, 0), (0, 1), (0, 0)))

GRAD_ORDER = (0, 1, 3, 2)

f32 = jnp.float32
bf16 = jnp.bfloat16
f16 = jnp.float16

ROWS_ROWS = (((1,), (1,)), ((), ()))
ROWS_COLS = (((1,), (0,)), ((), ()))
COLS_COLS = (((0,), (0,)), ((), ()))


def split(a):
    high = a.astype(bf16)
    return high, (a - high.astype(f32)).astype(bf16)


def product(a, b, dims):
    ka, kb = dims[0][0][0], dims[0][1][0]
    return lax.dot_general(
        jnp.concatenate([a[0], a[0], a[1]], axis=ka),
        jnp.concatenate([b[0], b[1], b[0]], axis=kb),
        dims,
        preferred_element_type=f32,
    )


def attention_kernel(lens_ref, weights_ref, scale_ref, merged_ref, square_ref, gain_ref, tap_ref, scaled_ref, cross_ref):
    slots = merged_ref.shape[0]
    heads = scale_ref.shape[0]
    first = pl.program_id(0) * slots
    place = lax.broadcasted_iota(jnp.int32, (SPAN, HEAD), 0)
    key = lax.broadcasted_iota(jnp.int32, (SPAN, HEAD), 1)
    eye = lax.broadcasted_iota(jnp.int32, (SPAN, SPAN), 0) == lax.broadcasted_iota(jnp.int32, (SPAN, SPAN), 1)
    pad = jnp.zeros((HEAD - SPAN, HEAD), f32)
    chains = [(s, h) for s in range(slots) for h in range(heads)]
    every = range(len(chains))
    width = 16 * heads * HEAD
    lens = [lens_ref[first + s] for s, _ in chains]
    weights = [weights_ref[first + s] for s, _ in chains]
    scales = [scale_ref[h] for _, h in chains]
    columns = [pl.ds(h * HEAD, HEAD) for _, h in chains]
    allowed = [(key <= place) & (key < lens[c]) for c in every]
    inverse = []
    for s in range(slots):
        across = lax.rsqrt(square_ref[s] / width + epsilon)
        inverse.append(jnp.sum(jnp.where(eye, across, 0.0), axis=1, keepdims=True))
    gains = [gain_ref[:, columns[c]] for c in every]
    start = [merged_ref[chains[c][0], :, columns[c]] * inverse[chains[c][0]] * gains[c] for c in every]
    keys = [split(jnp.concatenate([start[c], pad], axis=0)) for c in every]
    current = list(start)
    queries, shares, loss_grads = [], [], []
    for step in range(3):
        parts = [split(current[c]) for c in every]
        logits = [product(parts[c], keys[c], ROWS_ROWS) * scales[c] for c in every]
        logits = [jnp.where(allowed[c], logits[c], -1e30) for c in every]
        raised = [jnp.exp(logits[c] - jnp.max(logits[c], axis=1, keepdims=True)) for c in every]
        share = [raised[c] / jnp.sum(raised[c], axis=1, keepdims=True) for c in every]
        share_parts = [split(share[c]) for c in every]
        attended = [product(share_parts[c], keys[c], ROWS_COLS) for c in every]
        current = [current[c] + attended[c] for c in every]
        queries.append(parts)
        shares.append((share, share_parts))
        grads = []
        for c in every:
            later = pltpu.roll(tap_ref[chains[c][0], :, columns[c]].astype(f32), SPAN - (step + 1), 0)
            active = jnp.where(place + (step + 1) < lens[c], 2.0 * weights[c], 0.0)
            grads.append(active * (current[c] - later))
        loss_grads.append(grads)
    grad = loss_grads[2]
    key_grad = None
    for step in (2, 1, 0):
        share, share_parts = shares[step]
        parts = [split(grad[c]) for c in every]
        share_grad = [product(parts[c], keys[c], ROWS_ROWS) for c in every]
        inner = [jnp.sum(share_grad[c] * share[c], axis=1, keepdims=True) for c in every]
        logit_parts = [split(share[c] * (share_grad[c] - inner[c]) * scales[c]) for c in every]
        left = [tuple(jnp.concatenate(z, axis=0) for z in zip(share_parts[c], logit_parts[c])) for c in every]
        right = [tuple(jnp.concatenate(z, axis=0) for z in zip(parts[c], queries[step][c])) for c in every]
        added = [product(left[c], right[c], COLS_COLS) for c in every]
        key_grad = added if key_grad is None else [key_grad[c] + added[c] for c in every]
        grad = [grad[c] + product(logit_parts[c], keys[c], ROWS_COLS) for c in every]
        if step > 0:
            grad = [grad[c] + loss_grads[step - 1][c] for c in every]
    crossed = [None] * slots
    for c in every:
        s = chains[c][0]
        scaled = (grad[c] + key_grad[c][:SPAN]) * gains[c]
        scaled_ref[s, :, columns[c]] = scaled
        inner = jnp.sum(scaled * merged_ref[s, :, columns[c]], axis=1, keepdims=True)
        crossed[s] = inner if crossed[s] is None else crossed[s] + inner
    for s in range(slots):
        cross_ref[s] = jnp.sum(jnp.where(eye, crossed[s], 0.0), axis=0, keepdims=True)


def attention(lens, weights, scales, merged, squares, gain, taps, slots=8):
    count, span, wide = merged.shape
    scalar = pl.BlockSpec(memory_space=pltpu.SMEM)
    block = pl.BlockSpec((slots, span, wide), lambda i: (i, 0, 0))
    flat = pl.BlockSpec((slots, 1, span), lambda i: (i, 0, 0))
    return pl.pallas_call(
        attention_kernel,
        grid=(count // slots,),
        in_specs=[scalar, scalar, scalar, block, flat, pl.BlockSpec((1, wide), lambda i: (0, 0)), block],
        out_specs=[block, flat],
        out_shape=[
            jax.ShapeDtypeStruct((count, span, wide), f32),
            jax.ShapeDtypeStruct((count, 1, span), f32),
        ],
        compiler_params=pltpu.CompilerParams(vmem_limit_bytes=16 * 2**20),
        cost_estimate=pl.CostEstimate(flops=2 * 10**9, bytes_accessed=3 * 10**6, transcendentals=10**6),
    )(lens, weights, scales, merged, squares, gain, taps)


def gradient_kernel(places_ref, here_ref, first_ref, last_ref, *refs):
    number = 2 * len(GRAD_ORDER)
    own, other, old_ref, grad_ref, new_ref = refs[:number], refs[number : 2 * number], *refs[2 * number :]
    step = pl.program_id(0)
    same, core = places_ref[len(GRAD_ORDER)], places_ref[len(GRAD_ORDER) + 1]
    wide = own[0].shape[1]

    @pl.when(step == 0)
    def _():
        grad_ref[...] = jnp.zeros_like(grad_ref)

    for k in range(len(GRAD_ORDER)):

        @pl.when(step == k)
        def _():
            for half, parity in ((own, core), (other, 1 - core)):
                straight, crossed = half[2 * k][...], half[2 * k + 1][...]
                here = jnp.where(same == 1, straight, crossed)
                across = jnp.where(same == 1, crossed, straight)
                columns = pl.ds(pl.multiple_of(parity * wide, wide), wide)
                part = first_ref.shape[0]
                grad_ref[:, columns] += (
                    lax.dot_general(here_ref[...], here, COLS_COLS, preferred_element_type=f32)
                    + lax.dot_general(first_ref[...], across[:part], COLS_COLS, preferred_element_type=f32)
                    + lax.dot_general(last_ref[...], across[part:], COLS_COLS, preferred_element_type=f32)
                )

    @pl.when(step == len(GRAD_ORDER) - 1)
    def _():
        new_ref[...] = (old_ref[...].astype(f32) - step_size * grad_ref[...]).astype(bf16)


def gradient(places, here, first, last, own, other, weight):
    steps = len(GRAD_ORDER)
    rows, wide = own[0].shape
    depth = weight.shape[0]
    piece = pl.BlockSpec((rows, wide), lambda i, places: (0, 0))
    taps = pl.BlockSpec((rows, depth), lambda i, places: (places[i], 0))
    half = pl.BlockSpec((rows // 2, depth), lambda i, places: (places[i], 0))
    out = pl.BlockSpec((depth, 2 * wide), lambda i, places: (0, 0))
    old = pl.BlockSpec((depth, 2 * wide), lambda i, places: (0, places[steps + 2]))
    return pl.pallas_call(
        gradient_kernel,
        grid_spec=pltpu.PrefetchScalarGridSpec(
            num_scalar_prefetch=1,
            grid=(steps,),
            in_specs=[taps, half, half] + [piece] * (4 * steps) + [old],
            out_specs=[out, out],
        ),
        out_shape=[
            jax.ShapeDtypeStruct((depth, 2 * wide), f32),
            jax.ShapeDtypeStruct((depth, 2 * wide), bf16),
        ],
        compiler_params=pltpu.CompilerParams(vmem_limit_bytes=56 * 2**20),
        cost_estimate=pl.CostEstimate(
            flops=8 * steps * rows * depth * wide, bytes_accessed=20 * 2**20, transcendentals=0
        ),
    )(places, here, first, last, *own, *other, weight)


def row_major(a):
    return with_layout_constraint(a, Layout(major_to_minor=tuple(range(a.ndim))))


def buffer(shape, dtype):
    return pl.pallas_call(
        lambda out_ref: None,
        out_specs=pl.BlockSpec(memory_space=pl.ANY),
        out_shape=jax.ShapeDtypeStruct(shape, dtype),
    )()


def tr_index(y, x, core):
    return (y % RING * 2 + x % 2) * 2 + core % 2


def to_chip(value, dy, dx, dcore=0):
    pairs = [
        (tr_index(y, x, core), tr_index(y + dy, x + dx, core + dcore))
        for y in range(RING)
        for x in range(2)
        for core in range(2)
    ]
    return lax.ppermute(value, "tr", pairs)


def to_group(value, dz, dx):
    pairs = [(z * 2 + x, (z + dz) % RING * 2 + (x + dx) % 2) for z in range(RING) for x in range(2)]
    return lax.ppermute(value, "rep", pairs)


def to_sibling(value):
    return to_chip(value, 0, 0, 1)


def gather(value, send):
    got = {(0, 0): value}
    got[1, 0] = send(value, 1, 0)
    got[3, 0] = send(value, 3, 0)
    got[0, 1] = send(value, 0, 1)
    got[2, 0] = send(value, 2, 0)
    got[1, 1] = send(got[0, 1], 1, 0)
    got[3, 1] = send(got[0, 1], 3, 0)
    got[2, 1] = send(got[2, 0], 0, 1)
    return got


def gather_relayed(value, send):
    half = value.shape[0] // 2
    up, down, across = send(value, 1, 0), send(value, 3, 0), send(value, 0, 1)
    far_first = send(up[:half], 1, 0)
    far_last = send(down[half:], 3, 0)
    up_across, down_across = send(across, 1, 0), send(across, 3, 0)
    far_across = send(jnp.concatenate([far_first, far_last], axis=0), 0, 1)
    return [
        (0, 0, 0, value),
        (1, 0, 0, up),
        (3, 0, 0, down),
        (0, 1, 0, across),
        (2, 0, 0, far_first),
        (2, 0, half, far_last),
        (1, 1, 0, up_across),
        (3, 1, 0, down_across),
        (2, 1, 0, far_across),
    ]


def product_kernel(blocks_ref, rows_ref, weight_ref, out_ref):
    out_ref[0] = jnp.dot(rows_ref[...], weight_ref[...], preferred_element_type=f32)


def products(rows, weight, blocks, wide):
    count, depth = rows.shape
    number = blocks.shape[0]
    return pl.pallas_call(
        product_kernel,
        grid_spec=pltpu.PrefetchScalarGridSpec(
            num_scalar_prefetch=1,
            grid=(number,),
            in_specs=[
                pl.BlockSpec((count, depth), lambda i, blocks: (0, 0)),
                pl.BlockSpec((depth, wide), lambda i, blocks: (0, blocks[i])),
            ],
            out_specs=pl.BlockSpec((1, count, wide), lambda i, blocks: (i, 0, 0)),
        ),
        out_shape=jax.ShapeDtypeStruct((number, count, wide), f32),
        compiler_params=pltpu.CompilerParams(vmem_limit_bytes=8 * 2**20),
        cost_estimate=pl.CostEstimate(
            flops=2 * count * depth * wide * number,
            bytes_accessed=count * depth * 2 + number * wide * (count * 4 + depth * 2),
            transcendentals=0,
        ),
    )(blocks, rows, weight)


def sum_over_y(value):
    value = value + to_sibling(value)
    return value + to_chip(value, 1, 0) + to_chip(value, 2, 0) + to_chip(value, 3, 0)


def per_device(taps, routes, lengths, merge_weight, norm_gain, head_scale):
    rep = lax.axis_index("rep")
    tr = lax.axis_index("tr")
    core = tr % 2
    x_high = tr // 2 % 2
    y = tr // 4
    x_low = rep % 2
    z = rep // 2
    slots, span, tap_count, wide = taps.shape
    width_all = merge_weight.shape[2]
    flat_in = tap_count * wide
    block = width_all // lax.axis_size("rep")
    rows = row_major(taps.reshape(slots * span, flat_in))
    weight = merge_weight.reshape(flat_in, width_all)

    dest = routes[:, 0]
    target = jnp.maximum(lengths - 1, 0) + jnp.maximum(lengths - 2, 0) + jnp.maximum(lengths - 3, 0)
    own_dest = lax.dynamic_slice_in_dim(dest, rep * slots, slots)
    lens = lax.dynamic_slice_in_dim(lengths, rep * slots, slots)
    count = jnp.sum(jnp.where(own_dest[:, None] == dest[None, :], target[None, :], 0), axis=1)
    weights = 1.0 / count.astype(f32)

    along_z = [[at_z * 2 + at_x for at_z in range(RING)] for at_x in range(2)]

    def gather_taps(value):
        return row_major(lax.all_gather(value, "rep", axis=0, tiled=True, axis_index_groups=along_z))

    taps_here = gather_taps(rows)

    def sums(rows, offsets, parity):
        blocks = jnp.stack([tr_index(y + dy, x_high + dx, parity) for dy, dx in offsets])
        return products(rows, weight, blocks.astype(jnp.int32), wide)

    def chip_sums(rows, offsets):
        other = to_sibling(sums(rows, offsets, 1 - core))
        own = sums(rows, offsets, core)
        return {offset: (own[i] + other[i]) * SEND for i, offset in enumerate(offsets)}

    def send(value, dy, dx):
        return to_chip(value.astype(f16), dy, dx)

    first = chip_sums(rows, ORDER[0])
    far_across, up_across, down_across, rows_now = lax.optimization_barrier(
        tuple(first[offset].astype(f16) for offset in ORDER[0]) + (rows,)
    )
    far_across = send(far_across, 0, 1)
    up_across = send(up_across, 1, 0)
    down_across = send(down_across, 3, 0)
    second = chip_sums(rows_now, ORDER[1])
    up = send(second[1, 0], 1, 0).astype(f32)
    down = send(second[3, 0], 3, 0).astype(f32)
    far = send(second[2, 0] + far_across.astype(f32), 2, 0).astype(f32)
    second_across = (second[0, 1] + up_across.astype(f32) + down_across.astype(f32)).astype(f16)
    second_across, rows_now = lax.optimization_barrier((second_across, rows_now))
    across = send(second_across, 0, 1).astype(f32)
    part = slots * span // 2
    first_across = row_major(to_group(rows_now[:part], 0, 1))
    merged = (second[0, 0] + up + down + far + across) * (1.0 / SEND)
    merged = merged.reshape(slots, span, wide)
    squares = sum_over_y(jnp.sum(merged * merged, axis=2))
    squares, first_across = lax.optimization_barrier((squares, first_across))
    taps_first = gather_taps(first_across)
    squares = squares + to_chip(squares, 0, 1)
    squares, rows_now = lax.optimization_barrier((squares, rows_now))
    last_across = row_major(to_group(rows_now[part:], 0, 1))

    scaled, crossed = attention(
        lens,
        weights,
        head_scale,
        merged,
        squares.reshape(slots, 1, span),
        norm_gain.reshape(1, wide),
        taps[:, :, 2, :],
    )
    crossed, last_across = lax.optimization_barrier((crossed, last_across))
    crossed = sum_over_y(crossed.reshape(slots, span))
    crossed = crossed + to_chip(crossed, 0, 1)
    inverse = lax.rsqrt(squares / width_all + epsilon)
    merged_grad = (
        scaled * inverse[:, :, None]
        - merged * (inverse * inverse * inverse * crossed / width_all)[:, :, None]
    ).astype(bf16)

    chips = lax.axis_size("tr")
    pairs = [
        (
            (at_z * 2 + at_x) * chips + tr_index(at_y, at_high, at_core),
            (at_y * 2 + at_high) * chips + tr_index(2 * at_y - at_z, at_x, at_core),
        )
        for at_z in range(RING)
        for at_x in range(2)
        for at_y in range(RING)
        for at_high in range(2)
        for at_core in range(2)
    ]
    turned = lax.ppermute(merged_grad.reshape(slots * span, wide), ("rep", "tr"), pairs)
    turned, last_across = lax.optimization_barrier((turned, last_across))
    taps_last = gather_taps(last_across)
    own_half = gather(turned, to_chip)
    other_half = {k: to_sibling(v) for k, v in own_half.items()}

    offsets = [(a, b) for a in GRAD_ORDER for b in range(2)]
    places = [(2 * z - y + a) % RING for a in GRAD_ORDER] + [jnp.where(x_low == x_high, 1, 0), core, rep]
    grad, new_block = gradient(
        jnp.stack(places).astype(jnp.int32),
        taps_here,
        taps_first,
        taps_last,
        [own_half[k] for k in offsets],
        [other_half[k] for k in offsets],
        weight,
    )
    new = buffer((flat_in, width_all), bf16)
    for a, b, first, piece in gather_relayed(new_block, to_group):
        owner = (z - a) % RING * 2 + (x_low - b) % 2
        new = lax.dynamic_update_slice(new, piece, (first, owner * block))
    return grad.reshape(tap_count, wide, block), new.reshape(tap_count, wide, width_all)


def solution(mesh):
    in_specs = (P("rep", None, None, "tr"), P(), P(), P(None, "tr", None), P("tr"), P("tr"))
    out_specs = (P(None, "tr", "rep"), P(None, "tr", None))
    return jax.shard_map(
        per_device, mesh=mesh, in_specs=in_specs, out_specs=out_specs, check_vma=False
    )
```
